32 devices in a mesh: row: 4 (over x, core), col: 8 (over z, y).
Axes of the slice: x: 2, y: 2, z: 4, core: 2. Of those that a mesh axis runs over, the one named last changes fastest.
Arguments:
- test_points: float32 [3, 512], P(None, ('row', 'col')), may hold values from 0 to 1
- src_points: float32 [3, 32768], P(None, ('row', 'col')), may hold values from 0 to 1
- currents: float32 [2, 32768], P(None, ('row', 'col')), may hold values from -6 to 6
- near_blocks: float32 [256, 2, 16, 128], P(('row', 'col')), may hold values from -0.3 to 0.3
- near_dest: int32 [256, 1], P(('row', 'col')), may hold values from 0 to 7; in each aligned block of 8 rows (0 to 7, 8 to 15, ...) at most 2 rows name the same one
- near_tile: int32 [256, 1], P(('row', 'col')), may hold values from 0 to 7
Outputs:
- field: float32 [2, 512], P(None, ('row', 'col'))
The draws below stay inside these ranges and needn't reach their ends.
Inputs may be any that keep to these rules, and one draw needn't show every extreme that they name: `near_dest`: among the 8 blocks held by one device, at most 2 name the same column index; some device reaches 2 in every draw.
All inputs are finite; a program needn't handle non-finite values.
Results may differ from the reference program's by a relative error of at most 0.0003.
Values sent between devices are 32-bit elements; how exact they have to be, the bound alone decides.
No kernel may reach another device: no remote copies, remote signals or barrier semaphores. Data moves between devices by JAX's collectives and lax.ppermute only.
A program may use at most 64 MiB of HBM per device.

```python
import math
import jax
import jax.numpy as jnp
import numpy as np
from jax import lax

ROW_DEV = 16
STILE = 128
CAP = 2
ROWS = 512
SOURCES = 32768
TILES = 8
NEAR_DEV = 8
NEAR_ALL = 256
N_COL = 8
DEVICES = 32


def place_ends(drawn, rng, low, high):
    dims = drawn.shape
    spot = [jax.random.randint(jax.random.fold_in(rng, axis), (), 0, dims[axis]) for axis in range(len(dims))]
    drawn = drawn.at[tuple(spot)].set(low)
    longest = dims.index(max(dims))
    spot[longest] = (spot[longest] + 1) % dims[longest]
    return drawn.at[tuple(spot)].set(high)


def level_of(own_key, extent, cuts, least, largest):
    gain = 1.0
    for dim, blocks in cuts:
        heights = jax.random.uniform(jax.random.fold_in(jax.random.fold_in(own_key, 6), dim), (blocks,), jnp.float32, least / len(cuts), largest / len(cuts))
        gain = gain * jnp.repeat(jnp.exp(heights), extent[dim] // blocks).reshape((-1,) + (1,) * (len(extent) - 1 - dim))
    return gain


def deal_out(key, own, number, rows, amount, top, reach, lean):
    sequence = jax.random.permutation(key, amount)
    heavy_load, common = portions_of(amount, rows * top, reach, lean, True), portions_of(amount, rows * top, reach, lean, False)
    places = jnp.arange(amount)

    def named(sizes, offset_by):
        used = int((sizes > 0).sum())
        fixed = max(1, used // 4)
        passed = fixed + (places - fixed + offset_by * (used - fixed)) % max(1, amount - fixed)
        return jnp.zeros((amount,), jnp.int32).at[sequence[jnp.where(places < fixed, places, passed)]].set(jnp.asarray(sizes, jnp.int32))

    sizes = jnp.where(number % 4 == 0, named(heavy_load, number // 4), named(common, number - number // 4 - 1))
    mixed = jax.random.permutation(jax.random.fold_in(own, 3), amount)
    source_of, sink = mixed[0:amount // 2 * 2:2], mixed[1:amount // 2 * 2:2]
    slack = jnp.minimum(sizes[source_of] - 1, reach - sizes[sink]) // 2
    slack = jnp.where((source_of == sequence[0]) | (sink == sequence[0]) | (sizes[sink] == 0), 0, jnp.maximum(slack, 0))
    passed = jax.random.randint(jax.random.fold_in(own, 4), (amount // 2,), 0, 1 << 20) % (slack + 1)
    sizes = sizes.at[source_of].add(-passed).at[sink].add(passed)
    items = jnp.searchsorted(jnp.cumsum(sizes), jnp.arange(rows * top), side="right").astype(jnp.int32)
    listing = items.reshape(top, rows).T
    listing = listing[jax.random.permutation(jax.random.fold_in(own, 1), rows)]
    offset_by = jax.random.randint(jax.random.fold_in(own, 2), (rows, 1), 0, top)
    return jnp.take_along_axis(listing, (jnp.arange(top)[None, :] + offset_by) % top, axis=1)


def portions_of(amount, total, most, lean, full):
    weights = [(1 << 20) // math.isqrt(standing ** lean) + 1 for standing in range(1, amount + 1)]
    largest = most if full else min(most, max(-(-total // amount), total * weights[0] // sum(weights)))
    least = 1 if total - largest >= amount - 1 else 0
    given, spare = [largest] + [least] * (amount - 1), total - largest - least * (amount - 1)
    while spare > 0:
        candidates = [i for i in range(1, amount) if given[i] < largest] or [i for i in range(1, amount) if given[i] < most]
        whole, remaining = sum([weights[i] for i in candidates]), spare
        for i in candidates:
            addition = min(most - given[i], max(1, remaining * weights[i] // whole), spare)
            given[i] = given[i] + addition
            spare = spare - addition
    return np.array(given)


def scatter_about(rng, dims, width, reach, cuts=(), held_as=jnp.bfloat16):
    result = jax.random.normal(rng, dims, jnp.float32) * width
    if len(cuts) > 0:
        result = level_of(rng, dims, cuts, -0.22, 0.18) * result
    return jnp.clip(result, min=-reach, max=reach).astype(held_as)


def setup_inputs(seed: int = 0) -> dict:
    arg_keys = jax.random.split(jax.random.key(seed), 7)
    test_points = jnp.clip(1.0 * jax.random.uniform(arg_keys[0], (3, ROWS), jnp.float32) ** level_of(arg_keys[0], (3, ROWS), ((1, 32),), -0.2, 0.2), 0.0, 1.0)
    src_points = jnp.clip(1.0 * jax.random.uniform(arg_keys[1], (3, SOURCES), jnp.float32) ** level_of(arg_keys[1], (3, SOURCES), ((1, 32),), -0.2, 0.2), 0.0, 1.0)
    currents = scatter_about(arg_keys[2], (2, SOURCES), 1.0, 6.0, ((1, 32),), jnp.float32)
    near_blocks = scatter_about(arg_keys[3], (NEAR_ALL, 2, ROW_DEV, STILE), 0.05, 0.3, ((0, 32),), jnp.float32)
    near_dest_keys = jax.random.split(jax.random.fold_in(arg_keys[4], 1), NEAR_ALL // NEAR_DEV)
    near_dest_turns = jax.random.permutation(jax.random.fold_in(arg_keys[4], 3), NEAR_ALL // NEAR_DEV)
    near_dest = jax.vmap(lambda own, number: deal_out(jax.random.fold_in(arg_keys[4], 2), own, number, NEAR_DEV, N_COL, 1, CAP, 2))(near_dest_keys, near_dest_turns).reshape((NEAR_ALL, 1))
    near_tile = place_ends(jax.random.randint(arg_keys[5], (NEAR_ALL, 1), 0, TILES), jax.random.fold_in(arg_keys[5], 1), 0, TILES - 1).astype(jnp.int32)
    return dict(test_points=test_points, src_points=src_points, currents=currents, near_blocks=near_blocks, near_dest=near_dest, near_tile=near_tile)


WAVENUMBER = 40.0
SOFTENING = 0.01

def kernel_sum(targets, sources, current):
    delta_x = targets[0][:, None] - sources[0][None, :]
    delta_y = targets[1][:, None] - sources[1][None, :]
    delta_z = targets[2][:, None] - sources[2][None, :]
    distance = jnp.sqrt(delta_x * delta_x + delta_y * delta_y + delta_z * delta_z + SOFTENING * SOFTENING)
    phases = WAVENUMBER * distance
    kernel_re = jnp.cos(phases) / distance
    kernel_im = -jnp.sin(phases) / distance
    real_part = lax.optimization_barrier(jnp.sum(kernel_re * current[0][None, :] - kernel_im * current[1][None, :], axis=1))
    imag_part = lax.optimization_barrier(jnp.sum(kernel_re * current[1][None, :] + kernel_im * current[0][None, :], axis=1))
    return jnp.stack([real_part, imag_part])

def reference(test_points, src_points, currents, near_blocks, near_dest, near_tile):
    block_rows = math.gcd(ROWS, 64)
    row_blocks = test_points.reshape(3, ROWS // block_rows, block_rows).transpose(1, 0, 2)
    far_blocks = lax.map(lambda targets: kernel_sum(targets, src_points, currents), row_blocks)
    far = far_blocks.transpose(1, 0, 2).reshape(2, ROWS)
    holder = (jnp.arange(NEAR_ALL) // NEAR_DEV).astype(jnp.int32)
    target = (holder // N_COL * N_COL + near_dest[:, 0]).astype(jnp.int32)
    tiled = currents.reshape(2, DEVICES, TILES, STILE)
    chosen = tiled[:, holder, near_tile[:, 0], :]
    highest = lax.Precision.HIGHEST
    term_re = jnp.einsum('kij,kj->ki', near_blocks[:, 0], chosen[0], precision=highest) - jnp.einsum('kij,kj->ki', near_blocks[:, 1], chosen[1], precision=highest)
    term_im = jnp.einsum('kij,kj->ki', near_blocks[:, 0], chosen[1], precision=highest) + jnp.einsum('kij,kj->ki', near_blocks[:, 1], chosen[0], precision=highest)
    terms = jnp.stack([term_re, term_im], axis=1)
    summed = jax.ops.segment_sum(terms, target, num_segments=DEVICES)
    near = summed.transpose(1, 0, 2).reshape(2, ROWS)
    return far * (1.0 / math.sqrt(SOURCES)) + near
```

```python
import functools
import math

import jax
import jax.numpy as jnp
import numpy as np
from jax import lax
from jax.experimental import pallas as pl
from jax.experimental.pallas import tpu as pltpu
from jax.sharding import PartitionSpec as P

WAVENUMBER = 40.0
SOFTENING = 0.01
TURNS = WAVENUMBER / (2.0 * math.pi)
LANES = 128
SUB = 8


def even_fit(function, terms, reach):
    nodes = np.cos((np.arange(400) + 0.5) * np.pi / 400)
    squares = (nodes + 1) * 0.5 * reach * reach
    fit = np.polynomial.chebyshev.Chebyshev.fit(squares, function(np.sqrt(squares)), terms - 1)
    return [float(value) for value in fit.convert(kind=np.polynomial.Polynomial).coef]


ROOT2 = math.sqrt(2.0)
SINE = even_fit(lambda u: ROOT2 * math.pi * np.sinc(u), 5, 0.5)
COSINE = even_fit(lambda u: -ROOT2 * np.cos(np.pi * u), 5, 0.5)
ROUNDER = 1.5 * 2.0**23


def horner(coefficients, x):
    total = coefficients[-1] * x + coefficients[-2]
    for value in coefficients[-3::-1]:
        total = total * x + value
    return total


def lane_repeat(x, period):
    width = period
    lane = lax.broadcasted_iota(jnp.int32, x.shape, 1)
    while width < LANES:
        x = jnp.where(lane < width, x, pltpu.roll(x, width, 1))
        width *= 2
    return x


def field_kernel(
    columns, dest_ref, tile_ref, tests_ref, src_ref, cur_ref, blocks_ref, out_ref,
    source_rows, near_rows, start, padded, tests_wide
):
    devices, _, row_dev = tests_ref.shape
    width = src_ref.shape[1]
    items = blocks_ref.shape[0]
    per_row = LANES // row_dev
    tiles = width // LANES
    gain = TURNS / math.sqrt(width * devices)
    lane = lax.broadcasted_iota(jnp.int32, (SUB, LANES), 1)
    sub = lax.broadcasted_iota(jnp.int32, (SUB, LANES), 0)

    start[...] = jnp.zeros_like(start)
    row_base = lax.axis_index("row") * columns
    for group in range(items // per_row):
        owner = jnp.zeros((SUB, LANES), jnp.int32)
        for k in range(per_row):
            block = group * per_row + k
            tile = pl.multiple_of(tile_ref[block, 0] * LANES, LANES)
            cr = cur_ref[0:1, pl.ds(tile, LANES)]
            ci = cur_ref[1:2, pl.ds(tile, LANES)]
            br = blocks_ref[block, 0]
            bi = blocks_ref[block, 1]
            near_rows[0, pl.ds(k * row_dev, row_dev), :] = br * cr - bi * ci
            near_rows[1, pl.ds(k * row_dev, row_dev), :] = br * ci + bi * cr
            owner = jnp.where(lane // row_dev == k, dest_ref[block, 0], owner)
        ones = jnp.ones((SUB, LANES), jnp.float32)
        for part in range(2):
            term = lax.dot_general(
                ones, near_rows[part], (((1,), (1,)), ((), ())),
                precision=lax.Precision.HIGHEST, preferred_element_type=jnp.float32,
            )
            for block in range(columns // SUB):
                place = pl.ds(pl.multiple_of(row_base + block * SUB, SUB), SUB)
                start[part, place, :] += jnp.where(owner == sub + block * SUB, term, 0.0)

    padded[0:3, :] = src_ref[...] * TURNS
    cr = cur_ref[0:1, :]
    ci = cur_ref[1:2, :]
    padded[3:4, :] = jnp.sqrt(cr * cr + ci * ci) * gain
    padded[4:5, :] = jnp.arctan2(ci, cr) * (0.5 / math.pi)
    padded[5:8, :] = jnp.zeros((3, width), jnp.float32)
    pick = lane // row_dev
    for tile in range(tiles):
        x = padded[:, pl.ds(tile * LANES, LANES)]
        for j in range(row_dev):
            source_rows[tile * row_dev + j] = jnp.take_along_axis(x, pick + j * per_row, axis=1)

    for group in range(devices // SUB):
        for c in range(3):
            points = tests_ref[pl.ds(group * SUB, SUB), c, :] * TURNS
            points = jnp.concatenate([points, jnp.zeros((SUB, LANES - row_dev), jnp.float32)], axis=1)
            tests_wide[c, pl.ds(group * SUB, SUB), :] = lane_repeat(points, row_dev)

    chunk = min(4, devices // SUB)
    soft = (SOFTENING * TURNS) ** 2

    def far(block, _):
        places = [pl.ds(pl.multiple_of((block * chunk + g) * SUB, SUB), SUB) for g in range(chunk)]
        tests = [[tests_wide[c, place, :] for c in range(3)] for place in places]

        def step(r, sums):
            sx, sy, sz, size, turn = [
                jnp.broadcast_to(source_rows[r, c : c + 1, :], (SUB, LANES)) for c in range(5)
            ]
            new = []
            for (tx, ty, tz), (re, im) in zip(tests, sums):
                dx = tx - sx
                dy = ty - sy
                dz = tz - sz
                square = dx * dx + dy * dy + (dz * dz + soft)
                inverse = lax.rsqrt(square)
                t = square * inverse - turn
                u = t - ((t + ROUNDER) - ROUNDER)
                u2 = u * u
                s = u * horner(SINE, u2)
                c = horner(COSINE, u2)
                a = inverse * size
                new.append((re + a * (1.0 - s * s), im + a * (s * c)))
            return tuple(new)

        sums = tuple((start[0, place, :], start[1, place, :]) for place in places)
        sums = lax.fori_loop(0, width // per_row, step, sums, unroll=2)
        for place, (re, im) in zip(places, sums):
            shift = LANES // 2
            while shift >= row_dev:
                re = re + pltpu.roll(re, shift, 1)
                im = im + pltpu.roll(im, shift, 1)
                shift //= 2
            both = jnp.where(lane < row_dev, re, im)
            out_ref[place, :] = both[:, : 2 * row_dev]
        return 0

    lax.fori_loop(0, devices // (SUB * chunk), far, 0)


def local(test_points, src_points, currents, near_blocks, near_dest, near_tile):
    row_dev = test_points.shape[1]
    width = src_points.shape[1]
    columns = lax.axis_size("col")
    devices = lax.axis_size("row") * columns
    tests = lax.all_gather(test_points, ("row", "col"), axis=0, tiled=False)
    vmem = pl.BlockSpec(memory_space=pltpu.VMEM)
    smem = pl.BlockSpec(memory_space=pltpu.SMEM)
    partial = pl.pallas_call(
        functools.partial(field_kernel, columns),
        out_shape=jax.ShapeDtypeStruct((devices, 2 * row_dev), jnp.float32),
        in_specs=[smem, smem, vmem, vmem, vmem, vmem],
        out_specs=vmem,
        scratch_shapes=[
            pltpu.VMEM((width * row_dev // LANES, SUB, LANES), jnp.float32),
            pltpu.VMEM((2, LANES, LANES), jnp.float32),
            pltpu.VMEM((2, devices, LANES), jnp.float32),
            pltpu.VMEM((SUB, width), jnp.float32),
            pltpu.VMEM((3, devices, LANES), jnp.float32),
        ],
        compiler_params=pltpu.CompilerParams(vmem_limit_bytes=24 << 20),
    )(near_dest, near_tile, tests, src_points, currents, near_blocks)
    parts = lax.all_to_all(partial, ("row", "col"), split_axis=0, concat_axis=0, tiled=True)
    return parts.sum(axis=0).reshape(2, row_dev)


def solution(mesh):
    in_specs = (
        P(None, ("row", "col")),
        P(None, ("row", "col")),
        P(None, ("row", "col")),
        P(("row", "col"), None, None, None),
        P(("row", "col"), None),
        P(("row", "col"), None),
    )
    out_specs = P(None, ("row", "col"))
    return jax.shard_map(local, mesh=mesh, in_specs=in_specs, out_specs=out_specs, check_vma=False)
```

```python
import functools
import math

import jax
import jax.numpy as jnp
import numpy as np
from jax import lax
from jax.experimental import pallas as pl
from jax.experimental.pallas import tpu as pltpu
from jax.sharding import PartitionSpec as P

WAVENUMBER = 40.0
SOFTENING = 0.01
TURNS = WAVENUMBER / (2.0 * math.pi)
LANES = 128
SUB = 8


def even_fit(function, terms, reach):
    nodes = np.cos((np.arange(400) + 0.5) * np.pi / 400)
    squares = (nodes + 1) * 0.5 * reach * reach
    fit = np.polynomial.chebyshev.Chebyshev.fit(squares, function(np.sqrt(squares)), terms - 1)
    return [float(value) for value in fit.convert(kind=np.polynomial.Polynomial).coef]


ROOT2 = math.sqrt(2.0)
SINE = even_fit(lambda u: ROOT2 * math.pi * np.sinc(u), 5, 0.5)
COSINE = even_fit(lambda u: -ROOT2 * np.cos(np.pi * u), 5, 0.5)
ROUNDER = 1.5 * 2.0**23


def horner(coefficients, x):
    total = coefficients[-1] * x + coefficients[-2]
    for value in coefficients[-3::-1]:
        total = total * x + value
    return total


def lane_repeat(x, period):
    width = period
    lane = lax.broadcasted_iota(jnp.int32, x.shape, 1)
    while width < LANES:
        x = jnp.where(lane < width, x, pltpu.roll(x, width, 1))
        width *= 2
    return x


def field_kernel(
    columns, dest_ref, tile_ref, tests_ref, src_ref, cur_ref, blocks_hbm, out_ref,
    source_rows, near_rows, start, padded, tests_wide, blocks_ref, blocks_sem
):
    devices, _, row_dev = tests_ref.shape
    width = src_ref.shape[1]
    items = blocks_ref.shape[0]
    per_row = LANES // row_dev
    tiles = width // LANES
    gain = TURNS / math.sqrt(width * devices)
    lane = lax.broadcasted_iota(jnp.int32, (SUB, LANES), 1)
    sub = lax.broadcasted_iota(jnp.int32, (SUB, LANES), 0)

    blocks_copy = pltpu.make_async_copy(blocks_hbm, blocks_ref, blocks_sem)
    blocks_copy.start()

    padded[0:3, :] = src_ref[...] * TURNS
    cr = cur_ref[0:1, :]
    ci = cur_ref[1:2, :]
    padded[3:4, :] = jnp.sqrt(cr * cr + ci * ci) * gain
    padded[4:5, :] = jnp.arctan2(ci, cr) * (0.5 / math.pi)
    padded[5:8, :] = jnp.zeros((3, width), jnp.float32)
    pick = lane // row_dev
    for tile in range(tiles):
        x = padded[:, pl.ds(tile * LANES, LANES)]
        for j in range(row_dev):
            source_rows[tile * row_dev + j] = jnp.take_along_axis(x, pick + j * per_row, axis=1)

    blocks_copy.wait()
    start[...] = jnp.zeros_like(start)
    row_base = lax.axis_index("row") * columns
    for group in range(items // per_row):
        owner = jnp.zeros((SUB, LANES), jnp.int32)
        for k in range(per_row):
            block = group * per_row + k
            tile = pl.multiple_of(tile_ref[block] * LANES, LANES)
            cr = cur_ref[0:1, pl.ds(tile, LANES)]
            ci = cur_ref[1:2, pl.ds(tile, LANES)]
            br = blocks_ref[block, 0]
            bi = blocks_ref[block, 1]
            near_rows[0, pl.ds(k * row_dev, row_dev), :] = br * cr - bi * ci
            near_rows[1, pl.ds(k * row_dev, row_dev), :] = br * ci + bi * cr
            owner = jnp.where(lane // row_dev == k, dest_ref[block], owner)
        ones = jnp.ones((SUB, LANES), jnp.float32)
        for part in range(2):
            term = lax.dot_general(
                ones, near_rows[part], (((1,), (1,)), ((), ())),
                precision=lax.Precision.HIGHEST, preferred_element_type=jnp.float32,
            )
            for block in range(columns // SUB):
                place = pl.ds(pl.multiple_of(row_base + block * SUB, SUB), SUB)
                start[part, place, :] += jnp.where(owner == sub + block * SUB, term, 0.0)

    for group in range(devices // SUB):
        for c in range(3):
            points = tests_ref[pl.ds(group * SUB, SUB), c, :] * TURNS
            points = jnp.concatenate([points, jnp.zeros((SUB, LANES - row_dev), jnp.float32)], axis=1)
            tests_wide[c, pl.ds(group * SUB, SUB), :] = lane_repeat(points, row_dev)

    chunk = min(4, devices // SUB)
    soft = (SOFTENING * TURNS) ** 2

    def far(block, _):
        places = [pl.ds(pl.multiple_of((block * chunk + g) * SUB, SUB), SUB) for g in range(chunk)]
        tests = [[tests_wide[c, place, :] for c in range(3)] for place in places]

        def step(r, sums):
            sx, sy, sz, size, turn = [
                jnp.broadcast_to(source_rows[r, c : c + 1, :], (SUB, LANES)) for c in range(5)
            ]
            new = []
            for (tx, ty, tz), (re, im) in zip(tests, sums):
                dx = tx - sx
                dy = ty - sy
                dz = tz - sz
                square = dx * dx + dy * dy + (dz * dz + soft)
                inverse = lax.rsqrt(square)
                t = square * inverse - turn
                u = t - ((t + ROUNDER) - ROUNDER)
                u2 = u * u
                s = u * horner(SINE, u2)
                c = horner(COSINE, u2)
                a = inverse * size
                new.append((re + a * (1.0 - s * s), im + a * (s * c)))
            return tuple(new)

        sums = tuple((start[0, place, :], start[1, place, :]) for place in places)
        sums = lax.fori_loop(0, width // per_row, step, sums, unroll=2)
        for place, (re, im) in zip(places, sums):
            shift = LANES // 2
            while shift >= row_dev:
                re = re + pltpu.roll(re, shift, 1)
                im = im + pltpu.roll(im, shift, 1)
                shift //= 2
            out_ref[place, 0, :] = re[:, :row_dev]
            out_ref[place, 1, :] = im[:, :row_dev]
        return 0

    lax.fori_loop(0, devices // (SUB * chunk), far, 0)


def local(test_points, src_points, currents, near_blocks, near_dest, near_tile):
    row_dev = test_points.shape[1]
    width = src_points.shape[1]
    columns = lax.axis_size("col")
    devices = lax.axis_size("row") * columns
    copies = jnp.broadcast_to(test_points[None], (devices, 3, row_dev))
    tests = lax.all_to_all(copies, ("row", "col"), split_axis=0, concat_axis=0, tiled=True)
    vmem = pl.BlockSpec(memory_space=pltpu.VMEM)
    smem = pl.BlockSpec(memory_space=pltpu.SMEM)
    partial = pl.pallas_call(
        functools.partial(field_kernel, columns),
        out_shape=jax.ShapeDtypeStruct((devices, 2, row_dev), jnp.float32),
        in_specs=[smem, smem, vmem, vmem, vmem, pl.BlockSpec(memory_space=pl.ANY)],
        out_specs=vmem,
        scratch_shapes=[
            pltpu.VMEM((width * row_dev // LANES, SUB, LANES), jnp.float32),
            pltpu.VMEM((2, LANES, LANES), jnp.float32),
            pltpu.VMEM((2, devices, LANES), jnp.float32),
            pltpu.VMEM((SUB, width), jnp.float32),
            pltpu.VMEM((3, devices, LANES), jnp.float32),
            pltpu.VMEM(near_blocks.shape, jnp.float32),
            pltpu.SemaphoreType.DMA,
        ],
        compiler_params=pltpu.CompilerParams(vmem_limit_bytes=24 << 20),
    )(near_dest.reshape(-1), near_tile.reshape(-1), tests, src_points, currents, near_blocks)
    parts = lax.all_to_all(partial, ("row", "col"), split_axis=0, concat_axis=0, tiled=True)
    return parts.sum(axis=0)


def solution(mesh):
    in_specs = (
        P(None, ("row", "col")),
        P(None, ("row", "col")),
        P(None, ("row", "col")),
        P(("row", "col"), None, None, None),
        P(("row", "col"), None),
        P(("row", "col"), None),
    )
    out_specs = P(None, ("row", "col"))
    return jax.shard_map(local, mesh=mesh, in_specs=in_specs, out_specs=out_specs, check_vma=False)
```

```python
import functools
import math

import jax
import jax.numpy as jnp
import numpy as np
from jax import lax
from jax.experimental import pallas as pl
from jax.experimental.pallas import tpu as pltpu
from jax.sharding import PartitionSpec as P

WAVENUMBER = 40.0
SOFTENING = 0.01
TURNS = WAVENUMBER / (2.0 * math.pi)
LANES = 128
SUB = 8


def even_fit(function, terms, reach):
    nodes = np.cos((np.arange(400) + 0.5) * np.pi / 400)
    squares = (nodes + 1) * 0.5 * reach * reach
    fit = np.polynomial.chebyshev.Chebyshev.fit(squares, function(np.sqrt(squares)), terms - 1)
    return [float(value) for value in fit.convert(kind=np.polynomial.Polynomial).coef]


ROOT2 = math.sqrt(2.0)
SINE = even_fit(lambda u: ROOT2 * math.pi * np.sinc(u), 5, 0.5)
COSINE = even_fit(lambda u: -ROOT2 * np.cos(np.pi * u), 5, 0.5)
ROUNDER = 1.5 * 2.0**23


def horner(coefficients, x):
    total = coefficients[-1] * x + coefficients[-2]
    for value in coefficients[-3::-1]:
        total = total * x + value
    return total


def lane_repeat(x, period):
    width = period
    lane = lax.broadcasted_iota(jnp.int32, x.shape, 1)
    while width < LANES:
        x = jnp.where(lane < width, x, pltpu.roll(x, width, 1))
        width *= 2
    return x


def prepare_kernel(
    axes, dest_ref, tile_ref, src_ref, cur_ref, blocks_hbm, source_rows, start, near_rows, padded, blocks_ref, blocks_sem
):
    rows, columns = axes
    width = src_ref.shape[1]
    items, _, row_dev, _ = blocks_ref.shape
    per_row = LANES // row_dev
    tiles = width // LANES
    gain = TURNS / math.sqrt(width * rows * columns)
    lane = lax.broadcasted_iota(jnp.int32, (SUB, LANES), 1)
    sub = lax.broadcasted_iota(jnp.int32, (SUB, LANES), 0)
    blocks_copy = pltpu.make_async_copy(blocks_hbm, blocks_ref, blocks_sem)
    blocks_copy.start()

    padded[0:3, :] = src_ref[...] * TURNS
    cr = cur_ref[0:1, :]
    ci = cur_ref[1:2, :]
    padded[3:4, :] = jnp.sqrt(cr * cr + ci * ci) * gain
    padded[4:5, :] = jnp.arctan2(ci, cr) * (0.5 / math.pi)
    padded[5:8, :] = jnp.zeros((3, width), jnp.float32)
    pick = lane // row_dev
    for tile in range(tiles):
        x = padded[:, pl.ds(tile * LANES, LANES)]
        for j in range(row_dev):
            source_rows[tile * row_dev + j] = jnp.take_along_axis(x, pick + j * per_row, axis=1)

    blocks_copy.wait()
    start[...] = jnp.zeros_like(start)
    mine = lax.axis_index("col")
    for group in range(items // per_row):
        owner = jnp.zeros((SUB, LANES), jnp.int32)
        for k in range(per_row):
            block = group * per_row + k
            tile = pl.multiple_of(tile_ref[block] * LANES, LANES)
            cr = cur_ref[0:1, pl.ds(tile, LANES)]
            ci = cur_ref[1:2, pl.ds(tile, LANES)]
            br = blocks_ref[block, 0]
            bi = blocks_ref[block, 1]
            near_rows[0, pl.ds(k * row_dev, row_dev), :] = br * cr - bi * ci
            near_rows[1, pl.ds(k * row_dev, row_dev), :] = br * ci + bi * cr
            away = lax.rem(mine - dest_ref[block] + columns, columns) * rows
            owner = jnp.where(lane // row_dev == k, away, owner)
        ones = jnp.ones((SUB, LANES), jnp.float32)
        for part in range(2):
            term = lax.dot_general(
                ones, near_rows[part], (((1,), (1,)), ((), ())),
                precision=lax.Precision.HIGHEST, preferred_element_type=jnp.float32,
            )
            for block in range(rows * columns // SUB):
                place = pl.ds(block * SUB, SUB)
                start[part, place, :] += jnp.where(owner == sub + block * SUB, term, 0.0)


def far_kernel(axes, *refs):
    rows, columns = axes
    devices = rows * columns
    tests_refs, (source_rows, start, out_ref, tests_wide) = refs[:columns], refs[columns:]
    row_dev = out_ref.shape[2]
    lane = lax.broadcasted_iota(jnp.int32, (SUB, LANES), 1)

    per_group = SUB // rows
    for group in range(devices // SUB):
        for c in range(3):
            points = jnp.concatenate(
                [tests_refs[group * per_group + k][:, c, :] for k in range(per_group)], axis=0
            ) * TURNS
            points = jnp.concatenate([points, jnp.zeros((SUB, LANES - row_dev), jnp.float32)], axis=1)
            tests_wide[c, pl.ds(group * SUB, SUB), :] = lane_repeat(points, row_dev)

    chunk = min(4, devices // SUB)
    soft = (SOFTENING * TURNS) ** 2

    def far(block, _):
        places = [pl.ds(pl.multiple_of((block * chunk + g) * SUB, SUB), SUB) for g in range(chunk)]
        tests = [[tests_wide[c, place, :] for c in range(3)] for place in places]

        def step(r, sums):
            sx, sy, sz, size, turn = [
                jnp.broadcast_to(source_rows[r, c : c + 1, :], (SUB, LANES)) for c in range(5)
            ]
            new = []
            for (tx, ty, tz), (re, im) in zip(tests, sums):
                dx = tx - sx
                dy = ty - sy
                dz = tz - sz
                square = dx * dx + dy * dy + (dz * dz + soft)
                inverse = lax.rsqrt(square)
                t = square * inverse - turn
                u = t - ((t + ROUNDER) - ROUNDER)
                u2 = u * u
                s = u * horner(SINE, u2)
                c = horner(COSINE, u2)
                a = inverse * size
                new.append((re + a * (1.0 - s * s), im + a * (s * c)))
            return tuple(new)

        sums = tuple((start[0, place, :], start[1, place, :]) for place in places)
        sums = lax.fori_loop(0, source_rows.shape[0], step, sums, unroll=2)
        for place, (re, im) in zip(places, sums):
            shift = LANES // 2
            while shift >= row_dev:
                re = re + pltpu.roll(re, shift, 1)
                im = im + pltpu.roll(im, shift, 1)
                shift //= 2
            out_ref[place, 0, :] = re[:, :row_dev]
            out_ref[place, 1, :] = im[:, :row_dev]
        return 0

    lax.fori_loop(0, devices // (SUB * chunk), far, 0)


def forward(x, axis, size, steps):
    return lax.ppermute(x, axis, [(i, (i + steps) % size) for i in range(size)])


def local(rows, columns, test_points, src_points, currents, near_blocks, near_dest, near_tile):
    row_dev = test_points.shape[1]
    width = src_points.shape[1]
    devices = rows * columns
    vmem = pl.BlockSpec(memory_space=pltpu.VMEM)
    smem = pl.BlockSpec(memory_space=pltpu.SMEM)

    nearby = [test_points] + [forward(test_points, "row", rows, k) for k in range(1, rows)]
    nearby = jnp.stack(nearby)
    tests = [nearby] + [forward(nearby, "col", columns, k) for k in range(1, columns)]

    source_rows, start = pl.pallas_call(
        functools.partial(prepare_kernel, (rows, columns)),
        out_shape=(
            jax.ShapeDtypeStruct((width * row_dev // LANES, SUB, LANES), jnp.float32),
            jax.ShapeDtypeStruct((2, devices, LANES), jnp.float32),
        ),
        in_specs=[smem, smem, vmem, vmem, pl.BlockSpec(memory_space=pl.ANY)],
        out_specs=(vmem, vmem),
        scratch_shapes=[
            pltpu.VMEM((2, LANES, LANES), jnp.float32),
            pltpu.VMEM((SUB, width), jnp.float32),
            pltpu.VMEM(near_blocks.shape, jnp.float32),
            pltpu.SemaphoreType.DMA,
        ],
        compiler_params=pltpu.CompilerParams(vmem_limit_bytes=24 << 20),
        cost_estimate=pl.CostEstimate(flops=4 << 20, bytes_accessed=1 << 20, transcendentals=0),
    )(near_dest.reshape(-1), near_tile.reshape(-1), src_points, currents, near_blocks)

    partial = pl.pallas_call(
        functools.partial(far_kernel, (rows, columns)),
        out_shape=jax.ShapeDtypeStruct((devices, 2, row_dev), jnp.float32),
        in_specs=[vmem] * (columns + 2),
        out_specs=vmem,
        scratch_shapes=[pltpu.VMEM((3, devices, LANES), jnp.float32)],
        compiler_params=pltpu.CompilerParams(vmem_limit_bytes=24 << 20),
    )(*tests, source_rows, start)

    partial = partial.reshape(columns, rows, 2, row_dev)
    line = partial[0]
    for k in range(1, columns):
        line = line + forward(partial[k], "col", columns, columns - k)
    total = line[0]
    for k in range(1, rows):
        total = total + forward(line[k], "row", rows, rows - k)
    return total


def solution(mesh):
    in_specs = (
        P(None, ("row", "col")),
        P(None, ("row", "col")),
        P(None, ("row", "col")),
        P(("row", "col"), None, None, None),
        P(("row", "col"), None),
        P(("row", "col"), None),
    )
    out_specs = P(None, ("row", "col"))
    body = functools.partial(local, mesh.shape["row"], mesh.shape["col"])
    return jax.shard_map(body, mesh=mesh, in_specs=in_specs, out_specs=out_specs, check_vma=False)
```

```python
import functools
import math

import jax
import jax.numpy as jnp
import numpy as np
from jax import lax
from jax.experimental import pallas as pl
from jax.experimental.pallas import tpu as pltpu
from jax.sharding import PartitionSpec as P

WAVENUMBER = 40.0
SOFTENING = 0.01
TURNS = WAVENUMBER / (2.0 * math.pi)
LANES = 128
SUB = 8


def even_fit(function, terms, reach):
    nodes = np.cos((np.arange(400) + 0.5) * np.pi / 400)
    squares = (nodes + 1) * 0.5 * reach * reach
    fit = np.polynomial.chebyshev.Chebyshev.fit(squares, function(np.sqrt(squares)), terms - 1)
    return [float(value) for value in fit.convert(kind=np.polynomial.Polynomial).coef]


ROOT2 = math.sqrt(2.0)
SINE = even_fit(lambda u: ROOT2 * math.pi * np.sinc(u), 5, 0.5)
COSINE = even_fit(lambda u: -ROOT2 * np.cos(np.pi * u), 5, 0.5)
ROUNDER = 1.5 * 2.0**23


def horner(coefficients, x):
    total = coefficients[-1] * x + coefficients[-2]
    for value in coefficients[-3::-1]:
        total = total * x + value
    return total


def lane_repeat(x, period):
    width = period
    lane = lax.broadcasted_iota(jnp.int32, x.shape, 1)
    while width < LANES:
        x = jnp.where(lane < width, x, pltpu.roll(x, width, 1))
        width *= 2
    return x


def pack_kernel(copies, gain, tests_ref, src_ref, cur_ref, copies_ref, packed_ref):
    for member in range(copies):
        copies_ref[member] = tests_ref[...]
    packed_ref[0:3, :] = src_ref[...] * TURNS
    cr = cur_ref[0:1, :]
    ci = cur_ref[1:2, :]
    packed_ref[3:4, :] = jnp.sqrt(cr * cr + ci * ci) * gain
    packed_ref[4:5, :] = jnp.arctan2(ci, cr) * (0.5 / math.pi)
    packed_ref[5:8, :] = jnp.zeros((3, src_ref.shape[1]), jnp.float32)


def spread(packed_ref, rows_ref, row_dev, base):
    per_row = LANES // row_dev
    pick = lax.broadcasted_iota(jnp.int32, (SUB, LANES), 1) // row_dev
    for tile in range(packed_ref.shape[1] // LANES):
        x = packed_ref[:, pl.ds(tile * LANES, LANES)]
        for j in range(row_dev):
            rows_ref[base + tile * row_dev + j] = jnp.take_along_axis(x, pick + j * per_row, axis=1)


def prepare_kernel(columns, dest_ref, tile_ref, cur_ref, blocks_hbm, packed_ref, own_rows, start, near_rows, blocks_ref, blocks_sem):
    items, _, row_dev, _ = blocks_ref.shape
    per_row = LANES // row_dev
    lane = lax.broadcasted_iota(jnp.int32, (SUB, LANES), 1)
    sub = lax.broadcasted_iota(jnp.int32, (SUB, LANES), 0)
    blocks_copy = pltpu.make_async_copy(blocks_hbm, blocks_ref, blocks_sem)
    blocks_copy.start()
    spread(packed_ref, own_rows, row_dev, 0)

    blocks_copy.wait()
    start[...] = jnp.zeros_like(start)
    base = lax.axis_index("x") * columns
    for group in range(items // per_row):
        owner = jnp.zeros((SUB, LANES), jnp.int32)
        for k in range(per_row):
            block = group * per_row + k
            tile = pl.multiple_of(tile_ref[block] * LANES, LANES)
            cr = cur_ref[0:1, pl.ds(tile, LANES)]
            ci = cur_ref[1:2, pl.ds(tile, LANES)]
            br = blocks_ref[block, 0]
            bi = blocks_ref[block, 1]
            near_rows[0, pl.ds(k * row_dev, row_dev), :] = br * cr - bi * ci
            near_rows[1, pl.ds(k * row_dev, row_dev), :] = br * ci + bi * cr
            owner = jnp.where(lane // row_dev == k, dest_ref[block], owner)
        ones = jnp.ones((SUB, LANES), jnp.float32)
        for part in range(2):
            term = lax.dot_general(
                ones, near_rows[part], (((1,), (1,)), ((), ())),
                precision=lax.Precision.HIGHEST, preferred_element_type=jnp.float32,
            )
            for block in range(columns // SUB):
                place = pl.ds(pl.multiple_of(base + block * SUB, SUB), SUB)
                start[part, place, :] += jnp.where(owner == sub + block * SUB, term, 0.0)


def far_kernel(tests_ref, own_rows, other_ref, start, out_ref, tests_wide, other_rows):
    members, _, row_dev = tests_ref.shape
    lane = lax.broadcasted_iota(jnp.int32, (SUB, LANES), 1)
    spread(other_ref, other_rows, row_dev, 0)

    for group in range(members // SUB):
        for c in range(3):
            points = tests_ref[pl.ds(group * SUB, SUB), c, :] * TURNS
            points = jnp.concatenate([points, jnp.zeros((SUB, LANES - row_dev), jnp.float32)], axis=1)
            tests_wide[c, pl.ds(group * SUB, SUB), :] = lane_repeat(points, row_dev)

    chunk = min(4, members // SUB)
    soft = (SOFTENING * TURNS) ** 2

    def far(block, _):
        places = [pl.ds(pl.multiple_of((block * chunk + g) * SUB, SUB), SUB) for g in range(chunk)]
        tests = [[tests_wide[c, place, :] for c in range(3)] for place in places]

        def step(r, sums):
            for source_rows in (own_rows, other_rows):
                sx, sy, sz, size, turn = [
                    jnp.broadcast_to(source_rows[r, c : c + 1, :], (SUB, LANES)) for c in range(5)
                ]
                new = []
                for (tx, ty, tz), (re, im) in zip(tests, sums):
                    dx = tx - sx
                    dy = ty - sy
                    dz = tz - sz
                    square = dx * dx + dy * dy + (dz * dz + soft)
                    inverse = lax.rsqrt(square)
                    t = square * inverse - turn
                    u = t - ((t + ROUNDER) - ROUNDER)
                    u2 = u * u
                    s = u * horner(SINE, u2)
                    c = horner(COSINE, u2)
                    a = inverse * size
                    new.append((re + a * (1.0 - s * s), im + a * (s * c)))
                sums = tuple(new)
            return sums

        sums = tuple((start[0, place, :], start[1, place, :]) for place in places)
        sums = lax.fori_loop(0, own_rows.shape[0], step, sums, unroll=2)
        for place, (re, im) in zip(places, sums):
            shift = LANES // 2
            while shift >= row_dev:
                re = re + pltpu.roll(re, shift, 1)
                im = im + pltpu.roll(im, shift, 1)
                shift //= 2
            out_ref[place, 0, :] = re[:, :row_dev]
            out_ref[place, 1, :] = im[:, :row_dev]
        return 0

    lax.fori_loop(0, members // (SUB * chunk), far, 0)


def local(members, columns, test_points, src_points, currents, near_blocks, near_dest, near_tile):
    row_dev = test_points.shape[1]
    width = src_points.shape[1]
    devices = members * 2
    gain = TURNS / math.sqrt(width * devices)
    vmem = pl.BlockSpec(memory_space=pltpu.VMEM)
    smem = pl.BlockSpec(memory_space=pltpu.SMEM)
    params = pltpu.CompilerParams(vmem_limit_bytes=24 << 20)
    rows_shape = (width * row_dev // LANES, SUB, LANES)

    copies, packed = pl.pallas_call(
        functools.partial(pack_kernel, members, gain),
        out_shape=(
            jax.ShapeDtypeStruct((members, 3, row_dev), jnp.float32),
            jax.ShapeDtypeStruct((SUB, width), jnp.float32),
        ),
        in_specs=[vmem, vmem, vmem],
        out_specs=(vmem, vmem),
        compiler_params=params,
    )(test_points, src_points, currents)
    other = lax.ppermute(packed, "core", [(0, 1), (1, 0)])
    tests = lax.all_to_all(copies, ("x", "col"), split_axis=0, concat_axis=0, tiled=True)

    own_rows, start = pl.pallas_call(
        functools.partial(prepare_kernel, columns),
        out_shape=(
            jax.ShapeDtypeStruct(rows_shape, jnp.float32),
            jax.ShapeDtypeStruct((2, members, LANES), jnp.float32),
        ),
        in_specs=[smem, smem, vmem, pl.BlockSpec(memory_space=pl.ANY), vmem],
        out_specs=(vmem, vmem),
        scratch_shapes=[
            pltpu.VMEM((2, LANES, LANES), jnp.float32),
            pltpu.VMEM(near_blocks.shape, jnp.float32),
            pltpu.SemaphoreType.DMA,
        ],
        compiler_params=params,
        cost_estimate=pl.CostEstimate(flops=4 << 20, bytes_accessed=1 << 20, transcendentals=0),
    )(near_dest.reshape(-1), near_tile.reshape(-1), currents, near_blocks, packed)

    partial = pl.pallas_call(
        far_kernel,
        out_shape=jax.ShapeDtypeStruct((members, 2, row_dev), jnp.float32),
        in_specs=[vmem] * 4,
        out_specs=vmem,
        scratch_shapes=[
            pltpu.VMEM((3, members, LANES), jnp.float32),
            pltpu.VMEM(rows_shape, jnp.float32),
        ],
        compiler_params=params,
    )(tests, own_rows, other, start)
    parts = lax.all_to_all(partial, ("x", "col"), split_axis=0, concat_axis=0, tiled=True)
    return parts.sum(axis=0)


def solution(mesh):
    rows, columns = mesh.shape["row"], mesh.shape["col"]
    finer = jax.sharding.Mesh(mesh.devices.reshape(rows // 2, 2, columns), ("x", "core", "col"))
    every = ("x", "core", "col")
    in_specs = (
        P(None, every),
        P(None, every),
        P(None, every),
        P(every, None, None, None),
        P(every, None),
        P(every, None),
    )
    body = functools.partial(local, rows // 2 * columns, columns)
    return jax.shard_map(body, mesh=finer, in_specs=in_specs, out_specs=P(None, every), check_vma=False)
```

```python
import functools
import math

import jax
import jax.numpy as jnp
import numpy as np
from jax import lax
from jax.experimental import pallas as pl
from jax.experimental.pallas import tpu as pltpu
from jax.sharding import PartitionSpec as P

WAVENUMBER = 40.0
SOFTENING = 0.01
TURNS = WAVENUMBER / (2.0 * math.pi)
LANES = 128
SUB = 8


def even_fit(function, terms, reach):
    nodes = np.cos((np.arange(400) + 0.5) * np.pi / 400)
    squares = (nodes + 1) * 0.5 * reach * reach
    fit = np.polynomial.chebyshev.Chebyshev.fit(squares, function(np.sqrt(squares)), terms - 1)
    return [float(value) for value in fit.convert(kind=np.polynomial.Polynomial).coef]


ROOT2 = math.sqrt(2.0)
SINE = even_fit(lambda u: ROOT2 * math.pi * np.sinc(u), 5, 0.5)
COSINE = even_fit(lambda u: -ROOT2 * np.cos(np.pi * u), 5, 0.5)
ROUNDER = 1.5 * 2.0**23


def horner(coefficients, x):
    total = coefficients[-1] * x + coefficients[-2]
    for value in coefficients[-3::-1]:
        total = total * x + value
    return total


def pack_kernel(
    half_columns, gain, dest_hbm, tile_hbm, src_hbm, cur_hbm, blocks_hbm, copies_ref,
    dest_ref, tile_ref, src_ref, cur_ref, blocks_ref, message, near_rows, near_all, sems
):
    moves = [
        pltpu.make_async_copy(source, target, sems.at[k])
        for k, (source, target) in enumerate((
            (src_hbm, src_ref), (cur_hbm, cur_ref), (blocks_hbm, blocks_ref), (dest_hbm, dest_ref), (tile_hbm, tile_ref)
        ))
    ]
    for move in moves:
        move.start()
    members = copies_ref.shape[0]
    tiles = src_ref.shape[1] // LANES
    items, _, row_dev, _ = blocks_ref.shape
    per_row = LANES // row_dev
    columns = 2 * half_columns
    lane = lax.broadcasted_iota(jnp.int32, (SUB, LANES), 1)
    sub = lax.broadcasted_iota(jnp.int32, (SUB, LANES), 0)

    message[5 * tiles :, :] = jnp.zeros((message.shape[0] - 5 * tiles, LANES), jnp.float32)
    near_all[...] = jnp.zeros_like(near_all)
    moves[0].wait()
    moves[1].wait()
    for tile in range(tiles):
        part = pl.ds(tile * LANES, LANES)
        for c in range(3):
            message[c * tiles + tile : c * tiles + tile + 1, :] = src_ref[c : c + 1, part] * TURNS
        for c in range(2):
            message[(3 + c) * tiles + tile : (3 + c) * tiles + tile + 1, :] = cur_ref[c : c + 1, part]
    cr = message[3 * tiles : 4 * tiles, :]
    ci = message[4 * tiles : 5 * tiles, :]
    message[3 * tiles : 4 * tiles, :] = jnp.sqrt(cr * cr + ci * ci) * gain
    message[4 * tiles : 5 * tiles, :] = jnp.arctan2(ci, cr) * (0.5 / math.pi)

    def copy(member, _):
        copies_ref[member] = message[...]
        return 0

    lax.fori_loop(0, members, copy, 0, unroll=4)

    for move in moves[2:]:
        move.wait()
    for group in range(items // per_row):
        owner = jnp.zeros((SUB, LANES), jnp.int32)
        for k in range(per_row):
            block = group * per_row + k
            tile = pl.multiple_of(tile_ref[block] * LANES, LANES)
            cr = cur_ref[0:1, pl.ds(tile, LANES)]
            ci = cur_ref[1:2, pl.ds(tile, LANES)]
            br = blocks_ref[block, 0]
            bi = blocks_ref[block, 1]
            near_rows[pl.ds(k * row_dev, row_dev), :] = br * cr - bi * ci
            near_rows[pl.ds(LANES + k * row_dev, row_dev), :] = br * ci + bi * cr
            owner = jnp.where(lane // row_dev == k, dest_ref[block], owner)
        terms = lax.dot_general(
            jnp.ones((SUB, LANES), jnp.float32), near_rows[...], (((1,), (1,)), ((), ())),
            precision=lax.Precision.HIGHEST, preferred_element_type=jnp.float32,
        )
        for block in range(columns // SUB):
            place = pl.ds(block * SUB, SUB)
            mine = owner == sub + block * SUB
            near_all[0, place, :] += jnp.where(mine, terms[:, :LANES], 0.0)
            near_all[1, place, :] += jnp.where(mine, terms[:, LANES:], 0.0)
    for block in range(columns // SUB):
        place = pl.ds(block * SUB, SUB)
        re = near_all[0, place, :]
        im = near_all[1, place, :]
        shift = LANES // 2
        while shift >= row_dev:
            re = re + pltpu.roll(re, shift, 1)
            im = im + pltpu.roll(im, shift, 1)
            shift //= 2
        near_all[0, place, :] = jnp.where(lane < row_dev, re, jnp.where(lane < 2 * row_dev, im, 0.0))
    base = lax.axis_index("row") * half_columns
    for k in range(half_columns):
        for half in range(2):
            spot = 5 * tiles + half
            copies_ref[base + k, spot : spot + 1, :] = near_all[0, half * half_columns + k : half * half_columns + k + 1, :]


def far_kernel(half_columns, other, tests_ref, messages_ref, out_ref):
    members = messages_ref.shape[0]
    tiles = (messages_ref.shape[1] - SUB) // 5
    row_dev = tests_ref.shape[1]
    groups = row_dev // SUB
    lane = lax.broadcasted_iota(jnp.int32, (row_dev, LANES), 1)
    sub = lax.broadcasted_iota(jnp.int32, (row_dev, LANES), 0)
    soft = (SOFTENING * TURNS) ** 2

    points = jnp.concatenate([tests_ref[...], jnp.zeros((3, LANES - row_dev), jnp.float32)], axis=1) * TURNS
    tests = []
    for c in range(3):
        column = jnp.sum(jnp.where(lane == sub, points[c : c + 1, :], 0.0), axis=1, keepdims=True)
        wide = jnp.broadcast_to(column, (row_dev, LANES))
        tests.append([wide[g * SUB : (g + 1) * SUB] for g in range(groups)])

    def step(member, sums):
        for tile in range(tiles):
            sx, sy, sz, size, turn = [
                jnp.broadcast_to(messages_ref[member, c * tiles + tile : c * tiles + tile + 1, :], (SUB, LANES))
                for c in range(5)
            ]
            new = []
            for g, (re, im) in enumerate(sums):
                dx = tests[0][g] - sx
                dy = tests[1][g] - sy
                dz = tests[2][g] - sz
                square = dx * dx + dy * dy + (dz * dz + soft)
                inverse = lax.rsqrt(square)
                t = square * inverse - turn
                u = t - ((t + ROUNDER) - ROUNDER)
                u2 = u * u
                s = u * horner(SINE, u2)
                c = horner(COSINE, u2)
                a = inverse * size
                new.append((re + a * (1.0 - s * s), im + a * (s * c)))
            sums = tuple(new)
        return sums

    zero = jnp.zeros((SUB, LANES), jnp.float32)
    sums = lax.fori_loop(0, members, step, tuple((zero, zero) for _ in range(groups)))
    re, im = [
        jnp.concatenate([jnp.sum(pair[part], axis=1, keepdims=True) for pair in sums], axis=0) for part in range(2)
    ]
    both = jnp.where(lane == sub, re, jnp.where(lane == sub + row_dev, im, 0.0))
    both = jnp.sum(both, axis=0, keepdims=True)
    half = lax.axis_index("half")
    spot = 5 * tiles + (1 - half if other else half)
    base = lax.axis_index("row") * half_columns
    for k in range(half_columns):
        both = both + messages_ref[base + k, pl.ds(spot, 1), :]
    out_ref[0:1, :] = both[:, :row_dev]
    out_ref[1:2, :] = both[:, row_dev : 2 * row_dev]


def swap(x):
    return lax.ppermute(x, "half", [(0, 1), (1, 0)])


def local(rows, half_columns, test_points, src_points, currents, near_blocks, near_dest, near_tile):
    row_dev = test_points.shape[1]
    width = src_points.shape[1]
    items = near_blocks.shape[0]
    members = rows * half_columns
    gain = TURNS / math.sqrt(width * members * 2)
    message = (5 * width // LANES + SUB, LANES)
    vmem = pl.BlockSpec(memory_space=pltpu.VMEM)
    hbm = pl.BlockSpec(memory_space=pltpu.HBM)
    params = pltpu.CompilerParams(vmem_limit_bytes=24 << 20)

    partner_points = swap(test_points)
    copies = pl.pallas_call(
        functools.partial(pack_kernel, half_columns, gain),
        out_shape=jax.ShapeDtypeStruct((members,) + message, jnp.float32),
        in_specs=[hbm] * 5,
        out_specs=vmem,
        scratch_shapes=[
            pltpu.SMEM((items,), jnp.int32),
            pltpu.SMEM((items,), jnp.int32),
            pltpu.VMEM((3, width), jnp.float32),
            pltpu.VMEM((2, width), jnp.float32),
            pltpu.VMEM(near_blocks.shape, jnp.float32),
            pltpu.VMEM(message, jnp.float32),
            pltpu.VMEM((2 * LANES, LANES), jnp.float32),
            pltpu.VMEM((2, 2 * half_columns, LANES), jnp.float32),
            pltpu.SemaphoreType.DMA((5,)),
        ],
        compiler_params=params,
        cost_estimate=pl.CostEstimate(flops=1 << 20, bytes_accessed=1 << 20, transcendentals=0),
    )(near_dest.reshape(-1), near_tile.reshape(-1), src_points, currents, near_blocks)
    messages = lax.all_to_all(copies, ("row", "column"), split_axis=0, concat_axis=0, tiled=True)

    def far(points, other):
        evaluations = width * members * row_dev
        return pl.pallas_call(
            functools.partial(far_kernel, half_columns, other),
            out_shape=jax.ShapeDtypeStruct((2, row_dev), jnp.float32),
            in_specs=[vmem, vmem],
            out_specs=vmem,
            compiler_params=params,
            cost_estimate=pl.CostEstimate(flops=40 * evaluations, bytes_accessed=4 << 20, transcendentals=evaluations),
        )(points, messages)

    from_partner = swap(far(partner_points, True))
    return far(test_points, False) + from_partner


def solution(mesh):
    rows, columns = mesh.shape["row"], mesh.shape["col"]
    finer = jax.sharding.Mesh(mesh.devices.reshape(rows, 2, columns // 2), ("row", "half", "column"))
    every = ("row", "half", "column")
    in_specs = (
        P(None, every),
        P(None, every),
        P(None, every),
        P(every, None, None, None),
        P(every, None),
        P(every, None),
    )
    body = functools.partial(local, rows, columns // 2)
    return jax.shard_map(body, mesh=finer, in_specs=in_specs, out_specs=P(None, every), check_vma=False)
```

```python
import functools
import math

import jax
import jax.numpy as jnp
import numpy as np
from jax import lax
from jax.experimental import pallas as pl
from jax.experimental.pallas import tpu as pltpu
from jax.sharding import PartitionSpec as P

WAVENUMBER = 40.0
SOFTENING = 0.01
TURNS = WAVENUMBER / (2.0 * math.pi)
LANES = 128
SUB = 8


def even_fit(function, terms, reach):
    nodes = np.cos((np.arange(400) + 0.5) * np.pi / 400)
    squares = (nodes + 1) * 0.5 * reach * reach
    fit = np.polynomial.chebyshev.Chebyshev.fit(squares, function(np.sqrt(squares)), terms - 1)
    return [float(value) for value in fit.convert(kind=np.polynomial.Polynomial).coef]


ROOT2 = math.sqrt(2.0)
SINE = even_fit(lambda u: ROOT2 * math.pi * np.sinc(u), 4, 0.5)
COSINE = even_fit(lambda u: -ROOT2 * np.cos(np.pi * u), 5, 0.5)
ROUNDER = 1.5 * 2.0**23


def horner(coefficients, x):
    total = coefficients[-1] * x + coefficients[-2]
    for value in coefficients[-3::-1]:
        total = total * x + value
    return total


def pack_kernel(
    half_columns, gain, dest_hbm, tile_hbm, src_hbm, cur_hbm, blocks_hbm, copies_ref,
    dest_ref, tile_ref, src_ref, cur_ref, blocks_ref, message, near_all, sems
):
    moves = [
        pltpu.make_async_copy(source, target, sems.at[k])
        for k, (source, target) in enumerate((
            (src_hbm, src_ref), (cur_hbm, cur_ref), (blocks_hbm, blocks_ref), (dest_hbm, dest_ref), (tile_hbm, tile_ref)
        ))
    ]
    for move in moves:
        move.start()
    members = copies_ref.shape[0]
    tiles = src_ref.shape[1] // LANES
    items, _, row_dev, _ = blocks_ref.shape
    per_row = LANES // row_dev
    columns = 2 * half_columns
    lane = lax.broadcasted_iota(jnp.int32, (SUB, LANES), 1)
    sub = lax.broadcasted_iota(jnp.int32, (SUB, LANES), 0)

    message[5 * tiles :, :] = jnp.zeros((message.shape[0] - 5 * tiles, LANES), jnp.float32)
    near_all[...] = jnp.zeros_like(near_all)
    moves[0].wait()
    moves[1].wait()
    for tile in range(tiles):
        part = pl.ds(tile * LANES, LANES)
        for c in range(3):
            message[c * tiles + tile : c * tiles + tile + 1, :] = src_ref[c : c + 1, part] * TURNS
        for c in range(2):
            message[(3 + c) * tiles + tile : (3 + c) * tiles + tile + 1, :] = cur_ref[c : c + 1, part]
    cr = message[3 * tiles : 4 * tiles, :]
    ci = message[4 * tiles : 5 * tiles, :]
    message[3 * tiles : 4 * tiles, :] = jnp.sqrt(cr * cr + ci * ci) * gain
    message[4 * tiles : 5 * tiles, :] = jnp.arctan2(ci, cr) * (0.5 / math.pi)

    def copy(member, _):
        copies_ref[member] = message[...]
        return 0

    lax.fori_loop(0, members, copy, 0, unroll=4)

    for move in moves[2:]:
        move.wait()
    for group in range(items // per_row):
        owner = jnp.zeros((SUB, LANES), jnp.int32)
        sums = [jnp.zeros((SUB, LANES), jnp.float32)] * 2
        for k in range(per_row):
            block = group * per_row + k
            tile = pl.multiple_of(tile_ref[block] * LANES, LANES)
            cr = cur_ref[0:1, pl.ds(tile, LANES)]
            ci = cur_ref[1:2, pl.ds(tile, LANES)]
            br = blocks_ref[block, 0]
            bi = blocks_ref[block, 1]
            for part, product in enumerate((br * cr - bi * ci, br * ci + bi * cr)):
                total = jnp.sum(product, axis=1, keepdims=True)
                for piece in range(row_dev // SUB):
                    spot = lane == sub + (k * row_dev + piece * SUB)
                    sums[part] = jnp.where(spot, total[piece * SUB : (piece + 1) * SUB], sums[part])
            owner = jnp.where(lane // row_dev == k, dest_ref[block], owner)
        terms = [jnp.sum(x, axis=0, keepdims=True) for x in sums]
        for block in range(columns // SUB):
            place = pl.ds(block * SUB, SUB)
            mine = owner == sub + block * SUB
            for part in range(2):
                near_all[part, place, :] += jnp.where(mine, terms[part], 0.0)
    for block in range(columns // SUB):
        place = pl.ds(block * SUB, SUB)
        re = near_all[0, place, :]
        im = near_all[1, place, :]
        shift = LANES // 2
        while shift >= row_dev:
            re = re + pltpu.roll(re, shift, 1)
            im = im + pltpu.roll(im, shift, 1)
            shift //= 2
        near_all[0, place, :] = jnp.where(lane < row_dev, re, jnp.where(lane < 2 * row_dev, im, 0.0))
    base = lax.axis_index("row") * half_columns
    for k in range(half_columns):
        for half in range(2):
            spot = 5 * tiles + half
            copies_ref[base + k, spot : spot + 1, :] = near_all[0, half * half_columns + k : half * half_columns + k + 1, :]


def far_kernel(half_columns, other, tests_ref, messages_ref, out_ref):
    members = messages_ref.shape[0]
    tiles = (messages_ref.shape[1] - SUB) // 5
    row_dev = tests_ref.shape[1]
    groups = row_dev // SUB
    lane = lax.broadcasted_iota(jnp.int32, (row_dev, LANES), 1)
    sub = lax.broadcasted_iota(jnp.int32, (row_dev, LANES), 0)
    soft = (SOFTENING * TURNS) ** 2

    points = jnp.concatenate([tests_ref[...], jnp.zeros((3, LANES - row_dev), jnp.float32)], axis=1) * TURNS
    tests = []
    for c in range(3):
        column = jnp.sum(jnp.where(lane == sub, points[c : c + 1, :], 0.0), axis=1, keepdims=True)
        wide = jnp.broadcast_to(column, (row_dev, LANES))
        tests.append([wide[g * SUB : (g + 1) * SUB] for g in range(groups)])

    def step(member, sums):
        for tile in range(tiles):
            sx, sy, sz, size, turn = [
                jnp.broadcast_to(messages_ref[member, c * tiles + tile : c * tiles + tile + 1, :], (SUB, LANES))
                for c in range(5)
            ]
            new = []
            for g, (re, im) in enumerate(sums):
                dx = tests[0][g] - sx
                dy = tests[1][g] - sy
                dz = tests[2][g] - sz
                square = dx * dx + dy * dy + (dz * dz + soft)
                inverse = lax.rsqrt(square)
                t = square * inverse - turn
                u = t - ((t + ROUNDER) - ROUNDER)
                u2 = u * u
                s = u * horner(SINE, u2)
                c = horner(COSINE, u2)
                a = inverse * size
                p = a * s
                new.append(((re + a) - p * s, im + p * c))
            sums = tuple(new)
        return sums

    zero = jnp.zeros((SUB, LANES), jnp.float32)
    sums = lax.fori_loop(0, members, step, tuple((zero, zero) for _ in range(groups)), unroll=2)
    re, im = [
        jnp.concatenate([jnp.sum(pair[part], axis=1, keepdims=True) for pair in sums], axis=0) for part in range(2)
    ]
    both = jnp.where(lane == sub, re, jnp.where(lane == sub + row_dev, im, 0.0))
    both = jnp.sum(both, axis=0, keepdims=True)
    half = lax.axis_index("half")
    spot = 5 * tiles + (1 - half if other else half)
    base = lax.axis_index("row") * half_columns
    for k in range(half_columns):
        both = both + messages_ref[base + k, pl.ds(spot, 1), :]
    out_ref[0:1, :] = both[:, :row_dev]
    out_ref[1:2, :] = both[:, row_dev : 2 * row_dev]


def swap(x):
    return lax.ppermute(x, "half", [(0, 1), (1, 0)])


def local(rows, half_columns, test_points, src_points, currents, near_blocks, near_dest, near_tile):
    row_dev = test_points.shape[1]
    width = src_points.shape[1]
    items = near_blocks.shape[0]
    members = rows * half_columns
    gain = TURNS / math.sqrt(width * members * 2)
    message = (5 * width // LANES + SUB, LANES)
    vmem = pl.BlockSpec(memory_space=pltpu.VMEM)
    hbm = pl.BlockSpec(memory_space=pltpu.HBM)
    params = pltpu.CompilerParams(vmem_limit_bytes=24 << 20)

    partner_points = swap(test_points)
    copies = pl.pallas_call(
        functools.partial(pack_kernel, half_columns, gain),
        out_shape=jax.ShapeDtypeStruct((members,) + message, jnp.float32),
        in_specs=[hbm] * 5,
        out_specs=vmem,
        scratch_shapes=[
            pltpu.SMEM((items,), jnp.int32),
            pltpu.SMEM((items,), jnp.int32),
            pltpu.VMEM((3, width), jnp.float32),
            pltpu.VMEM((2, width), jnp.float32),
            pltpu.VMEM(near_blocks.shape, jnp.float32),
            pltpu.VMEM(message, jnp.float32),
            pltpu.VMEM((2, 2 * half_columns, LANES), jnp.float32),
            pltpu.SemaphoreType.DMA((5,)),
        ],
        cost_estimate=pl.CostEstimate(flops=1 << 20, bytes_accessed=1 << 20, transcendentals=0),
    )(near_dest.reshape(-1), near_tile.reshape(-1), src_points, currents, near_blocks)
    messages = lax.all_to_all(copies, ("row", "column"), split_axis=0, concat_axis=0, tiled=True)

    def far(points, other):
        evaluations = width * members * row_dev
        return pl.pallas_call(
            functools.partial(far_kernel, half_columns, other),
            out_shape=jax.ShapeDtypeStruct((2, row_dev), jnp.float32),
            in_specs=[vmem, vmem],
            out_specs=vmem,
            compiler_params=params,
            cost_estimate=pl.CostEstimate(flops=40 * evaluations, bytes_accessed=4 << 20, transcendentals=evaluations),
        )(points, messages)

    from_partner = swap(far(partner_points, True))
    return far(test_points, False) + from_partner


def solution(mesh):
    rows, columns = mesh.shape["row"], mesh.shape["col"]
    finer = jax.sharding.Mesh(mesh.devices.reshape(rows, 2, columns // 2), ("row", "half", "column"))
    every = ("row", "half", "column")
    in_specs = (
        P(None, every),
        P(None, every),
        P(None, every),
        P(every, None, None, None),
        P(every, None),
        P(every, None),
    )
    body = functools.partial(local, rows, columns // 2)
    return jax.shard_map(body, mesh=finer, in_specs=in_specs, out_specs=P(None, every), check_vma=False)
```

```python
import functools
import math

import jax
import jax.numpy as jnp
import numpy as np
from jax import lax
from jax.experimental import pallas as pl
from jax.experimental.pallas import tpu as pltpu
from jax.sharding import PartitionSpec as P

WAVENUMBER = 40.0
SOFTENING = 0.01
TURNS = WAVENUMBER / (2.0 * math.pi)
LANES = 128
SUB = 8


def even_fit(function, terms, reach):
    nodes = np.cos((np.arange(400) + 0.5) * np.pi / 400)
    squares = (nodes + 1) * 0.5 * reach * reach
    fit = np.polynomial.chebyshev.Chebyshev.fit(squares, function(np.sqrt(squares)), terms - 1)
    return [float(value) for value in fit.convert(kind=np.polynomial.Polynomial).coef]


ROOT2 = math.sqrt(2.0)
SINE = even_fit(lambda u: ROOT2 * math.pi * np.sinc(u), 4, 0.5)
COSINE = even_fit(lambda u: -ROOT2 * np.cos(np.pi * u), 5, 0.5)
ROUNDER = 1.5 * 2.0**23


def horner(coefficients, x):
    total = coefficients[-1] * x + coefficients[-2]
    for value in coefficients[-3::-1]:
        total = total * x + value
    return total


def pack_kernel(
    half_columns, gain, dest_hbm, tile_hbm, src_hbm, cur_hbm, blocks_hbm, copies_ref,
    dest_ref, tile_ref, src_ref, cur_ref, blocks_ref, message, near_all, sems
):
    moves = [
        pltpu.make_async_copy(source, target, sems.at[k])
        for k, (source, target) in enumerate((
            (src_hbm, src_ref), (cur_hbm, cur_ref), (blocks_hbm, blocks_ref), (dest_hbm, dest_ref), (tile_hbm, tile_ref)
        ))
    ]
    for move in moves:
        move.start()
    members = copies_ref.shape[0]
    tiles = src_ref.shape[1] // LANES
    items, _, row_dev, _ = blocks_ref.shape
    per_row = LANES // row_dev
    columns = 2 * half_columns
    lane = lax.broadcasted_iota(jnp.int32, (SUB, LANES), 1)
    sub = lax.broadcasted_iota(jnp.int32, (SUB, LANES), 0)

    message[5 * tiles :, :] = jnp.zeros((message.shape[0] - 5 * tiles, LANES), jnp.float32)
    near_all[...] = jnp.zeros_like(near_all)
    for move in moves:
        move.wait()

    for group in range(items // per_row):
        owner = jnp.zeros((SUB, LANES), jnp.int32)
        sums = [jnp.zeros((SUB, LANES), jnp.float32)] * 2
        for k in range(per_row):
            block = group * per_row + k
            tile = pl.multiple_of(tile_ref[block] * LANES, LANES)
            cr = cur_ref[0:1, pl.ds(tile, LANES)]
            ci = cur_ref[1:2, pl.ds(tile, LANES)]
            br = blocks_ref[block, 0]
            bi = blocks_ref[block, 1]
            for part, product in enumerate((br * cr - bi * ci, br * ci + bi * cr)):
                total = jnp.sum(product, axis=1, keepdims=True)
                for piece in range(row_dev // SUB):
                    spot = lane == sub + (k * row_dev + piece * SUB)
                    sums[part] = jnp.where(spot, total[piece * SUB : (piece + 1) * SUB], sums[part])
            owner = jnp.where(lane // row_dev == k, dest_ref[block], owner)
        terms = [jnp.sum(x, axis=0, keepdims=True) for x in sums]
        for block in range(columns // SUB):
            place = pl.ds(block * SUB, SUB)
            mine = owner == sub + block * SUB
            for part in range(2):
                near_all[part, place, :] += jnp.where(mine, terms[part], 0.0)
    for block in range(columns // SUB):
        place = pl.ds(block * SUB, SUB)
        re = near_all[0, place, :]
        im = near_all[1, place, :]
        shift = LANES // 2
        while shift >= row_dev:
            re = re + pltpu.roll(re, shift, 1)
            im = im + pltpu.roll(im, shift, 1)
            shift //= 2
        near_all[0, place, :] = jnp.where(lane < row_dev, re, jnp.where(lane < 2 * row_dev, im, 0.0))

    for tile in range(tiles):
        part = pl.ds(tile * LANES, LANES)
        for c in range(3):
            message[c * tiles + tile : c * tiles + tile + 1, :] = src_ref[c : c + 1, part] * TURNS
        for c in range(2):
            message[(3 + c) * tiles + tile : (3 + c) * tiles + tile + 1, :] = cur_ref[c : c + 1, part]
    cr = message[3 * tiles : 4 * tiles, :]
    ci = message[4 * tiles : 5 * tiles, :]
    message[3 * tiles : 4 * tiles, :] = jnp.sqrt(cr * cr + ci * ci) * gain
    message[4 * tiles : 5 * tiles, :] = jnp.arctan2(ci, cr) * (0.5 / math.pi)

    def copy(member, _):
        copies_ref[member] = message[...]
        return 0

    lax.fori_loop(0, members, copy, 0, unroll=16)

    base = lax.axis_index("row") * half_columns
    for k in range(half_columns):
        for half in range(2):
            spot = 5 * tiles + half
            copies_ref[base + k, spot : spot + 1, :] = near_all[0, half * half_columns + k : half * half_columns + k + 1, :]


def far_sums(half_columns, other, tests_ref, messages_ref, out_ref):
    members = messages_ref.shape[0]
    tiles = (messages_ref.shape[1] - SUB) // 5
    row_dev = tests_ref.shape[1]
    groups = row_dev // SUB
    lane = lax.broadcasted_iota(jnp.int32, (row_dev, LANES), 1)
    sub = lax.broadcasted_iota(jnp.int32, (row_dev, LANES), 0)
    soft = (SOFTENING * TURNS) ** 2

    points = jnp.concatenate([tests_ref[...], jnp.zeros((3, LANES - row_dev), jnp.float32)], axis=1) * TURNS
    tests = []
    for c in range(3):
        column = jnp.sum(jnp.where(lane == sub, points[c : c + 1, :], 0.0), axis=1, keepdims=True)
        wide = jnp.broadcast_to(column, (row_dev, LANES))
        tests.append([wide[g * SUB : (g + 1) * SUB] for g in range(groups)])

    def step(member, sums):
        for tile in range(tiles):
            sx, sy, sz, size, turn = [
                jnp.broadcast_to(messages_ref[member, c * tiles + tile : c * tiles + tile + 1, :], (SUB, LANES))
                for c in range(5)
            ]
            new = []
            for g, (re, im) in enumerate(sums):
                dx = tests[0][g] - sx
                dy = tests[1][g] - sy
                dz = tests[2][g] - sz
                square = dx * dx + dy * dy + (dz * dz + soft)
                inverse = lax.rsqrt(square)
                t = square * inverse - turn
                u = t - ((t + ROUNDER) - ROUNDER)
                u2 = u * u
                s = u * horner(SINE, u2)
                c = horner(COSINE, u2)
                a = inverse * size
                p = a * s
                new.append(((re + a) - p * s, im + p * c))
            sums = tuple(new)
        return sums

    zero = jnp.zeros((SUB, LANES), jnp.float32)
    sums = lax.fori_loop(0, members, step, tuple((zero, zero) for _ in range(groups)), unroll=2)
    re, im = [
        jnp.concatenate([jnp.sum(pair[part], axis=1, keepdims=True) for pair in sums], axis=0) for part in range(2)
    ]
    both = jnp.where(lane == sub, re, jnp.where(lane == sub + row_dev, im, 0.0))
    both = jnp.sum(both, axis=0, keepdims=True)
    half = lax.axis_index("half")
    spot = 5 * tiles + (1 - half if other else half)
    base = lax.axis_index("row") * half_columns
    for k in range(half_columns):
        both = both + messages_ref[base + k, pl.ds(spot, 1), :]
    out_ref[0:1, :] = both[:, :row_dev]
    out_ref[1:2, :] = both[:, row_dev : 2 * row_dev]


def partner_kernel(half_columns, tests_ref, messages_ref, out_ref):
    far_sums(half_columns, True, tests_ref, messages_ref, out_ref)


def early_kernel(half_columns, tests_ref, messages_ref, sent_ref, out_ref, send_ref):
    send_ref[...] = sent_ref[...]

    @pl.when(lax.axis_index("half") == 0)
    def _():
        far_sums(half_columns, False, tests_ref, messages_ref, out_ref)

    @pl.when(lax.axis_index("half") != 0)
    def _():
        out_ref[...] = jnp.zeros_like(out_ref)


def late_kernel(half_columns, tests_ref, messages_ref, early_ref, out_ref):
    @pl.when(lax.axis_index("half") == 0)
    def _():
        out_ref[...] = early_ref[...]

    @pl.when(lax.axis_index("half") != 0)
    def _():
        far_sums(half_columns, False, tests_ref, messages_ref, out_ref)


def local(rows, half_columns, test_points, src_points, currents, near_blocks, near_dest, near_tile):
    row_dev = test_points.shape[1]
    width = src_points.shape[1]
    items = near_blocks.shape[0]
    members = rows * half_columns
    gain = TURNS / math.sqrt(width * members * 2)
    message = (5 * width // LANES + SUB, LANES)
    vmem = pl.BlockSpec(memory_space=pltpu.VMEM)
    hbm = pl.BlockSpec(memory_space=pltpu.HBM)
    params = pltpu.CompilerParams(vmem_limit_bytes=24 << 20)

    partner_points = lax.ppermute(test_points, "half", [(0, 1), (1, 0)])
    copies = pl.pallas_call(
        functools.partial(pack_kernel, half_columns, gain),
        out_shape=jax.ShapeDtypeStruct((members,) + message, jnp.float32),
        in_specs=[hbm] * 5,
        out_specs=vmem,
        scratch_shapes=[
            pltpu.SMEM((items,), jnp.int32),
            pltpu.SMEM((items,), jnp.int32),
            pltpu.VMEM((3, width), jnp.float32),
            pltpu.VMEM((2, width), jnp.float32),
            pltpu.VMEM(near_blocks.shape, jnp.float32),
            pltpu.VMEM(message, jnp.float32),
            pltpu.VMEM((2, 2 * half_columns, LANES), jnp.float32),
            pltpu.SemaphoreType.DMA((5,)),
        ],
        cost_estimate=pl.CostEstimate(flops=1 << 20, bytes_accessed=1 << 20, transcendentals=0),
    )(near_dest.reshape(-1), near_tile.reshape(-1), src_points, currents, near_blocks)
    messages = lax.all_to_all(copies, ("row", "column"), split_axis=0, concat_axis=0, tiled=True)

    evaluations = width * members * row_dev
    sums = jax.ShapeDtypeStruct((2, row_dev), jnp.float32)

    def far(body, outs, *operands):
        return pl.pallas_call(
            functools.partial(body, half_columns),
            out_shape=[sums] * outs,
            in_specs=[vmem] * len(operands),
            out_specs=[vmem] * outs,
            compiler_params=params,
            cost_estimate=pl.CostEstimate(flops=40 * evaluations, bytes_accessed=4 << 20, transcendentals=evaluations),
        )(*operands)

    (sent,) = far(partner_kernel, 1, partner_points, messages)
    to_first = lax.ppermute(sent, "half", [(1, 0)])
    early, send = far(early_kernel, 2, test_points, messages, sent)
    to_second = lax.ppermute(send, "half", [(0, 1)])
    (own,) = far(late_kernel, 1, test_points, messages, early)
    return own + to_first + to_second


def solution(mesh):
    rows, columns = mesh.shape["row"], mesh.shape["col"]
    finer = jax.sharding.Mesh(mesh.devices.reshape(rows, 2, columns // 2), ("row", "half", "column"))
    every = ("row", "half", "column")
    in_specs = (
        P(None, every),
        P(None, every),
        P(None, every),
        P(every, None, None, None),
        P(every, None),
        P(every, None),
    )
    body = functools.partial(local, rows, columns // 2)
    return jax.shard_map(body, mesh=finer, in_specs=in_specs, out_specs=P(None, every), check_vma=False)
```

```python
import functools
import math

import jax
import jax.numpy as jnp
import numpy as np
from jax import lax
from jax.experimental import pallas as pl
from jax.experimental.pallas import tpu as pltpu
from jax.sharding import PartitionSpec as P

WAVENUMBER = 40.0
SOFTENING = 0.01
TURNS = WAVENUMBER / (2.0 * math.pi)
LANES = 128
SUB = 8


def even_fit(function, terms, reach):
    nodes = np.cos((np.arange(400) + 0.5) * np.pi / 400)
    squares = (nodes + 1) * 0.5 * reach * reach
    fit = np.polynomial.chebyshev.Chebyshev.fit(squares, function(np.sqrt(squares)), terms - 1)
    return [float(value) for value in fit.convert(kind=np.polynomial.Polynomial).coef]


ROOT2 = math.sqrt(2.0)
SINE = even_fit(lambda u: ROOT2 * math.pi * np.sinc(u), 4, 0.5)
COSINE = even_fit(lambda u: -ROOT2 * np.cos(np.pi * u), 5, 0.5)
ROUNDER = 1.5 * 2.0**23


def horner(coefficients, x):
    total = coefficients[-1] * x + coefficients[-2]
    for value in coefficients[-3::-1]:
        total = total * x + value
    return total


def pack_kernel(gain, src_hbm, cur_hbm, copies_ref, src_ref, cur_ref, message, sems):
    moves = [
        pltpu.make_async_copy(source, target, sems.at[k])
        for k, (source, target) in enumerate(((src_hbm, src_ref), (cur_hbm, cur_ref)))
    ]
    for move in moves:
        move.start()
    for move in moves:
        move.wait()
    members = copies_ref.shape[0]
    tiles = src_ref.shape[1] // LANES
    for tile in range(tiles):
        part = pl.ds(tile * LANES, LANES)
        for c in range(2):
            message[(3 + c) * tiles + tile : (3 + c) * tiles + tile + 1, :] = cur_ref[c : c + 1, part]
        for c in range(3):
            message[c * tiles + tile : c * tiles + tile + 1, :] = src_ref[c : c + 1, part] * TURNS
    cr = message[3 * tiles : 4 * tiles, :]
    ci = message[4 * tiles : 5 * tiles, :]
    message[3 * tiles : 4 * tiles, :] = jnp.sqrt(cr * cr + ci * ci) * gain
    message[4 * tiles : 5 * tiles, :] = jnp.arctan2(ci, cr) * (0.5 / math.pi)

    def copy(member, _):
        copies_ref[member] = message[...]
        return 0

    lax.fori_loop(0, members, copy, 0, unroll=16)


def near_kernel(dest_hbm, tile_hbm, cur_hbm, blocks_hbm, after_ref, out_ref, dest_ref, tile_ref, cur_ref, blocks_ref, near_all, sems):
    moves = [
        pltpu.make_async_copy(source, target, sems.at[k])
        for k, (source, target) in enumerate((
            (dest_hbm, dest_ref), (tile_hbm, tile_ref), (cur_hbm, cur_ref), (blocks_hbm, blocks_ref)
        ))
    ]
    for move in moves:
        move.start()
    items, _, row_dev, _ = blocks_ref.shape
    per_row = LANES // row_dev
    columns = out_ref.shape[0]
    lane = lax.broadcasted_iota(jnp.int32, (SUB, LANES), 1)
    sub = lax.broadcasted_iota(jnp.int32, (SUB, LANES), 0)
    near_all[...] = jnp.zeros_like(near_all)
    for move in moves:
        move.wait()
    for group in range(items // per_row):
        owner = jnp.zeros((SUB, LANES), jnp.int32)
        sums = [jnp.zeros((SUB, LANES), jnp.float32)] * 2
        for k in range(per_row):
            block = group * per_row + k
            tile = pl.multiple_of(tile_ref[block] * LANES, LANES)
            cr = cur_ref[0:1, pl.ds(tile, LANES)]
            ci = cur_ref[1:2, pl.ds(tile, LANES)]
            br = blocks_ref[block, 0]
            bi = blocks_ref[block, 1]
            for part, product in enumerate((br * cr - bi * ci, br * ci + bi * cr)):
                total = jnp.sum(product, axis=1, keepdims=True)
                for piece in range(row_dev // SUB):
                    spot = lane == sub + (k * row_dev + piece * SUB)
                    sums[part] = jnp.where(spot, total[piece * SUB : (piece + 1) * SUB], sums[part])
            owner = jnp.where(lane >= k * row_dev, dest_ref[block], owner)
        terms = [jnp.sum(x, axis=0, keepdims=True) for x in sums]
        for block in range(columns // SUB):
            place = pl.ds(block * SUB, SUB)
            mine = owner == sub + block * SUB
            for part in range(2):
                near_all[part, place, :] += jnp.where(mine, terms[part], 0.0)
    for block in range(columns // SUB):
        place = pl.ds(block * SUB, SUB)
        re = near_all[0, place, :]
        im = near_all[1, place, :]
        shift = LANES // 2
        while shift >= row_dev:
            re = re + pltpu.roll(re, shift, 1)
            im = im + pltpu.roll(im, shift, 1)
            shift //= 2
        out_ref[place, 0, :] = re[:, :row_dev]
        out_ref[place, 1, :] = im[:, :row_dev]


def far_kernel(tests_ref, messages_ref, *refs):
    out_ref = refs[-1]
    members = messages_ref.shape[0]
    tiles = messages_ref.shape[1] // 5
    row_dev = tests_ref.shape[1]
    groups = row_dev // SUB
    lane = lax.broadcasted_iota(jnp.int32, (row_dev, LANES), 1)
    sub = lax.broadcasted_iota(jnp.int32, (row_dev, LANES), 0)
    soft = (SOFTENING * TURNS) ** 2

    points = jnp.concatenate([tests_ref[...], jnp.zeros((3, LANES - row_dev), jnp.float32)], axis=1) * TURNS
    tests = []
    for c in range(3):
        column = jnp.sum(jnp.where(lane == sub, points[c : c + 1, :], 0.0), axis=1, keepdims=True)
        wide = jnp.broadcast_to(column, (row_dev, LANES))
        tests.append([wide[g * SUB : (g + 1) * SUB] for g in range(groups)])

    def step(member, sums):
        for tile in range(tiles):
            sx, sy, sz, size, turn = [
                jnp.broadcast_to(messages_ref[member, c * tiles + tile : c * tiles + tile + 1, :], (SUB, LANES))
                for c in range(5)
            ]
            new = []
            for g, (re, im) in enumerate(sums):
                dx = tests[0][g] - sx
                dy = tests[1][g] - sy
                dz = tests[2][g] - sz
                square = dx * dx + dy * dy + (dz * dz + soft)
                inverse = lax.rsqrt(square)
                t = square * inverse - turn
                u = t - ((t + ROUNDER) - ROUNDER)
                u2 = u * u
                s = u * horner(SINE, u2)
                c = horner(COSINE, u2)
                a = inverse * size
                p = a * s
                new.append(((re + a) - p * s, im + p * c))
            sums = tuple(new)
        return sums

    zero = jnp.zeros((SUB, LANES), jnp.float32)
    sums = lax.fori_loop(0, members, step, tuple((zero, zero) for _ in range(groups)), unroll=2)
    re, im = [
        jnp.concatenate([jnp.sum(pair[part], axis=1, keepdims=True) for pair in sums], axis=0) for part in range(2)
    ]
    both = jnp.where(lane == sub, re, jnp.where(lane == sub + row_dev, im, 0.0))
    both = jnp.sum(both, axis=0, keepdims=True)
    out_ref[0:1, :] = both[:, :row_dev]
    out_ref[1:2, :] = both[:, row_dev : 2 * row_dev]
    for near_ref in refs[:-1]:
        out_ref[...] += jnp.sum(near_ref[...], axis=0)


def swap(x):
    return lax.ppermute(x, "half", [(0, 1), (1, 0)])


def local(rows, half_columns, test_points, src_points, currents, near_blocks, near_dest, near_tile):
    row_dev = test_points.shape[1]
    width = src_points.shape[1]
    items = near_blocks.shape[0]
    members = rows * half_columns
    gain = TURNS / math.sqrt(width * members * 2)
    message = (5 * width // LANES, LANES)
    vmem = pl.BlockSpec(memory_space=pltpu.VMEM)
    hbm = pl.BlockSpec(memory_space=pltpu.HBM)
    params = pltpu.CompilerParams(vmem_limit_bytes=24 << 20)

    partner_points = swap(test_points)
    copies = pl.pallas_call(
        functools.partial(pack_kernel, gain),
        out_shape=jax.ShapeDtypeStruct((members,) + message, jnp.float32),
        in_specs=[hbm] * 2,
        out_specs=vmem,
        scratch_shapes=[
            pltpu.VMEM((3, width), jnp.float32),
            pltpu.VMEM((2, width), jnp.float32),
            pltpu.VMEM(message, jnp.float32),
            pltpu.SemaphoreType.DMA((2,)),
        ],
        cost_estimate=pl.CostEstimate(flops=1 << 20, bytes_accessed=1 << 20, transcendentals=0),
    )(src_points, currents)
    messages = lax.all_to_all(copies, ("row", "column"), split_axis=0, concat_axis=0, tiled=True)

    near = pl.pallas_call(
        near_kernel,
        out_shape=jax.ShapeDtypeStruct((2 * half_columns, 2, row_dev), jnp.float32),
        in_specs=[hbm] * 5,
        out_specs=vmem,
        scratch_shapes=[
            pltpu.SMEM((items,), jnp.int32),
            pltpu.SMEM((items,), jnp.int32),
            pltpu.VMEM((2, width), jnp.float32),
            pltpu.VMEM(near_blocks.shape, jnp.float32),
            pltpu.VMEM((2, 2 * half_columns, LANES), jnp.float32),
            pltpu.SemaphoreType.DMA((4,)),
        ],
        cost_estimate=pl.CostEstimate(flops=1 << 20, bytes_accessed=1 << 20, transcendentals=0),
    )(near_dest.reshape(-1), near_tile.reshape(-1), currents, near_blocks, copies)
    near = lax.all_to_all(near, ("half", "column"), split_axis=0, concat_axis=0, tiled=True)

    def far(*operands):
        evaluations = width * members * row_dev
        return pl.pallas_call(
            far_kernel,
            out_shape=jax.ShapeDtypeStruct((2, row_dev), jnp.float32),
            in_specs=[vmem] * len(operands),
            out_specs=vmem,
            compiler_params=params,
            cost_estimate=pl.CostEstimate(flops=40 * evaluations, bytes_accessed=4 << 20, transcendentals=evaluations),
        )(*operands)

    from_partner = swap(far(partner_points, messages))
    return far(test_points, messages, near) + from_partner


def solution(mesh):
    rows, columns = mesh.shape["row"], mesh.shape["col"]
    finer = jax.sharding.Mesh(mesh.devices.reshape(rows, 2, columns // 2), ("row", "half", "column"))
    every = ("row", "half", "column")
    in_specs = (
        P(None, every),
        P(None, every),
        P(None, every),
        P(every, None, None, None),
        P(every, None),
        P(every, None),
    )
    body = functools.partial(local, rows, columns // 2)
    return jax.shard_map(body, mesh=finer, in_specs=in_specs, out_specs=P(None, every), check_vma=False)
```

```python
import functools
import math

import jax
import jax.numpy as jnp
import numpy as np
from jax import lax
from jax.experimental import pallas as pl
from jax.experimental.pallas import tpu as pltpu
from jax.sharding import PartitionSpec as P

WAVENUMBER = 40.0
SOFTENING = 0.01
TURNS = WAVENUMBER / (2.0 * math.pi)
LANES = 128
SUB = 8


def even_fit(function, terms, reach):
    nodes = np.cos((np.arange(400) + 0.5) * np.pi / 400)
    squares = (nodes + 1) * 0.5 * reach * reach
    fit = np.polynomial.chebyshev.Chebyshev.fit(squares, function(np.sqrt(squares)), terms - 1)
    return [float(value) for value in fit.convert(kind=np.polynomial.Polynomial).coef]


ROOT2 = math.sqrt(2.0)
SINE = even_fit(lambda u: ROOT2 * math.pi * np.sinc(u), 4, 0.5)
COSINE = even_fit(lambda u: -ROOT2 * np.cos(np.pi * u), 5, 0.5)
ROUNDER = 1.5 * 2.0**23


def horner(coefficients, x):
    total = coefficients[-1] * x + coefficients[-2]
    for value in coefficients[-3::-1]:
        total = total * x + value
    return total


def pack_kernel(
    half_columns, gain, dest_hbm, tile_hbm, src_hbm, cur_hbm, blocks_hbm, copies_ref,
    dest_ref, tile_ref, src_ref, cur_ref, blocks_ref, message, near_all, sems
):
    moves = [
        pltpu.make_async_copy(source, target, sems.at[k])
        for k, (source, target) in enumerate((
            (src_hbm, src_ref), (cur_hbm, cur_ref), (blocks_hbm, blocks_ref), (dest_hbm, dest_ref), (tile_hbm, tile_ref)
        ))
    ]
    for move in moves:
        move.start()
    members = copies_ref.shape[0]
    tiles = src_ref.shape[1] // LANES
    items, _, row_dev, _ = blocks_ref.shape
    per_row = LANES // row_dev
    columns = 2 * half_columns
    lane = lax.broadcasted_iota(jnp.int32, (SUB, LANES), 1)
    sub = lax.broadcasted_iota(jnp.int32, (SUB, LANES), 0)

    message[5 * tiles :, :] = jnp.zeros((message.shape[0] - 5 * tiles, LANES), jnp.float32)
    near_all[...] = jnp.zeros_like(near_all)
    for move in moves:
        move.wait()

    for group in range(items // per_row):
        owner = jnp.zeros((SUB, LANES), jnp.int32)
        sums = [jnp.zeros((SUB, LANES), jnp.float32)] * 2
        for k in range(per_row):
            block = group * per_row + k
            tile = pl.multiple_of(tile_ref[block] * LANES, LANES)
            cr = cur_ref[0:1, pl.ds(tile, LANES)]
            ci = cur_ref[1:2, pl.ds(tile, LANES)]
            br = blocks_ref[block, 0]
            bi = blocks_ref[block, 1]
            for part, product in enumerate((br * cr - bi * ci, br * ci + bi * cr)):
                total = jnp.sum(product, axis=1, keepdims=True)
                for piece in range(row_dev // SUB):
                    spot = lane == sub + (k * row_dev + piece * SUB)
                    sums[part] = jnp.where(spot, total[piece * SUB : (piece + 1) * SUB], sums[part])
            owner = jnp.where(lane >= k * row_dev, dest_ref[block], owner)
        terms = [jnp.sum(x, axis=0, keepdims=True) for x in sums]
        for block in range(columns // SUB):
            place = pl.ds(block * SUB, SUB)
            mine = owner == sub + block * SUB
            for part in range(2):
                near_all[part, place, :] += jnp.where(mine, terms[part], 0.0)
    for block in range(columns // SUB):
        place = pl.ds(block * SUB, SUB)
        re = near_all[0, place, :]
        im = near_all[1, place, :]
        shift = LANES // 2
        while shift >= row_dev:
            re = re + pltpu.roll(re, shift, 1)
            im = im + pltpu.roll(im, shift, 1)
            shift //= 2
        near_all[0, place, :] = jnp.where(lane < row_dev, re, jnp.where(lane < 2 * row_dev, im, 0.0))

    for tile in range(tiles):
        part = pl.ds(tile * LANES, LANES)
        for c in range(3):
            message[c * tiles + tile : c * tiles + tile + 1, :] = src_ref[c : c + 1, part] * TURNS
        for c in range(2):
            message[(3 + c) * tiles + tile : (3 + c) * tiles + tile + 1, :] = cur_ref[c : c + 1, part]
    cr = message[3 * tiles : 4 * tiles, :]
    ci = message[4 * tiles : 5 * tiles, :]
    message[3 * tiles : 4 * tiles, :] = jnp.sqrt(cr * cr + ci * ci) * gain
    message[4 * tiles : 5 * tiles, :] = jnp.arctan2(ci, cr) * (0.5 / math.pi)

    def copy(member, _):
        copies_ref[member] = message[...]
        return 0

    lax.fori_loop(0, members, copy, 0, unroll=16)

    base = lax.axis_index("x") * half_columns
    for k in range(half_columns):
        for half in range(2):
            spot = 5 * tiles + half
            copies_ref[base + k, spot : spot + 1, :] = near_all[0, half * half_columns + k : half * half_columns + k + 1, :]


def wide_points(tests_ref):
    row_dev = tests_ref.shape[1]
    lane = lax.broadcasted_iota(jnp.int32, (row_dev, LANES), 1)
    sub = lax.broadcasted_iota(jnp.int32, (row_dev, LANES), 0)
    points = jnp.concatenate([tests_ref[...], jnp.zeros((3, LANES - row_dev), jnp.float32)], axis=1) * TURNS
    columns = []
    for c in range(3):
        column = jnp.sum(jnp.where(lane == sub, points[c : c + 1, :], 0.0), axis=1, keepdims=True)
        columns.append(jnp.broadcast_to(column, (row_dev, LANES)))
    return [[column[g * SUB : (g + 1) * SUB] for column in columns] for g in range(row_dev // SUB)]


def far_loop(tests, sums, messages_ref):
    members = messages_ref.shape[0]
    tiles = (messages_ref.shape[1] - SUB) // 5
    soft = (SOFTENING * TURNS) ** 2

    def step(member, sums):
        for tile in range(tiles):
            sx, sy, sz, size, turn = [
                jnp.broadcast_to(messages_ref[member, c * tiles + tile : c * tiles + tile + 1, :], (SUB, LANES))
                for c in range(5)
            ]
            new = []
            for (tx, ty, tz), (re, im) in zip(tests, sums):
                dx = tx - sx
                dy = ty - sy
                dz = tz - sz
                square = dx * dx + dy * dy + (dz * dz + soft)
                inverse = lax.rsqrt(square)
                t = square * inverse - turn
                u = t - ((t + ROUNDER) - ROUNDER)
                u2 = u * u
                s = u * horner(SINE, u2)
                c = horner(COSINE, u2)
                a = inverse * size
                p = a * s
                new.append(((re + a) - p * s, im + p * c))
            sums = tuple(new)
        return sums

    return lax.fori_loop(0, members, step, tuple(sums), unroll=4 // len(tests))


def first_kernel(partner_ref, tests_ref, messages_ref, sums_ref):
    groups = tests_ref.shape[1] // SUB
    tests = wide_points(partner_ref) + wide_points(tests_ref)
    zero = jnp.zeros((SUB, LANES), jnp.float32)
    for k, pair in enumerate(far_loop(tests, [(zero, zero)] * len(tests), messages_ref)):
        for part in range(2):
            sums_ref[k // groups, part, pl.ds(k % groups * SUB, SUB), :] = pair[part]


def second_kernel(half_columns, other, tests_ref, sums_ref, messages_ref, sibling_ref, out_ref):
    row_dev = tests_ref.shape[1]
    tiles = (messages_ref.shape[1] - SUB) // 5
    lane = lax.broadcasted_iota(jnp.int32, (row_dev, LANES), 1)
    sub = lax.broadcasted_iota(jnp.int32, (row_dev, LANES), 0)
    tests = wide_points(tests_ref)
    which = 0 if other else 1
    sums = [
        (sums_ref[which, 0, pl.ds(g * SUB, SUB), :], sums_ref[which, 1, pl.ds(g * SUB, SUB), :]) for g in range(len(tests))
    ]
    sums = far_loop(tests, sums, sibling_ref)
    re, im = [
        jnp.concatenate([jnp.sum(pair[part], axis=1, keepdims=True) for pair in sums], axis=0) for part in range(2)
    ]
    both = jnp.where(lane == sub, re, jnp.where(lane == sub + row_dev, im, 0.0))
    both = jnp.sum(both, axis=0, keepdims=True)
    half = lax.axis_index("half")
    spot = 5 * tiles + (1 - half if other else half)
    base = lax.axis_index("x") * half_columns
    for k in range(half_columns):
        both = both + messages_ref[base + k, pl.ds(spot, 1), :]
    out_ref[0:1, :] = both[:, :row_dev]
    out_ref[1:2, :] = both[:, row_dev : 2 * row_dev]


def swap(x, axis):
    return lax.ppermute(x, axis, [(0, 1), (1, 0)])


def local(rows, half_columns, test_points, src_points, currents, near_blocks, near_dest, near_tile):
    row_dev = test_points.shape[1]
    width = src_points.shape[1]
    items = near_blocks.shape[0]
    members = rows // 2 * half_columns
    gain = TURNS / math.sqrt(width * members * 4)
    message = (5 * width // LANES + SUB, LANES)
    vmem = pl.BlockSpec(memory_space=pltpu.VMEM)
    hbm = pl.BlockSpec(memory_space=pltpu.HBM)
    params = pltpu.CompilerParams(vmem_limit_bytes=24 << 20)

    partner_points = swap(test_points, "half")
    copies = pl.pallas_call(
        functools.partial(pack_kernel, half_columns, gain),
        out_shape=jax.ShapeDtypeStruct((members,) + message, jnp.float32),
        in_specs=[hbm] * 5,
        out_specs=vmem,
        scratch_shapes=[
            pltpu.SMEM((items,), jnp.int32),
            pltpu.SMEM((items,), jnp.int32),
            pltpu.VMEM((3, width), jnp.float32),
            pltpu.VMEM((2, width), jnp.float32),
            pltpu.VMEM(near_blocks.shape, jnp.float32),
            pltpu.VMEM(message, jnp.float32),
            pltpu.VMEM((2, 2 * half_columns, LANES), jnp.float32),
            pltpu.SemaphoreType.DMA((5,)),
        ],
        cost_estimate=pl.CostEstimate(flops=1 << 20, bytes_accessed=1 << 20, transcendentals=0),
    )(near_dest.reshape(-1), near_tile.reshape(-1), src_points, currents, near_blocks)
    messages = lax.all_to_all(copies, ("x", "column"), split_axis=0, concat_axis=0, tiled=True)

    sibling = swap(messages, "core")

    evaluations = width * members * row_dev

    def cost(times):
        return dict(
            compiler_params=params,
            cost_estimate=pl.CostEstimate(
                flops=40 * evaluations * times, bytes_accessed=2 << 20, transcendentals=evaluations * times
            ),
        )

    sums = pl.pallas_call(
        first_kernel,
        out_shape=jax.ShapeDtypeStruct((2, 2, row_dev, LANES), jnp.float32),
        in_specs=[vmem] * 3,
        out_specs=vmem,
        **cost(2),
    )(partner_points, test_points, messages)

    def second(points, other):
        return pl.pallas_call(
            functools.partial(second_kernel, half_columns, other),
            out_shape=jax.ShapeDtypeStruct((2, row_dev), jnp.float32),
            in_specs=[vmem] * 4,
            out_specs=vmem,
            **cost(1),
        )(points, sums, messages, sibling)

    from_partner = swap(second(partner_points, True), "half")
    return second(test_points, False) + from_partner


def solution(mesh):
    rows, columns = mesh.shape["row"], mesh.shape["col"]
    finer = jax.sharding.Mesh(mesh.devices.reshape(rows // 2, 2, 2, columns // 2), ("x", "core", "half", "column"))
    every = ("x", "core", "half", "column")
    in_specs = (
        P(None, every),
        P(None, every),
        P(None, every),
        P(every, None, None, None),
        P(every, None),
        P(every, None),
    )
    body = functools.partial(local, rows, columns // 2)
    return jax.shard_map(body, mesh=finer, in_specs=in_specs, out_specs=P(None, every), check_vma=False)
```

```python
import functools
import math

import jax
import jax.numpy as jnp
import numpy as np
from jax import lax
from jax.experimental import pallas as pl
from jax.experimental.pallas import tpu as pltpu
from jax.sharding import PartitionSpec as P

WAVENUMBER = 40.0
SOFTENING = 0.01
TURNS = WAVENUMBER / (2.0 * math.pi)
LANES = 128
SUB = 8


def even_fit(function, terms, reach):
    nodes = np.cos((np.arange(400) + 0.5) * np.pi / 400)
    squares = (nodes + 1) * 0.5 * reach * reach
    fit = np.polynomial.chebyshev.Chebyshev.fit(squares, function(np.sqrt(squares)), terms - 1)
    return [float(value) for value in fit.convert(kind=np.polynomial.Polynomial).coef]


ROOT2 = math.sqrt(2.0)
SINE = even_fit(lambda u: ROOT2 * math.pi * np.sinc(u), 4, 0.5)
COSINE = even_fit(lambda u: -ROOT2 * np.cos(np.pi * u), 5, 0.5)
ROUNDER = 1.5 * 2.0**23


def horner(coefficients, x):
    total = coefficients[-1] * x + coefficients[-2]
    for value in coefficients[-3::-1]:
        total = total * x + value
    return total


def pack_kernel(
    half_columns, gain, dest_hbm, tile_hbm, src_hbm, cur_hbm, blocks_hbm, copies_ref,
    dest_ref, tile_ref, src_ref, cur_ref, blocks_ref, message, near_all, sems
):
    moves = [
        pltpu.make_async_copy(source, target, sems.at[k])
        for k, (source, target) in enumerate((
            (src_hbm, src_ref), (cur_hbm, cur_ref), (blocks_hbm, blocks_ref), (dest_hbm, dest_ref), (tile_hbm, tile_ref)
        ))
    ]
    for move in moves:
        move.start()
    members = copies_ref.shape[0]
    tiles = src_ref.shape[1] // LANES
    items, _, row_dev, _ = blocks_ref.shape
    per_row = LANES // row_dev
    columns = 2 * half_columns
    lane = lax.broadcasted_iota(jnp.int32, (SUB, LANES), 1)
    sub = lax.broadcasted_iota(jnp.int32, (SUB, LANES), 0)

    message[5 * tiles :, :] = jnp.zeros((message.shape[0] - 5 * tiles, LANES), jnp.float32)
    near_all[...] = jnp.zeros_like(near_all)
    for move in moves:
        move.wait()

    for group in range(items // per_row):
        owner = jnp.zeros((SUB, LANES), jnp.int32)
        sums = [jnp.zeros((SUB, LANES), jnp.float32)] * 2
        for k in range(per_row):
            block = group * per_row + k
            tile = pl.multiple_of(tile_ref[block] * LANES, LANES)
            cr = cur_ref[0:1, pl.ds(tile, LANES)]
            ci = cur_ref[1:2, pl.ds(tile, LANES)]
            br = blocks_ref[block, 0]
            bi = blocks_ref[block, 1]
            for part, product in enumerate((br * cr - bi * ci, br * ci + bi * cr)):
                total = jnp.sum(product, axis=1, keepdims=True)
                for piece in range(row_dev // SUB):
                    spot = lane == sub + (k * row_dev + piece * SUB)
                    sums[part] = jnp.where(spot, total[piece * SUB : (piece + 1) * SUB], sums[part])
            owner = jnp.where(lane >= k * row_dev, dest_ref[block], owner)
        terms = [jnp.sum(x, axis=0, keepdims=True) for x in sums]
        for block in range(columns // SUB):
            place = pl.ds(block * SUB, SUB)
            mine = owner == sub + block * SUB
            for part in range(2):
                near_all[part, place, :] += jnp.where(mine, terms[part], 0.0)
    for block in range(columns // SUB):
        place = pl.ds(block * SUB, SUB)
        re = near_all[0, place, :]
        im = near_all[1, place, :]
        shift = LANES // 2
        while shift >= row_dev:
            re = re + pltpu.roll(re, shift, 1)
            im = im + pltpu.roll(im, shift, 1)
            shift //= 2
        near_all[0, place, :] = jnp.where(lane < row_dev, re, jnp.where(lane < 2 * row_dev, im, 0.0))

    for tile in range(tiles):
        part = pl.ds(tile * LANES, LANES)
        for c in range(3):
            message[c * tiles + tile : c * tiles + tile + 1, :] = src_ref[c : c + 1, part] * TURNS
        for c in range(2):
            message[(3 + c) * tiles + tile : (3 + c) * tiles + tile + 1, :] = cur_ref[c : c + 1, part]
    cr = message[3 * tiles : 4 * tiles, :]
    ci = message[4 * tiles : 5 * tiles, :]
    message[3 * tiles : 4 * tiles, :] = jnp.sqrt(cr * cr + ci * ci) * gain
    message[4 * tiles : 5 * tiles, :] = jnp.arctan2(ci, cr) * (0.5 / math.pi)

    def copy(member, _):
        copies_ref[member] = message[...]
        return 0

    lax.fori_loop(0, members, copy, 0, unroll=16)

    base = lax.axis_index("x") * half_columns
    for k in range(half_columns):
        for half in range(2):
            spot = 5 * tiles + half
            copies_ref[base + k, spot : spot + 1, :] = near_all[0, half * half_columns + k : half * half_columns + k + 1, :]


def points_kernel(partner_ref, tests_ref, wide_ref):
    row_dev = tests_ref.shape[1]
    lane = lax.broadcasted_iota(jnp.int32, (row_dev, LANES), 1)
    sub = lax.broadcasted_iota(jnp.int32, (row_dev, LANES), 0)
    for which, ref in enumerate((partner_ref, tests_ref)):
        points = jnp.concatenate([ref[...], jnp.zeros((3, LANES - row_dev), jnp.float32)], axis=1) * TURNS
        for c in range(3):
            column = jnp.sum(jnp.where(lane == sub, points[c : c + 1, :], 0.0), axis=1, keepdims=True)
            wide_ref[which, c] = jnp.broadcast_to(column, (row_dev, LANES))


def groups_of(wide_ref, which):
    return [[wide_ref[which, c, pl.ds(g * SUB, SUB), :] for c in range(3)] for g in range(wide_ref.shape[2] // SUB)]


def far_loop(tests, sums, messages_ref):
    members = messages_ref.shape[0]
    tiles = (messages_ref.shape[1] - SUB) // 5
    soft = (SOFTENING * TURNS) ** 2

    def step(member, sums):
        for tile in range(tiles):
            sx, sy, sz, size, turn = [
                jnp.broadcast_to(messages_ref[member, c * tiles + tile : c * tiles + tile + 1, :], (SUB, LANES))
                for c in range(5)
            ]
            new = []
            for (tx, ty, tz), (re, im) in zip(tests, sums):
                dx = tx - sx
                dy = ty - sy
                dz = tz - sz
                square = dx * dx + dy * dy + (dz * dz + soft)
                inverse = lax.rsqrt(square)
                t = square * inverse - turn
                u = t - ((t + ROUNDER) - ROUNDER)
                u2 = u * u
                s = u * horner(SINE, u2)
                c = horner(COSINE, u2)
                a = inverse * size
                p = a * s
                new.append(((re + a) - p * s, im + p * c))
            sums = tuple(new)
        return sums

    return lax.fori_loop(0, members, step, tuple(sums), unroll=4 // len(tests))


def first_kernel(wide_ref, messages_ref, sums_ref):
    groups = wide_ref.shape[2] // SUB
    tests = groups_of(wide_ref, 0) + groups_of(wide_ref, 1)
    zero = jnp.zeros((SUB, LANES), jnp.float32)
    for k, pair in enumerate(far_loop(tests, [(zero, zero)] * len(tests), messages_ref)):
        for part in range(2):
            sums_ref[k // groups, part, pl.ds(k % groups * SUB, SUB), :] = pair[part]


def second_kernel(half_columns, other, wide_ref, sums_ref, messages_ref, sibling_ref, out_ref):
    row_dev = wide_ref.shape[2]
    tiles = (messages_ref.shape[1] - SUB) // 5
    lane = lax.broadcasted_iota(jnp.int32, (row_dev, LANES), 1)
    sub = lax.broadcasted_iota(jnp.int32, (row_dev, LANES), 0)
    which = 0 if other else 1
    tests = groups_of(wide_ref, which)
    sums = [
        (sums_ref[which, 0, pl.ds(g * SUB, SUB), :], sums_ref[which, 1, pl.ds(g * SUB, SUB), :]) for g in range(len(tests))
    ]
    sums = far_loop(tests, sums, sibling_ref)
    re, im = [
        jnp.concatenate([jnp.sum(pair[part], axis=1, keepdims=True) for pair in sums], axis=0) for part in range(2)
    ]
    both = jnp.where(lane == sub, re, jnp.where(lane == sub + row_dev, im, 0.0))
    both = jnp.sum(both, axis=0, keepdims=True)
    half = lax.axis_index("half")
    spot = 5 * tiles + (1 - half if other else half)
    base = lax.axis_index("x") * half_columns
    for k in range(half_columns):
        both = both + messages_ref[base + k, pl.ds(spot, 1), :]
    out_ref[0:1, :] = both[:, :row_dev]
    out_ref[1:2, :] = both[:, row_dev : 2 * row_dev]


def swap(x, axis):
    return lax.ppermute(x, axis, [(0, 1), (1, 0)])


def local(rows, half_columns, test_points, src_points, currents, near_blocks, near_dest, near_tile):
    row_dev = test_points.shape[1]
    width = src_points.shape[1]
    items = near_blocks.shape[0]
    members = rows // 2 * half_columns
    gain = TURNS / math.sqrt(width * members * 4)
    message = (5 * width // LANES + SUB, LANES)
    vmem = pl.BlockSpec(memory_space=pltpu.VMEM)
    hbm = pl.BlockSpec(memory_space=pltpu.HBM)
    params = pltpu.CompilerParams(vmem_limit_bytes=24 << 20)

    partner_points = swap(test_points, "half")
    copies = pl.pallas_call(
        functools.partial(pack_kernel, half_columns, gain),
        out_shape=jax.ShapeDtypeStruct((members,) + message, jnp.float32),
        in_specs=[hbm] * 5,
        out_specs=vmem,
        scratch_shapes=[
            pltpu.SMEM((items,), jnp.int32),
            pltpu.SMEM((items,), jnp.int32),
            pltpu.VMEM((3, width), jnp.float32),
            pltpu.VMEM((2, width), jnp.float32),
            pltpu.VMEM(near_blocks.shape, jnp.float32),
            pltpu.VMEM(message, jnp.float32),
            pltpu.VMEM((2, 2 * half_columns, LANES), jnp.float32),
            pltpu.SemaphoreType.DMA((5,)),
        ],
        cost_estimate=pl.CostEstimate(flops=1 << 20, bytes_accessed=1 << 20, transcendentals=0),
    )(near_dest.reshape(-1), near_tile.reshape(-1), src_points, currents, near_blocks)
    messages = lax.all_to_all(copies, ("x", "column"), split_axis=0, concat_axis=0, tiled=True)

    sibling = swap(messages, "core")

    evaluations = width * members * row_dev

    def cost(times):
        return dict(
            compiler_params=params,
            cost_estimate=pl.CostEstimate(
                flops=40 * evaluations * times, bytes_accessed=2 << 20, transcendentals=evaluations * times
            ),
        )

    wide = pl.pallas_call(
        points_kernel,
        out_shape=jax.ShapeDtypeStruct((2, 3, row_dev, LANES), jnp.float32),
        in_specs=[vmem] * 2,
        out_specs=vmem,
        **cost(1),
    )(partner_points, test_points)

    sums = pl.pallas_call(
        first_kernel,
        out_shape=jax.ShapeDtypeStruct((2, 2, row_dev, LANES), jnp.float32),
        in_specs=[vmem] * 2,
        out_specs=vmem,
        **cost(2),
    )(wide, messages)

    def second(other):
        return pl.pallas_call(
            functools.partial(second_kernel, half_columns, other),
            out_shape=jax.ShapeDtypeStruct((2, row_dev), jnp.float32),
            in_specs=[vmem] * 4,
            out_specs=vmem,
            **cost(1),
        )(wide, sums, messages, sibling)

    from_partner = swap(second(True), "half")
    return second(False) + from_partner


def solution(mesh):
    rows, columns = mesh.shape["row"], mesh.shape["col"]
    finer = jax.sharding.Mesh(mesh.devices.reshape(rows // 2, 2, 2, columns // 2), ("x", "core", "half", "column"))
    every = ("x", "core", "half", "column")
    in_specs = (
        P(None, every),
        P(None, every),
        P(None, every),
        P(every, None, None, None),
        P(every, None),
        P(every, None),
    )
    body = functools.partial(local, rows, columns // 2)
    return jax.shard_map(body, mesh=finer, in_specs=in_specs, out_specs=P(None, every), check_vma=False)
```

```python
import functools
import math

import jax
import jax.numpy as jnp
import numpy as np
from jax import lax
from jax.experimental import pallas as pl
from jax.experimental.pallas import tpu as pltpu
from jax.sharding import PartitionSpec as P

WAVENUMBER = 40.0
SOFTENING = 0.01
TURNS = WAVENUMBER / (2.0 * math.pi)
LANES = 128
SUB = 8


def even_fit(function, terms, reach):
    nodes = np.cos((np.arange(400) + 0.5) * np.pi / 400)
    squares = (nodes + 1) * 0.5 * reach * reach
    fit = np.polynomial.chebyshev.Chebyshev.fit(squares, function(np.sqrt(squares)), terms - 1)
    return [float(value) for value in fit.convert(kind=np.polynomial.Polynomial).coef]


ROOT2 = math.sqrt(2.0)
SINE = even_fit(lambda u: ROOT2 * math.pi * np.sinc(u), 4, 0.5)
COSINE = even_fit(lambda u: -ROOT2 * np.cos(np.pi * u), 5, 0.5)
ROUNDER = 1.5 * 2.0**23


def horner(coefficients, x):
    total = coefficients[-1] * x + coefficients[-2]
    for value in coefficients[-3::-1]:
        total = total * x + value
    return total


def pack_kernel(
    half_columns, gain, dest_hbm, tile_hbm, src_hbm, cur_hbm, blocks_hbm, copies_ref,
    dest_ref, tile_ref, src_ref, cur_ref, blocks_ref, message, near_all, sems
):
    moves = [
        pltpu.make_async_copy(source, target, sems.at[k])
        for k, (source, target) in enumerate((
            (src_hbm, src_ref), (cur_hbm, cur_ref), (blocks_hbm, blocks_ref), (dest_hbm, dest_ref), (tile_hbm, tile_ref)
        ))
    ]
    for move in moves:
        move.start()
    members = copies_ref.shape[0]
    tiles = src_ref.shape[1] // LANES
    items, _, row_dev, _ = blocks_ref.shape
    per_row = LANES // row_dev
    columns = 2 * half_columns
    lane = lax.broadcasted_iota(jnp.int32, (SUB, LANES), 1)
    sub = lax.broadcasted_iota(jnp.int32, (SUB, LANES), 0)

    message[5 * tiles :, :] = jnp.zeros((message.shape[0] - 5 * tiles, LANES), jnp.float32)
    near_all[...] = jnp.zeros_like(near_all)
    for move in moves:
        move.wait()

    for group in range(items // per_row):
        owner = jnp.zeros((SUB, LANES), jnp.int32)
        sums = [jnp.zeros((SUB, LANES), jnp.float32)] * 2
        for k in range(per_row):
            block = group * per_row + k
            tile = pl.multiple_of(tile_ref[block] * LANES, LANES)
            cr = cur_ref[0:1, pl.ds(tile, LANES)]
            ci = cur_ref[1:2, pl.ds(tile, LANES)]
            br = blocks_ref[block, 0]
            bi = blocks_ref[block, 1]
            for part, product in enumerate((br * cr - bi * ci, br * ci + bi * cr)):
                total = jnp.sum(product, axis=1, keepdims=True)
                for piece in range(row_dev // SUB):
                    spot = lane == sub + (k * row_dev + piece * SUB)
                    sums[part] = jnp.where(spot, total[piece * SUB : (piece + 1) * SUB], sums[part])
            owner = jnp.where(lane >= k * row_dev, dest_ref[block], owner)
        terms = [jnp.sum(x, axis=0, keepdims=True) for x in sums]
        for block in range(columns // SUB):
            place = pl.ds(block * SUB, SUB)
            mine = owner == sub + block * SUB
            for part in range(2):
                near_all[part, place, :] += jnp.where(mine, terms[part], 0.0)
    for block in range(columns // SUB):
        place = pl.ds(block * SUB, SUB)
        re = near_all[0, place, :]
        im = near_all[1, place, :]
        shift = LANES // 2
        while shift >= row_dev:
            re = re + pltpu.roll(re, shift, 1)
            im = im + pltpu.roll(im, shift, 1)
            shift //= 2
        near_all[0, place, :] = jnp.where(lane < row_dev, re, jnp.where(lane < 2 * row_dev, im, 0.0))

    for tile in range(tiles):
        part = pl.ds(tile * LANES, LANES)
        for c in range(3):
            message[c * tiles + tile : c * tiles + tile + 1, :] = src_ref[c : c + 1, part] * TURNS
        for c in range(2):
            message[(3 + c) * tiles + tile : (3 + c) * tiles + tile + 1, :] = cur_ref[c : c + 1, part]
    cr = message[3 * tiles : 4 * tiles, :]
    ci = message[4 * tiles : 5 * tiles, :]
    message[3 * tiles : 4 * tiles, :] = jnp.sqrt(cr * cr + ci * ci) * gain
    message[4 * tiles : 5 * tiles, :] = jnp.arctan2(ci, cr) * (0.5 / math.pi)

    def copy(member, _):
        copies_ref[member] = message[...]
        return 0

    lax.fori_loop(0, members, copy, 0, unroll=16)

    base = lax.axis_index("x") * half_columns
    for k in range(half_columns):
        for half in range(2):
            spot = 5 * tiles + half
            copies_ref[base + k, spot : spot + 1, :] = near_all[0, half * half_columns + k : half * half_columns + k + 1, :]


def points_kernel(partner_ref, tests_ref, wide_ref):
    row_dev = tests_ref.shape[1]
    lane = lax.broadcasted_iota(jnp.int32, (row_dev, LANES), 1)
    sub = lax.broadcasted_iota(jnp.int32, (row_dev, LANES), 0)
    for which, ref in enumerate((partner_ref, tests_ref)):
        points = jnp.concatenate([ref[...], jnp.zeros((3, LANES - row_dev), jnp.float32)], axis=1) * TURNS
        for c in range(3):
            column = jnp.sum(jnp.where(lane == sub, points[c : c + 1, :], 0.0), axis=1, keepdims=True)
            wide_ref[which, c] = jnp.broadcast_to(column, (row_dev, LANES))


def groups_of(wide_ref, which):
    return [[wide_ref[which, c, pl.ds(g * SUB, SUB), :] for c in range(3)] for g in range(wide_ref.shape[2] // SUB)]


def far_loop(tests, sums, messages_ref):
    members = messages_ref.shape[0]
    tiles = (messages_ref.shape[1] - SUB) // 5
    soft = (SOFTENING * TURNS) ** 2

    def step(member, sums):
        for tile in range(tiles):
            sx, sy, sz, size, turn = [
                jnp.broadcast_to(messages_ref[member, c * tiles + tile : c * tiles + tile + 1, :], (SUB, LANES))
                for c in range(5)
            ]
            new = []
            for (tx, ty, tz), (re, im) in zip(tests, sums):
                dx = tx - sx
                dy = ty - sy
                dz = tz - sz
                square = dx * dx + dy * dy + (dz * dz + soft)
                inverse = lax.rsqrt(square)
                t = square * inverse - turn
                u = t - ((t + ROUNDER) - ROUNDER)
                u2 = u * u
                s = u * horner(SINE, u2)
                c = horner(COSINE, u2)
                a = inverse * size
                p = a * s
                new.append(((re + a) - p * s, im + p * c))
            sums = tuple(new)
        return sums

    return lax.fori_loop(0, members, step, tuple(sums), unroll=4 // len(tests))


def first_kernel(wide_ref, messages_ref, sums_ref):
    groups = wide_ref.shape[2] // SUB
    tests = groups_of(wide_ref, 0) + groups_of(wide_ref, 1)
    zero = jnp.zeros((SUB, LANES), jnp.float32)
    for k, pair in enumerate(far_loop(tests, [(zero, zero)] * len(tests), messages_ref)):
        for part in range(2):
            sums_ref[k // groups, part, pl.ds(k % groups * SUB, SUB), :] = pair[part]


def second_kernel(half_columns, other, wide_ref, sums_ref, messages_ref, sibling_ref, out_ref):
    row_dev = wide_ref.shape[2]
    tiles = (messages_ref.shape[1] - SUB) // 5
    lane = lax.broadcasted_iota(jnp.int32, (row_dev, LANES), 1)
    sub = lax.broadcasted_iota(jnp.int32, (row_dev, LANES), 0)
    which = 0 if other else 1
    tests = groups_of(wide_ref, which)
    sums = [
        (sums_ref[which, 0, pl.ds(g * SUB, SUB), :], sums_ref[which, 1, pl.ds(g * SUB, SUB), :]) for g in range(len(tests))
    ]
    sums = far_loop(tests, sums, sibling_ref)
    re, im = [
        jnp.concatenate([jnp.sum(pair[part], axis=1, keepdims=True) for pair in sums], axis=0) for part in range(2)
    ]
    both = jnp.where(lane == sub, re, jnp.where(lane == sub + row_dev, im, 0.0))
    both = jnp.sum(both, axis=0, keepdims=True)
    half = lax.axis_index("half")
    spot = 5 * tiles + (1 - half if other else half)
    base = lax.axis_index("x") * half_columns
    for k in range(half_columns):
        both = both + messages_ref[base + k, pl.ds(spot, 1), :]
    out_ref[0:1, :] = both[:, :row_dev]
    out_ref[1:2, :] = both[:, row_dev : 2 * row_dev]


def swap(x, axis):
    return lax.ppermute(x, axis, [(0, 1), (1, 0)])


def local(rows, half_columns, test_points, src_points, currents, near_blocks, near_dest, near_tile):
    row_dev = test_points.shape[1]
    width = src_points.shape[1]
    items = near_blocks.shape[0]
    members = rows // 2 * half_columns
    gain = TURNS / math.sqrt(width * members * 4)
    message = (5 * width // LANES + SUB, LANES)
    vmem = pl.BlockSpec(memory_space=pltpu.VMEM)
    hbm = pl.BlockSpec(memory_space=pltpu.HBM)
    params = pltpu.CompilerParams(vmem_limit_bytes=24 << 20)

    partner_points = swap(test_points, "half")
    copies = pl.pallas_call(
        functools.partial(pack_kernel, half_columns, gain),
        out_shape=jax.ShapeDtypeStruct((members,) + message, jnp.float32),
        in_specs=[hbm] * 5,
        out_specs=vmem,
        scratch_shapes=[
            pltpu.SMEM((items,), jnp.int32),
            pltpu.SMEM((items,), jnp.int32),
            pltpu.VMEM((3, width), jnp.float32),
            pltpu.VMEM((2, width), jnp.float32),
            pltpu.VMEM(near_blocks.shape, jnp.float32),
            pltpu.VMEM(message, jnp.float32),
            pltpu.VMEM((2, 2 * half_columns, LANES), jnp.float32),
            pltpu.SemaphoreType.DMA((5,)),
        ],
        cost_estimate=pl.CostEstimate(flops=1 << 20, bytes_accessed=1 << 20, transcendentals=0),
    )(near_dest.reshape(-1), near_tile.reshape(-1), src_points, currents, near_blocks)
    messages = lax.all_to_all(copies, ("x", "column"), split_axis=0, concat_axis=0, tiled=True)


    evaluations = width * members * row_dev

    def cost(times):
        return dict(
            compiler_params=params,
            cost_estimate=pl.CostEstimate(
                flops=40 * evaluations * times, bytes_accessed=2 << 20, transcendentals=evaluations * times
            ),
        )

    wide = pl.pallas_call(
        points_kernel,
        out_shape=jax.ShapeDtypeStruct((2, 3, row_dev, LANES), jnp.float32),
        in_specs=[vmem] * 2,
        out_specs=vmem,
        **cost(1),
    )(partner_points, test_points)

    messages, wide = lax.optimization_barrier((messages, wide))
    sibling = swap(messages, "core")
    sums = pl.pallas_call(
        first_kernel,
        out_shape=jax.ShapeDtypeStruct((2, 2, row_dev, LANES), jnp.float32),
        in_specs=[vmem] * 2,
        out_specs=vmem,
        **cost(2),
    )(wide, messages)

    def second(other):
        return pl.pallas_call(
            functools.partial(second_kernel, half_columns, other),
            out_shape=jax.ShapeDtypeStruct((2, row_dev), jnp.float32),
            in_specs=[vmem] * 4,
            out_specs=vmem,
            **cost(1),
        )(wide, sums, messages, sibling)

    from_partner = swap(second(True), "half")
    return second(False) + from_partner


def solution(mesh):
    rows, columns = mesh.shape["row"], mesh.shape["col"]
    finer = jax.sharding.Mesh(mesh.devices.reshape(rows // 2, 2, 2, columns // 2), ("x", "core", "half", "column"))
    every = ("x", "core", "half", "column")
    in_specs = (
        P(None, every),
        P(None, every),
        P(None, every),
        P(every, None, None, None),
        P(every, None),
        P(every, None),
    )
    body = functools.partial(local, rows, columns // 2)
    return jax.shard_map(body, mesh=finer, in_specs=in_specs, out_specs=P(None, every), check_vma=False)
```

```python
import functools
import math

import jax
import jax.numpy as jnp
import numpy as np
from jax import lax
from jax.experimental import pallas as pl
from jax.experimental.pallas import tpu as pltpu
from jax.sharding import PartitionSpec as P

WAVENUMBER = 40.0
SOFTENING = 0.01
TURNS = WAVENUMBER / (2.0 * math.pi)
LANES = 128
SUB = 8


def even_fit(function, terms, reach):
    nodes = np.cos((np.arange(400) + 0.5) * np.pi / 400)
    squares = (nodes + 1) * 0.5 * reach * reach
    fit = np.polynomial.chebyshev.Chebyshev.fit(squares, function(np.sqrt(squares)), terms - 1)
    return [float(value) for value in fit.convert(kind=np.polynomial.Polynomial).coef]


ROOT2 = math.sqrt(2.0)
SINE = even_fit(lambda u: ROOT2 * math.pi * np.sinc(u), 4, 0.5)
COSINE = even_fit(lambda u: -ROOT2 * np.cos(np.pi * u), 5, 0.5)
ANGLE = even_fit(lambda r: np.arctan(r) / (2 * np.pi * r), 9, 1.0)
ROUNDER = 1.5 * 2.0**23


def horner(coefficients, x):
    total = coefficients[-1] * x + coefficients[-2]
    for value in coefficients[-3::-1]:
        total = total * x + value
    return total


def phase_of(re, im):
    wide = jnp.abs(re)
    high = jnp.abs(im)
    larger = jnp.maximum(wide, high)
    ratio = jnp.minimum(wide, high) / jnp.where(larger == 0.0, 1.0, larger)
    turn = ratio * horner(ANGLE, ratio * ratio)
    turn = jnp.where(high > wide, 0.25 - turn, turn)
    turn = jnp.where(re < 0.0, 0.5 - turn, turn)
    return jnp.where(im < 0.0, -turn, turn)


def pack_kernel(
    half_columns, gain, dest_hbm, tile_hbm, src_hbm, cur_hbm, blocks_hbm, copies_ref,
    dest_ref, tile_ref, src_ref, cur_ref, blocks_ref, message, near_all, sems
):
    moves = [
        pltpu.make_async_copy(source, target, sems.at[k])
        for k, (source, target) in enumerate((
            (src_hbm, src_ref), (cur_hbm, cur_ref), (blocks_hbm, blocks_ref), (dest_hbm, dest_ref), (tile_hbm, tile_ref)
        ))
    ]
    for move in moves:
        move.start()
    members = copies_ref.shape[0]
    tiles = src_ref.shape[1] // LANES
    items, _, row_dev, _ = blocks_ref.shape
    columns = 2 * half_columns
    lane = lax.broadcasted_iota(jnp.int32, (SUB, LANES), 1)
    sub = lax.broadcasted_iota(jnp.int32, (SUB, LANES), 0)
    for move in moves:
        move.wait()

    for tile in range(tiles):
        part = pl.ds(tile * LANES, LANES)
        message[pl.ds(3 * tiles + tile, 2, stride=tiles), :] = cur_ref[:, part]
        message[pl.ds(tile, 3, stride=tiles), :] = src_ref[:, part]
    cr = message[3 * tiles : 4 * tiles, :]
    ci = message[4 * tiles : 5 * tiles, :]
    places = message[: 3 * tiles, :] * TURNS
    size = jnp.sqrt(cr * cr + ci * ci) * gain
    turn = phase_of(cr, ci)

    near = [jnp.zeros((SUB, LANES), jnp.float32)] * (columns // SUB)
    for block in range(items):
        tile = pl.multiple_of(tile_ref[block] * LANES, LANES)
        cr = cur_ref[0:1, pl.ds(tile, LANES)]
        ci = cur_ref[1:2, pl.ds(tile, LANES)]
        br = blocks_ref[block, 0]
        bi = blocks_ref[block, 1]
        row = jnp.zeros((SUB, LANES), jnp.float32)
        for part, product in enumerate((br * cr - bi * ci, br * ci + bi * cr)):
            total = jnp.sum(product, axis=1, keepdims=True)
            for piece in range(row_dev // SUB):
                spot = lane == sub + (part * row_dev + piece * SUB)
                row = jnp.where(spot, total[piece * SUB : (piece + 1) * SUB], row)
        row = jnp.sum(row, axis=0, keepdims=True)
        for group in range(columns // SUB):
            near[group] = near[group] + jnp.where(sub + group * SUB == dest_ref[block], row, 0.0)
    for group in range(columns // SUB):
        near_all[pl.ds(group * SUB, SUB), :] = near[group]

    def copy(member, _):
        copies_ref[member, : 3 * tiles, :] = places
        copies_ref[member, 3 * tiles : 4 * tiles, :] = size
        copies_ref[member, 4 * tiles : 5 * tiles, :] = turn
        copies_ref[member, 5 * tiles :, :] = jnp.zeros((SUB, LANES), jnp.float32)
        return 0

    lax.fori_loop(0, members, copy, 0, unroll=8)
    base = lax.axis_index("x") * half_columns
    for k in range(half_columns):
        for half in range(2):
            spot = 5 * tiles + half
            copies_ref[base + k, spot : spot + 1, :] = near_all[half * half_columns + k : half * half_columns + k + 1, :]


def points_kernel(partner_ref, across_ref, tests_ref, wide_ref):
    row_dev = tests_ref.shape[1]
    lane = lax.broadcasted_iota(jnp.int32, (row_dev, LANES), 1)
    sub = lax.broadcasted_iota(jnp.int32, (row_dev, LANES), 0)
    for which, ref in enumerate((partner_ref, across_ref, tests_ref)):
        points = jnp.concatenate([ref[...], jnp.zeros((3, LANES - row_dev), jnp.float32)], axis=1) * TURNS
        for c in range(3):
            column = jnp.sum(jnp.where(lane == sub, points[c : c + 1, :], 0.0), axis=1, keepdims=True)
            wide_ref[which, c] = jnp.broadcast_to(column, (row_dev, LANES))


def groups_of(wide_ref, which):
    return [[wide_ref[which, c, pl.ds(g * SUB, SUB), :] for c in range(3)] for g in range(wide_ref.shape[2] // SUB)]


def far_loop(tests, sums, messages_ref):
    members = messages_ref.shape[0]
    tiles = (messages_ref.shape[1] - SUB) // 5
    soft = (SOFTENING * TURNS) ** 2

    def step(member, sums):
        for tile in range(tiles):
            sx, sy, sz, size, turn = [
                jnp.broadcast_to(messages_ref[member, c * tiles + tile : c * tiles + tile + 1, :], (SUB, LANES))
                for c in range(5)
            ]
            new = []
            for (tx, ty, tz), (re, im) in zip(tests, sums):
                dx = tx - sx
                dy = ty - sy
                dz = tz - sz
                square = dx * dx + dy * dy + (dz * dz + soft)
                inverse = lax.rsqrt(square)
                t = square * inverse - turn
                u = t - ((t + ROUNDER) - ROUNDER)
                u2 = u * u
                s = u * horner(SINE, u2)
                c = horner(COSINE, u2)
                a = inverse * size
                p = a * s
                new.append(((re + a) - p * s, im + p * c))
            sums = tuple(new)
        return sums

    return lax.fori_loop(0, members, step, tuple(sums), unroll=4 // len(tests))


def rows_of(sums):
    row_dev = len(sums) * SUB
    diagonal = lax.broadcasted_iota(jnp.int32, (row_dev, LANES), 1) == lax.broadcasted_iota(jnp.int32, (row_dev, LANES), 0)
    rows = []
    for part in range(2):
        column = jnp.concatenate([jnp.sum(pair[part], axis=1, keepdims=True) for pair in sums], axis=0)
        rows.append(jnp.sum(jnp.where(diagonal, column, 0.0), axis=0, keepdims=True))
    return rows


def near_of(half_columns, other, messages_ref):
    half = lax.axis_index("half")
    spot = messages_ref.shape[1] - SUB + (1 - half if other else half)
    base = lax.axis_index("x") * half_columns
    total = messages_ref[base, pl.ds(spot, 1), :]
    for k in range(1, half_columns):
        total = total + messages_ref[base + k, pl.ds(spot, 1), :]
    return total


def first_kernel(half_columns, wide_ref, messages_ref, partner_out, across_out):
    row_dev = wide_ref.shape[2]
    groups = row_dev // SUB
    near = near_of(half_columns, True, messages_ref)
    zero = jnp.zeros((SUB, LANES), jnp.float32)
    sums = far_loop(groups_of(wide_ref, 0) + groups_of(wide_ref, 1), [(zero, zero)] * (2 * groups), messages_ref)
    re, im = rows_of(sums[:groups])
    partner_out[0:1, :] = re[:, :row_dev] + near[:, :row_dev]
    partner_out[1:2, :] = im[:, :row_dev] + near[:, row_dev : 2 * row_dev]
    re, im = rows_of(sums[groups:])
    across_out[0:1, :] = re[:, :row_dev]
    across_out[1:2, :] = im[:, :row_dev]


def second_kernel(half_columns, wide_ref, messages_ref, sibling_ref, out_ref):
    row_dev = wide_ref.shape[2]
    near = near_of(half_columns, False, messages_ref)
    tests = groups_of(wide_ref, 2)
    zero = jnp.zeros((SUB, LANES), jnp.float32)
    sums = far_loop(tests, [(zero, zero)] * len(tests), messages_ref)
    re, im = rows_of(far_loop(tests, sums, sibling_ref))
    out_ref[0:1, :] = re[:, :row_dev] + near[:, :row_dev]
    out_ref[1:2, :] = im[:, :row_dev] + near[:, row_dev : 2 * row_dev]


def swap(x, axis):
    return lax.ppermute(x, axis, [(0, 1), (1, 0)])


def across(x):
    return lax.ppermute(x, ("core", "half"), [(i, 3 - i) for i in range(4)])


def local(rows, half_columns, test_points, src_points, currents, near_blocks, near_dest, near_tile):
    row_dev = test_points.shape[1]
    width = src_points.shape[1]
    items = near_blocks.shape[0]
    members = rows // 2 * half_columns
    gain = TURNS / math.sqrt(width * members * 4)
    message = (5 * width // LANES + SUB, LANES)
    vmem = pl.BlockSpec(memory_space=pltpu.VMEM)
    hbm = pl.BlockSpec(memory_space=pltpu.HBM)
    params = pltpu.CompilerParams(vmem_limit_bytes=24 << 20)

    partner_points = swap(test_points, "half")
    across_points = across(test_points)
    copies = pl.pallas_call(
        functools.partial(pack_kernel, half_columns, gain),
        out_shape=jax.ShapeDtypeStruct((members,) + message, jnp.float32),
        in_specs=[hbm] * 5,
        out_specs=vmem,
        scratch_shapes=[
            pltpu.SMEM((items,), jnp.int32),
            pltpu.SMEM((items,), jnp.int32),
            pltpu.VMEM((3, width), jnp.float32),
            pltpu.VMEM((2, width), jnp.float32),
            pltpu.VMEM(near_blocks.shape, jnp.float32),
            pltpu.VMEM(message, jnp.float32),
            pltpu.VMEM((2 * half_columns, LANES), jnp.float32),
            pltpu.SemaphoreType.DMA((5,)),
        ],
        cost_estimate=pl.CostEstimate(flops=1 << 20, bytes_accessed=1 << 20, transcendentals=0),
    )(near_dest.reshape(-1), near_tile.reshape(-1), src_points, currents, near_blocks)
    messages = lax.all_to_all(copies, ("x", "column"), split_axis=0, concat_axis=0, tiled=True)


    evaluations = width * members * row_dev

    def cost(times):
        return dict(
            compiler_params=params,
            cost_estimate=pl.CostEstimate(
                flops=40 * evaluations * times, bytes_accessed=2 << 20, transcendentals=evaluations * times
            ),
        )

    wide = pl.pallas_call(
        points_kernel,
        out_shape=jax.ShapeDtypeStruct((3, 3, row_dev, LANES), jnp.float32),
        in_specs=[vmem] * 3,
        out_specs=vmem,
        **cost(1),
    )(partner_points, across_points, test_points)

    messages, wide = lax.optimization_barrier((messages, wide))
    sibling = swap(messages, "core")
    sums = jax.ShapeDtypeStruct((2, row_dev), jnp.float32)
    to_partner, to_across = pl.pallas_call(
        functools.partial(first_kernel, half_columns),
        out_shape=(sums, sums),
        in_specs=[vmem] * 2,
        out_specs=(vmem, vmem),
        **cost(2),
    )(wide, messages)
    from_partner = swap(to_partner, "half")
    from_across = across(to_across)
    own = pl.pallas_call(
        functools.partial(second_kernel, half_columns),
        out_shape=sums,
        in_specs=[vmem] * 3,
        out_specs=vmem,
        **cost(2),
    )(wide, messages, sibling)
    return own + from_partner + from_across


def solution(mesh):
    rows, columns = mesh.shape["row"], mesh.shape["col"]
    finer = jax.sharding.Mesh(mesh.devices.reshape(rows // 2, 2, 2, columns // 2), ("x", "core", "half", "column"))
    every = ("x", "core", "half", "column")
    in_specs = (
        P(None, every),
        P(None, every),
        P(None, every),
        P(every, None, None, None),
        P(every, None),
        P(every, None),
    )
    body = functools.partial(local, rows, columns // 2)
    return jax.shard_map(body, mesh=finer, in_specs=in_specs, out_specs=P(None, every), check_vma=False)
```

```python
import functools
import math

import jax
import jax.numpy as jnp
import numpy as np
from jax import lax
from jax.experimental import pallas as pl
from jax.experimental.pallas import tpu as pltpu
from jax.sharding import PartitionSpec as P

WAVENUMBER = 40.0
SOFTENING = 0.01
TURNS = WAVENUMBER / (2.0 * math.pi)
LANES = 128
SUB = 8


def even_fit(function, terms, reach):
    nodes = np.cos((np.arange(400) + 0.5) * np.pi / 400)
    squares = (nodes + 1) * 0.5 * reach * reach
    fit = np.polynomial.chebyshev.Chebyshev.fit(squares, function(np.sqrt(squares)), terms - 1)
    return [float(value) for value in fit.convert(kind=np.polynomial.Polynomial).coef]


ROOT2 = math.sqrt(2.0)
SINE = even_fit(lambda u: ROOT2 * math.pi * np.sinc(u), 4, 0.5)
COSINE = even_fit(lambda u: -ROOT2 * np.cos(np.pi * u), 5, 0.5)
ANGLE = even_fit(lambda r: np.arctan(r) / (2 * np.pi * r), 9, 1.0)
ROUNDER = 1.5 * 2.0**23


def horner(coefficients, x):
    total = coefficients[-1] * x + coefficients[-2]
    for value in coefficients[-3::-1]:
        total = total * x + value
    return total


def phase_of(re, im):
    wide = jnp.abs(re)
    high = jnp.abs(im)
    larger = jnp.maximum(wide, high)
    ratio = jnp.minimum(wide, high) / jnp.where(larger == 0.0, 1.0, larger)
    turn = ratio * horner(ANGLE, ratio * ratio)
    turn = jnp.where(high > wide, 0.25 - turn, turn)
    turn = jnp.where(re < 0.0, 0.5 - turn, turn)
    return jnp.where(im < 0.0, -turn, turn)


def pack_kernel(
    half_columns, gain, dest_hbm, tile_hbm, src_hbm, cur_hbm, blocks_hbm, copies_ref,
    dest_ref, tile_ref, src_ref, cur_ref, blocks_ref, message, near_all, sems
):
    moves = [
        pltpu.make_async_copy(source, target, sems.at[k])
        for k, (source, target) in enumerate((
            (src_hbm, src_ref), (cur_hbm, cur_ref), (blocks_hbm, blocks_ref), (dest_hbm, dest_ref), (tile_hbm, tile_ref)
        ))
    ]
    for move in moves:
        move.start()
    members = copies_ref.shape[0]
    tiles = src_ref.shape[1] // LANES
    items, _, row_dev, _ = blocks_ref.shape
    columns = 2 * half_columns
    lane = lax.broadcasted_iota(jnp.int32, (SUB, LANES), 1)
    sub = lax.broadcasted_iota(jnp.int32, (SUB, LANES), 0)
    for move in moves:
        move.wait()

    for tile in range(tiles):
        part = pl.ds(tile * LANES, LANES)
        message[pl.ds(3 * tiles + tile, 2, stride=tiles), :] = cur_ref[:, part]
        message[pl.ds(tile, 3, stride=tiles), :] = src_ref[:, part]
    cr = message[3 * tiles : 4 * tiles, :]
    ci = message[4 * tiles : 5 * tiles, :]
    places = message[: 3 * tiles, :] * TURNS
    size = jnp.sqrt(cr * cr + ci * ci) * gain
    turn = phase_of(cr, ci)

    near = [jnp.zeros((SUB, LANES), jnp.float32)] * (columns // SUB)
    for block in range(items):
        tile = pl.multiple_of(tile_ref[block] * LANES, LANES)
        cr = cur_ref[0:1, pl.ds(tile, LANES)]
        ci = cur_ref[1:2, pl.ds(tile, LANES)]
        br = blocks_ref[block, 0]
        bi = blocks_ref[block, 1]
        row = jnp.zeros((SUB, LANES), jnp.float32)
        for part, product in enumerate((br * cr - bi * ci, br * ci + bi * cr)):
            total = jnp.sum(product, axis=1, keepdims=True)
            for piece in range(row_dev // SUB):
                spot = lane == sub + (part * row_dev + piece * SUB)
                row = jnp.where(spot, total[piece * SUB : (piece + 1) * SUB], row)
        row = jnp.sum(row, axis=0, keepdims=True)
        for group in range(columns // SUB):
            near[group] = near[group] + jnp.where(sub + group * SUB == dest_ref[block], row, 0.0)
    for group in range(columns // SUB):
        near_all[pl.ds(group * SUB, SUB), :] = near[group]

    def copy(member, _):
        copies_ref[member, : 3 * tiles, :] = places
        copies_ref[member, 3 * tiles : 4 * tiles, :] = size
        copies_ref[member, 4 * tiles : 5 * tiles, :] = turn
        copies_ref[member, 5 * tiles :, :] = jnp.zeros((SUB, LANES), jnp.float32)
        return 0

    lax.fori_loop(0, members, copy, 0, unroll=8)
    base = lax.axis_index("x") * half_columns
    for k in range(half_columns):
        for half in range(2):
            spot = 5 * tiles + half
            copies_ref[base + k, spot : spot + 1, :] = near_all[half * half_columns + k : half * half_columns + k + 1, :]


def points_kernel(partner_ref, tests_ref, wide_ref):
    row_dev = tests_ref.shape[1]
    lane = lax.broadcasted_iota(jnp.int32, (row_dev, LANES), 1)
    sub = lax.broadcasted_iota(jnp.int32, (row_dev, LANES), 0)
    for which, ref in enumerate((partner_ref, tests_ref)):
        points = jnp.concatenate([ref[...], jnp.zeros((3, LANES - row_dev), jnp.float32)], axis=1) * TURNS
        for c in range(3):
            column = jnp.sum(jnp.where(lane == sub, points[c : c + 1, :], 0.0), axis=1, keepdims=True)
            wide_ref[which, c] = jnp.broadcast_to(column, (row_dev, LANES))


def groups_of(wide_ref, which):
    return [[wide_ref[which, c, pl.ds(g * SUB, SUB), :] for c in range(3)] for g in range(wide_ref.shape[2] // SUB)]


def far_loop(tests, sums, messages_ref):
    members = messages_ref.shape[0]
    tiles = (messages_ref.shape[1] - SUB) // 5
    soft = (SOFTENING * TURNS) ** 2

    def step(member, sums):
        for tile in range(tiles):
            sx, sy, sz, size, turn = [
                jnp.broadcast_to(messages_ref[member, c * tiles + tile : c * tiles + tile + 1, :], (SUB, LANES))
                for c in range(5)
            ]
            new = []
            for (tx, ty, tz), (re, im) in zip(tests, sums):
                dx = tx - sx
                dy = ty - sy
                dz = tz - sz
                square = dx * dx + dy * dy + (dz * dz + soft)
                inverse = lax.rsqrt(square)
                t = square * inverse - turn
                u = t - ((t + ROUNDER) - ROUNDER)
                u2 = u * u
                s = u * horner(SINE, u2)
                c = horner(COSINE, u2)
                a = inverse * size
                p = a * s
                new.append(((re + a) - p * s, im + p * c))
            sums = tuple(new)
        return sums

    return lax.fori_loop(0, members, step, tuple(sums), unroll=8 // len(tests))


def rows_of(sums):
    row_dev = len(sums) * SUB
    diagonal = lax.broadcasted_iota(jnp.int32, (row_dev, LANES), 1) == lax.broadcasted_iota(jnp.int32, (row_dev, LANES), 0)
    rows = []
    for part in range(2):
        column = jnp.concatenate([jnp.sum(pair[part], axis=1, keepdims=True) for pair in sums], axis=0)
        rows.append(jnp.sum(jnp.where(diagonal, column, 0.0), axis=0, keepdims=True))
    return rows


def near_of(half_columns, other, messages_ref):
    half = lax.axis_index("half")
    spot = messages_ref.shape[1] - SUB + (1 - half if other else half)
    base = lax.axis_index("x") * half_columns
    total = messages_ref[base, pl.ds(spot, 1), :]
    for k in range(1, half_columns):
        total = total + messages_ref[base + k, pl.ds(spot, 1), :]
    return total


def first_kernel(wide_ref, messages_ref, sums_ref):
    groups = wide_ref.shape[2] // SUB
    tests = groups_of(wide_ref, 0) + groups_of(wide_ref, 1)
    zero = jnp.zeros((SUB, LANES), jnp.float32)
    for k, pair in enumerate(far_loop(tests, [(zero, zero)] * len(tests), messages_ref)):
        for part in range(2):
            sums_ref[k // groups, part, pl.ds(k % groups * SUB, SUB), :] = pair[part]


def second_kernel(half_columns, other, wide_ref, sums_ref, messages_ref, sibling_ref, out_ref):
    row_dev = wide_ref.shape[2]
    which = 0 if other else 1
    tests = groups_of(wide_ref, which)
    near = near_of(half_columns, other, messages_ref)
    sums = [
        (sums_ref[which, 0, pl.ds(g * SUB, SUB), :], sums_ref[which, 1, pl.ds(g * SUB, SUB), :]) for g in range(len(tests))
    ]
    re, im = rows_of(far_loop(tests, sums, sibling_ref))
    out_ref[0:1, :] = re[:, :row_dev] + near[:, :row_dev]
    out_ref[1:2, :] = im[:, :row_dev] + near[:, row_dev : 2 * row_dev]


def swap(x, axis):
    return lax.ppermute(x, axis, [(0, 1), (1, 0)])


def local(rows, half_columns, test_points, src_points, currents, near_blocks, near_dest, near_tile):
    row_dev = test_points.shape[1]
    width = src_points.shape[1]
    items = near_blocks.shape[0]
    members = rows // 2 * half_columns
    gain = TURNS / math.sqrt(width * members * 4)
    message = (5 * width // LANES + SUB, LANES)
    vmem = pl.BlockSpec(memory_space=pltpu.VMEM)
    hbm = pl.BlockSpec(memory_space=pltpu.HBM)
    params = pltpu.CompilerParams(vmem_limit_bytes=24 << 20)

    partner_points = swap(test_points, "half")
    copies = pl.pallas_call(
        functools.partial(pack_kernel, half_columns, gain),
        out_shape=jax.ShapeDtypeStruct((members,) + message, jnp.float32),
        in_specs=[hbm] * 5,
        out_specs=vmem,
        scratch_shapes=[
            pltpu.SMEM((items,), jnp.int32),
            pltpu.SMEM((items,), jnp.int32),
            pltpu.VMEM((3, width), jnp.float32),
            pltpu.VMEM((2, width), jnp.float32),
            pltpu.VMEM(near_blocks.shape, jnp.float32),
            pltpu.VMEM(message, jnp.float32),
            pltpu.VMEM((2 * half_columns, LANES), jnp.float32),
            pltpu.SemaphoreType.DMA((5,)),
        ],
        cost_estimate=pl.CostEstimate(flops=1 << 20, bytes_accessed=1 << 20, transcendentals=0),
    )(near_dest.reshape(-1), near_tile.reshape(-1), src_points, currents, near_blocks)
    messages = lax.all_to_all(copies, ("x", "column"), split_axis=0, concat_axis=0, tiled=True)


    evaluations = width * members * row_dev

    def cost(times):
        return dict(
            compiler_params=params,
            cost_estimate=pl.CostEstimate(
                flops=40 * evaluations * times, bytes_accessed=2 << 20, transcendentals=evaluations * times
            ),
        )

    wide = pl.pallas_call(
        points_kernel,
        out_shape=jax.ShapeDtypeStruct((2, 3, row_dev, LANES), jnp.float32),
        in_specs=[vmem] * 2,
        out_specs=vmem,
        **cost(1),
    )(partner_points, test_points)

    messages, wide = lax.optimization_barrier((messages, wide))
    sibling = swap(messages, "core")
    sums = pl.pallas_call(
        first_kernel,
        out_shape=jax.ShapeDtypeStruct((2, 2, row_dev, LANES), jnp.float32),
        in_specs=[vmem] * 2,
        out_specs=vmem,
        **cost(2),
    )(wide, messages)

    def second(other):
        return pl.pallas_call(
            functools.partial(second_kernel, half_columns, other),
            out_shape=jax.ShapeDtypeStruct((2, row_dev), jnp.float32),
            in_specs=[vmem] * 4,
            out_specs=vmem,
            **cost(1),
        )(wide, sums, messages, sibling)

    from_partner = swap(second(True), "half")
    return second(False) + from_partner


def solution(mesh):
    rows, columns = mesh.shape["row"], mesh.shape["col"]
    finer = jax.sharding.Mesh(mesh.devices.reshape(rows // 2, 2, 2, columns // 2), ("x", "core", "half", "column"))
    every = ("x", "core", "half", "column")
    in_specs = (
        P(None, every),
        P(None, every),
        P(None, every),
        P(every, None, None, None),
        P(every, None),
        P(every, None),
    )
    body = functools.partial(local, rows, columns // 2)
    return jax.shard_map(body, mesh=finer, in_specs=in_specs, out_specs=P(None, every), check_vma=False)
```

```python
import functools
import math

import jax
import jax.numpy as jnp
import numpy as np
from jax import lax
from jax.experimental import pallas as pl
from jax.experimental.pallas import tpu as pltpu
from jax.sharding import PartitionSpec as P

WAVENUMBER = 40.0
SOFTENING = 0.01
TURNS = WAVENUMBER / (2.0 * math.pi)
LANES = 128
SUB = 8
QUAD = 4


def even_fit(function, terms, reach):
    nodes = np.cos((np.arange(400) + 0.5) * np.pi / 400)
    squares = (nodes + 1) * 0.5 * reach * reach
    fit = np.polynomial.chebyshev.Chebyshev.fit(squares, function(np.sqrt(squares)), terms - 1)
    return [float(value) for value in fit.convert(kind=np.polynomial.Polynomial).coef]


ROOT2 = math.sqrt(2.0)
SINE = even_fit(lambda u: ROOT2 * math.pi * np.sinc(u), 4, 0.5)
COSINE = even_fit(lambda u: -ROOT2 * np.cos(np.pi * u), 5, 0.5)
ANGLE = even_fit(lambda r: np.arctan(r) / (2 * np.pi * r), 9, 1.0)
ROUNDER = 1.5 * 2.0**23


def horner(coefficients, x):
    total = coefficients[-1] * x + coefficients[-2]
    for value in coefficients[-3::-1]:
        total = total * x + value
    return total


def phase_of(re, im):
    wide = jnp.abs(re)
    high = jnp.abs(im)
    larger = jnp.maximum(wide, high)
    ratio = jnp.minimum(wide, high) / jnp.where(larger == 0.0, 1.0, larger)
    turn = ratio * horner(ANGLE, ratio * ratio)
    turn = jnp.where(high > wide, 0.25 - turn, turn)
    turn = jnp.where(re < 0.0, 0.5 - turn, turn)
    return jnp.where(im < 0.0, -turn, turn)


def pack_kernel(
    half_columns, gain, dest_hbm, tile_hbm, src_hbm, cur_hbm, blocks_hbm, copies_ref,
    dest_ref, tile_ref, src_ref, cur_ref, blocks_ref, message, near_all, sems
):
    moves = [
        pltpu.make_async_copy(source, target, sems.at[k])
        for k, (source, target) in enumerate((
            (src_hbm, src_ref), (cur_hbm, cur_ref), (blocks_hbm, blocks_ref), (dest_hbm, dest_ref), (tile_hbm, tile_ref)
        ))
    ]
    for move in moves:
        move.start()
    members = copies_ref.shape[0]
    tiles = src_ref.shape[1] // LANES
    items, _, row_dev, _ = blocks_ref.shape
    columns = 2 * half_columns
    lane = lax.broadcasted_iota(jnp.int32, (SUB, LANES), 1)
    sub = lax.broadcasted_iota(jnp.int32, (SUB, LANES), 0)
    moves[0].wait()
    moves[1].wait()

    for tile in range(tiles):
        part = pl.ds(tile * LANES, LANES)
        message[pl.ds(3 * tiles + tile, 2, stride=tiles), :] = cur_ref[:, part]
        message[pl.ds(tile, 3, stride=tiles), :] = src_ref[:, part]
    cr = message[3 * tiles : 4 * tiles, :]
    ci = message[4 * tiles : 5 * tiles, :]
    values = [message[c * tiles : (c + 1) * tiles, :] * TURNS for c in range(3)]
    values += [jnp.sqrt(cr * cr + ci * ci) * gain, phase_of(cr, ci)]
    pieces = [value[part * QUAD : (part + 1) * QUAD] for value in values for part in range(tiles // QUAD)]
    last = len(pieces) * LANES

    def copy(member, _):
        for slot, piece in enumerate(pieces):
            copies_ref[member, :, slot * LANES : (slot + 1) * LANES] = piece
        copies_ref[member, :, last:] = jnp.zeros((QUAD, LANES), jnp.float32)
        return 0

    lax.fori_loop(0, members, copy, 0, unroll=8)

    for move in moves[2:]:
        move.wait()
    near = [jnp.zeros((SUB, LANES), jnp.float32)] * (columns // SUB)
    for block in range(items):
        tile = pl.multiple_of(tile_ref[block] * LANES, LANES)
        cr = cur_ref[0:1, pl.ds(tile, LANES)]
        ci = cur_ref[1:2, pl.ds(tile, LANES)]
        br = blocks_ref[block, 0]
        bi = blocks_ref[block, 1]
        row = jnp.zeros((SUB, LANES), jnp.float32)
        for part, product in enumerate((br * cr - bi * ci, br * ci + bi * cr)):
            total = jnp.sum(product, axis=1, keepdims=True)
            for piece in range(row_dev // SUB):
                spot = lane == sub + (part * row_dev + piece * SUB)
                row = jnp.where(spot, total[piece * SUB : (piece + 1) * SUB], row)
        row = jnp.sum(row, axis=0, keepdims=True)
        for group in range(columns // SUB):
            near[group] = near[group] + jnp.where(sub + group * SUB == dest_ref[block], row, 0.0)
    for group in range(columns // SUB):
        near_all[pl.ds(group * SUB, SUB), :] = near[group]

    base = lax.axis_index("x") * half_columns
    for k in range(half_columns):
        for half in range(2):
            copies_ref[base + k, half : half + 1, last:] = near_all[half * half_columns + k : half * half_columns + k + 1, :]


def points_kernel(partner_ref, tests_ref, wide_ref):
    row_dev = tests_ref.shape[1]
    lane = lax.broadcasted_iota(jnp.int32, (row_dev, LANES), 1)
    sub = lax.broadcasted_iota(jnp.int32, (row_dev, LANES), 0)
    for which, ref in enumerate((partner_ref, tests_ref)):
        points = jnp.concatenate([ref[...], jnp.zeros((3, LANES - row_dev), jnp.float32)], axis=1) * TURNS
        for c in range(3):
            column = jnp.sum(jnp.where(lane == sub, points[c : c + 1, :], 0.0), axis=1, keepdims=True)
            wide_ref[which, c] = jnp.broadcast_to(column, (row_dev, LANES))


def groups_of(wide_ref, which):
    return [[wide_ref[which, c, pl.ds(g * SUB, SUB), :] for c in range(3)] for g in range(wide_ref.shape[2] // SUB)]


def far_loop(tests, sums, messages_ref):
    members = messages_ref.shape[0]
    slots = (messages_ref.shape[2] // LANES - 1) // 5
    soft = (SOFTENING * TURNS) ** 2

    def step(member, sums):
        for slot, row in [(slot, row) for slot in range(slots) for row in range(QUAD)]:
            sx, sy, sz, size, turn = [
                jnp.broadcast_to(
                    messages_ref[member, row : row + 1, (c * slots + slot) * LANES : (c * slots + slot + 1) * LANES], (SUB, LANES)
                )
                for c in range(5)
            ]
            new = []
            for (tx, ty, tz), (re, im) in zip(tests, sums):
                dx = tx - sx
                dy = ty - sy
                dz = tz - sz
                square = dx * dx + dy * dy + (dz * dz + soft)
                inverse = lax.rsqrt(square)
                t = square * inverse - turn
                u = t - ((t + ROUNDER) - ROUNDER)
                u2 = u * u
                s = u * horner(SINE, u2)
                c = horner(COSINE, u2)
                a = inverse * size
                p = a * s
                new.append(((re + a) - p * s, im + p * c))
            sums = tuple(new)
        return sums

    return lax.fori_loop(0, members, step, tuple(sums), unroll=8 // len(tests))


def rows_of(sums):
    row_dev = len(sums) * SUB
    diagonal = lax.broadcasted_iota(jnp.int32, (row_dev, LANES), 1) == lax.broadcasted_iota(jnp.int32, (row_dev, LANES), 0)
    rows = []
    for part in range(2):
        column = jnp.concatenate([jnp.sum(pair[part], axis=1, keepdims=True) for pair in sums], axis=0)
        rows.append(jnp.sum(jnp.where(diagonal, column, 0.0), axis=0, keepdims=True))
    return rows


def near_of(half_columns, other, messages_ref):
    last = messages_ref.shape[2] - LANES
    base = lax.axis_index("x") * half_columns
    total = messages_ref[base, :, last:]
    for k in range(1, half_columns):
        total = total + messages_ref[base + k, :, last:]
    first = lax.axis_index("half") == (1 if other else 0)
    return jnp.where(first, total[0:1], total[1:2])


def first_kernel(wide_ref, messages_ref, sums_ref):
    groups = wide_ref.shape[2] // SUB
    tests = groups_of(wide_ref, 0) + groups_of(wide_ref, 1)
    zero = jnp.zeros((SUB, LANES), jnp.float32)
    for k, pair in enumerate(far_loop(tests, [(zero, zero)] * len(tests), messages_ref)):
        for part in range(2):
            sums_ref[k // groups, part, pl.ds(k % groups * SUB, SUB), :] = pair[part]


def second_kernel(half_columns, other, wide_ref, sums_ref, messages_ref, sibling_ref, out_ref):
    row_dev = wide_ref.shape[2]
    which = 0 if other else 1
    tests = groups_of(wide_ref, which)
    near = near_of(half_columns, other, messages_ref)
    sums = [
        (sums_ref[which, 0, pl.ds(g * SUB, SUB), :], sums_ref[which, 1, pl.ds(g * SUB, SUB), :]) for g in range(len(tests))
    ]
    re, im = rows_of(far_loop(tests, sums, sibling_ref))
    out_ref[0:1, :] = re[:, :row_dev] + near[:, :row_dev]
    out_ref[1:2, :] = im[:, :row_dev] + near[:, row_dev : 2 * row_dev]


def swap(x, axis):
    return lax.ppermute(x, axis, [(0, 1), (1, 0)])


def local(rows, half_columns, test_points, src_points, currents, near_blocks, near_dest, near_tile):
    row_dev = test_points.shape[1]
    width = src_points.shape[1]
    items = near_blocks.shape[0]
    members = rows // 2 * half_columns
    gain = TURNS / math.sqrt(width * members * 4)
    message = (QUAD, 5 * width // QUAD + LANES)
    vmem = pl.BlockSpec(memory_space=pltpu.VMEM)
    hbm = pl.BlockSpec(memory_space=pltpu.HBM)
    params = pltpu.CompilerParams(vmem_limit_bytes=24 << 20)

    partner_points = swap(test_points, "half")
    copies = pl.pallas_call(
        functools.partial(pack_kernel, half_columns, gain),
        out_shape=jax.ShapeDtypeStruct((members,) + message, jnp.float32),
        in_specs=[hbm] * 5,
        out_specs=vmem,
        scratch_shapes=[
            pltpu.SMEM((items,), jnp.int32),
            pltpu.SMEM((items,), jnp.int32),
            pltpu.VMEM((3, width), jnp.float32),
            pltpu.VMEM((2, width), jnp.float32),
            pltpu.VMEM(near_blocks.shape, jnp.float32),
            pltpu.VMEM((5 * width // LANES, LANES), jnp.float32),
            pltpu.VMEM((2 * half_columns, LANES), jnp.float32),
            pltpu.SemaphoreType.DMA((5,)),
        ],
        cost_estimate=pl.CostEstimate(flops=1 << 20, bytes_accessed=1 << 20, transcendentals=0),
    )(near_dest.reshape(-1), near_tile.reshape(-1), src_points, currents, near_blocks)
    messages = lax.all_to_all(copies, ("x", "column"), split_axis=0, concat_axis=0, tiled=True)


    evaluations = width * members * row_dev

    def cost(times):
        return dict(
            compiler_params=params,
            cost_estimate=pl.CostEstimate(
                flops=40 * evaluations * times, bytes_accessed=2 << 20, transcendentals=evaluations * times
            ),
        )

    wide = pl.pallas_call(
        points_kernel,
        out_shape=jax.ShapeDtypeStruct((2, 3, row_dev, LANES), jnp.float32),
        in_specs=[vmem] * 2,
        out_specs=vmem,
        **cost(1),
    )(partner_points, test_points)

    messages, wide = lax.optimization_barrier((messages, wide))
    sibling = swap(messages, "core")
    sums = pl.pallas_call(
        first_kernel,
        out_shape=jax.ShapeDtypeStruct((2, 2, row_dev, LANES), jnp.float32),
        in_specs=[vmem] * 2,
        out_specs=vmem,
        **cost(2),
    )(wide, messages)

    def second(other):
        return pl.pallas_call(
            functools.partial(second_kernel, half_columns, other),
            out_shape=jax.ShapeDtypeStruct((2, row_dev), jnp.float32),
            in_specs=[vmem] * 4,
            out_specs=vmem,
            **cost(1),
        )(wide, sums, messages, sibling)

    from_partner = swap(second(True), "half")
    return second(False) + from_partner


def solution(mesh):
    rows, columns = mesh.shape["row"], mesh.shape["col"]
    finer = jax.sharding.Mesh(mesh.devices.reshape(rows // 2, 2, 2, columns // 2), ("x", "core", "half", "column"))
    every = ("x", "core", "half", "column")
    in_specs = (
        P(None, every),
        P(None, every),
        P(None, every),
        P(every, None, None, None),
        P(every, None),
        P(every, None),
    )
    body = functools.partial(local, rows, columns // 2)
    return jax.shard_map(body, mesh=finer, in_specs=in_specs, out_specs=P(None, every), check_vma=False)
```

```python
import functools
import math

import jax
import jax.numpy as jnp
import numpy as np
from jax import lax
from jax.experimental import pallas as pl
from jax.experimental.pallas import tpu as pltpu
from jax.sharding import PartitionSpec as P

WAVENUMBER = 40.0
SOFTENING = 0.01
TURNS = WAVENUMBER / (2.0 * math.pi)
LANES = 128
SUB = 8
QUAD = 4


def even_fit(function, terms, reach):
    nodes = np.cos((np.arange(400) + 0.5) * np.pi / 400)
    squares = (nodes + 1) * 0.5 * reach * reach
    fit = np.polynomial.chebyshev.Chebyshev.fit(squares, function(np.sqrt(squares)), terms - 1)
    return [float(value) for value in fit.convert(kind=np.polynomial.Polynomial).coef]


ROOT2 = math.sqrt(2.0)
SINE = even_fit(lambda u: ROOT2 * math.pi * np.sinc(u), 4, 0.5)
COSINE = even_fit(lambda u: -ROOT2 * np.cos(np.pi * u), 5, 0.5)
ANGLE = even_fit(lambda r: np.arctan(r) / (2 * np.pi * r), 9, 1.0)
ROUNDER = 1.5 * 2.0**23


def horner(coefficients, x):
    total = coefficients[-1] * x + coefficients[-2]
    for value in coefficients[-3::-1]:
        total = total * x + value
    return total


def phase_of(re, im):
    wide = jnp.abs(re)
    high = jnp.abs(im)
    larger = jnp.maximum(wide, high)
    ratio = jnp.minimum(wide, high) / jnp.where(larger == 0.0, 1.0, larger)
    turn = ratio * horner(ANGLE, ratio * ratio)
    turn = jnp.where(high > wide, 0.25 - turn, turn)
    turn = jnp.where(re < 0.0, 0.5 - turn, turn)
    return jnp.where(im < 0.0, -turn, turn)


def pack_kernel(
    half_columns, gain, dest_hbm, tile_hbm, src_hbm, cur_hbm, blocks_hbm, copies_ref,
    dest_ref, tile_ref, src_ref, cur_ref, blocks_ref, message, near_all, sems
):
    moves = [
        pltpu.make_async_copy(source, target, sems.at[k])
        for k, (source, target) in enumerate((
            (src_hbm, src_ref), (cur_hbm, cur_ref), (blocks_hbm, blocks_ref), (dest_hbm, dest_ref), (tile_hbm, tile_ref)
        ))
    ]
    for move in moves:
        move.start()
    members = copies_ref.shape[0]
    tiles = src_ref.shape[1] // LANES
    items, _, row_dev, _ = blocks_ref.shape
    columns = 2 * half_columns
    lane = lax.broadcasted_iota(jnp.int32, (SUB, LANES), 1)
    sub = lax.broadcasted_iota(jnp.int32, (SUB, LANES), 0)
    moves[0].wait()
    moves[1].wait()

    for tile in range(tiles):
        part = pl.ds(tile * LANES, LANES)
        message[pl.ds(3 * tiles + tile, 2, stride=tiles), :] = cur_ref[:, part]
        message[pl.ds(tile, 3, stride=tiles), :] = src_ref[:, part]
    cr = message[3 * tiles : 4 * tiles, :]
    ci = message[4 * tiles : 5 * tiles, :]
    values = [message[c * tiles : (c + 1) * tiles, :] * TURNS for c in range(3)]
    values += [jnp.sqrt(cr * cr + ci * ci) * gain, phase_of(cr, ci)]
    pieces = [value[part * QUAD : (part + 1) * QUAD] for value in values for part in range(tiles // QUAD)]
    last = len(pieces) * LANES

    def copy(member, _):
        for slot, piece in enumerate(pieces):
            copies_ref[member, :, slot * LANES : (slot + 1) * LANES] = piece
        copies_ref[member, :, last:] = jnp.zeros((QUAD, LANES), jnp.float32)
        return 0

    lax.fori_loop(0, members, copy, 0, unroll=8)

    for move in moves[2:]:
        move.wait()
    near = [jnp.zeros((SUB, LANES), jnp.float32)] * (columns // SUB)
    for block in range(items):
        tile = pl.multiple_of(tile_ref[block] * LANES, LANES)
        cr = cur_ref[0:1, pl.ds(tile, LANES)]
        ci = cur_ref[1:2, pl.ds(tile, LANES)]
        br = blocks_ref[block, 0]
        bi = blocks_ref[block, 1]
        row = jnp.zeros((SUB, LANES), jnp.float32)
        for part, product in enumerate((br * cr - bi * ci, br * ci + bi * cr)):
            total = jnp.sum(product, axis=1, keepdims=True)
            for piece in range(row_dev // SUB):
                spot = lane == sub + (part * row_dev + piece * SUB)
                row = jnp.where(spot, total[piece * SUB : (piece + 1) * SUB], row)
        row = jnp.sum(row, axis=0, keepdims=True)
        for group in range(columns // SUB):
            near[group] = near[group] + jnp.where(sub + group * SUB == dest_ref[block], row, 0.0)
    for group in range(columns // SUB):
        near_all[pl.ds(group * SUB, SUB), :] = near[group]

    base = lax.axis_index("x") * half_columns
    for k in range(half_columns):
        for half in range(2):
            copies_ref[base + k, half : half + 1, last:] = near_all[half * half_columns + k : half * half_columns + k + 1, :]


def points_kernel(partner_ref, tests_ref, wide_ref):
    row_dev = tests_ref.shape[1]
    lane = lax.broadcasted_iota(jnp.int32, (row_dev, LANES), 1)
    sub = lax.broadcasted_iota(jnp.int32, (row_dev, LANES), 0)
    for which, ref in enumerate((partner_ref, tests_ref)):
        points = jnp.concatenate([ref[...], jnp.zeros((3, LANES - row_dev), jnp.float32)], axis=1) * TURNS
        for c in range(3):
            column = jnp.sum(jnp.where(lane == sub, points[c : c + 1, :], 0.0), axis=1, keepdims=True)
            wide_ref[which, c] = jnp.broadcast_to(column, (row_dev, LANES))


def groups_of(wide_ref, which):
    return [[wide_ref[which, c, pl.ds(g * SUB, SUB), :] for c in range(3)] for g in range(wide_ref.shape[2] // SUB)]


def far_loop(tests, sums, messages_ref):
    members = messages_ref.shape[0]
    slots = (messages_ref.shape[2] // LANES - 1) // 5
    soft = (SOFTENING * TURNS) ** 2

    def step(member, sums):
        for slot, row in [(slot, row) for slot in range(slots) for row in range(QUAD)]:
            sx, sy, sz, size, turn = [
                jnp.broadcast_to(
                    messages_ref[member, row : row + 1, (c * slots + slot) * LANES : (c * slots + slot + 1) * LANES], (SUB, LANES)
                )
                for c in range(5)
            ]
            new = []
            for (tx, ty, tz), (re, im) in zip(tests, sums):
                dx = tx - sx
                dy = ty - sy
                dz = tz - sz
                square = dx * dx + dy * dy + (dz * dz + soft)
                inverse = lax.rsqrt(square)
                t = square * inverse - turn
                u = t - ((t + ROUNDER) - ROUNDER)
                u2 = u * u
                s = u * horner(SINE, u2)
                c = horner(COSINE, u2)
                a = inverse * size
                p = a * s
                new.append(((re + a) - p * s, im + p * c))
            sums = tuple(new)
        return sums

    return lax.fori_loop(0, members, step, tuple(sums), unroll=8 // len(tests))


def rows_of(sums):
    row_dev = len(sums) * SUB
    diagonal = lax.broadcasted_iota(jnp.int32, (row_dev, LANES), 1) == lax.broadcasted_iota(jnp.int32, (row_dev, LANES), 0)
    rows = []
    for part in range(2):
        column = jnp.concatenate([jnp.sum(pair[part], axis=1, keepdims=True) for pair in sums], axis=0)
        rows.append(jnp.sum(jnp.where(diagonal, column, 0.0), axis=0, keepdims=True))
    return rows


def near_of(half_columns, other, messages_ref):
    last = messages_ref.shape[2] - LANES
    base = lax.axis_index("x") * half_columns
    total = messages_ref[base, :, last:]
    for k in range(1, half_columns):
        total = total + messages_ref[base + k, :, last:]
    first = lax.axis_index("half") == (1 if other else 0)
    return jnp.where(first, total[0:1], total[1:2])


def first_kernel(wide_ref, messages_ref, sums_ref):
    groups = wide_ref.shape[2] // SUB
    tests = groups_of(wide_ref, 0) + groups_of(wide_ref, 1)
    zero = jnp.zeros((SUB, LANES), jnp.float32)
    for k, pair in enumerate(far_loop(tests, [(zero, zero)] * len(tests), messages_ref)):
        for part in range(2):
            sums_ref[k // groups, part, pl.ds(k % groups * SUB, SUB), :] = pair[part]


def second_kernel(half_columns, other, wide_ref, sums_ref, messages_ref, sibling_ref, out_ref):
    row_dev = wide_ref.shape[2]
    which = 0 if other else 1
    tests = groups_of(wide_ref, which)
    near = near_of(half_columns, other, sibling_ref if other else messages_ref)
    sums = [
        (sums_ref[which, 0, pl.ds(g * SUB, SUB), :], sums_ref[which, 1, pl.ds(g * SUB, SUB), :]) for g in range(len(tests))
    ]
    re, im = rows_of(far_loop(tests, sums, sibling_ref))
    out_ref[0:1, :] = re[:, :row_dev] + near[:, :row_dev]
    out_ref[1:2, :] = im[:, :row_dev] + near[:, row_dev : 2 * row_dev]


def across(x):
    return lax.ppermute(x, ("core", "half"), [(i, 3 - i) for i in range(4)])


def local(rows, half_columns, test_points, src_points, currents, near_blocks, near_dest, near_tile):
    row_dev = test_points.shape[1]
    width = src_points.shape[1]
    items = near_blocks.shape[0]
    members = rows // 2 * half_columns
    gain = TURNS / math.sqrt(width * members * 4)
    message = (QUAD, 5 * width // QUAD + LANES)
    vmem = pl.BlockSpec(memory_space=pltpu.VMEM)
    hbm = pl.BlockSpec(memory_space=pltpu.HBM)
    params = pltpu.CompilerParams(vmem_limit_bytes=24 << 20)

    partner_points = across(test_points)
    copies = pl.pallas_call(
        functools.partial(pack_kernel, half_columns, gain),
        out_shape=jax.ShapeDtypeStruct((members,) + message, jnp.float32),
        in_specs=[hbm] * 5,
        out_specs=vmem,
        scratch_shapes=[
            pltpu.SMEM((items,), jnp.int32),
            pltpu.SMEM((items,), jnp.int32),
            pltpu.VMEM((3, width), jnp.float32),
            pltpu.VMEM((2, width), jnp.float32),
            pltpu.VMEM(near_blocks.shape, jnp.float32),
            pltpu.VMEM((5 * width // LANES, LANES), jnp.float32),
            pltpu.VMEM((2 * half_columns, LANES), jnp.float32),
            pltpu.SemaphoreType.DMA((5,)),
        ],
        cost_estimate=pl.CostEstimate(flops=1 << 20, bytes_accessed=1 << 20, transcendentals=0),
    )(near_dest.reshape(-1), near_tile.reshape(-1), src_points, currents, near_blocks)
    messages = lax.all_to_all(copies, ("x", "column"), split_axis=0, concat_axis=0, tiled=True)


    evaluations = width * members * row_dev

    def cost(times):
        return dict(
            compiler_params=params,
            cost_estimate=pl.CostEstimate(
                flops=40 * evaluations * times, bytes_accessed=2 << 20, transcendentals=evaluations * times
            ),
        )

    wide = pl.pallas_call(
        points_kernel,
        out_shape=jax.ShapeDtypeStruct((2, 3, row_dev, LANES), jnp.float32),
        in_specs=[vmem] * 2,
        out_specs=vmem,
        **cost(1),
    )(partner_points, test_points)

    messages, wide = lax.optimization_barrier((messages, wide))
    sibling = lax.ppermute(messages, "core", [(0, 1), (1, 0)])
    sums = pl.pallas_call(
        first_kernel,
        out_shape=jax.ShapeDtypeStruct((2, 2, row_dev, LANES), jnp.float32),
        in_specs=[vmem] * 2,
        out_specs=vmem,
        **cost(2),
    )(wide, messages)

    def second(other):
        return pl.pallas_call(
            functools.partial(second_kernel, half_columns, other),
            out_shape=jax.ShapeDtypeStruct((2, row_dev), jnp.float32),
            in_specs=[vmem] * 4,
            out_specs=vmem,
            **cost(1),
        )(wide, sums, messages, sibling)

    from_partner = across(second(True))
    return second(False) + from_partner


def solution(mesh):
    rows, columns = mesh.shape["row"], mesh.shape["col"]
    finer = jax.sharding.Mesh(mesh.devices.reshape(rows // 2, 2, 2, columns // 2), ("x", "core", "half", "column"))
    every = ("x", "core", "half", "column")
    in_specs = (
        P(None, every),
        P(None, every),
        P(None, every),
        P(every, None, None, None),
        P(every, None),
        P(every, None),
    )
    body = functools.partial(local, rows, columns // 2)
    return jax.shard_map(body, mesh=finer, in_specs=in_specs, out_specs=P(None, every), check_vma=False)
```

```python
import functools
import math

import jax
import jax.numpy as jnp
import numpy as np
from jax import lax
from jax.experimental import pallas as pl
from jax.experimental.pallas import tpu as pltpu
from jax.sharding import PartitionSpec as P

WAVENUMBER = 40.0
SOFTENING = 0.01
TURNS = WAVENUMBER / (2.0 * math.pi)
LANES = 128
SUB = 8
QUAD = 4


def even_fit(function, terms, reach):
    nodes = np.cos((np.arange(400) + 0.5) * np.pi / 400)
    squares = (nodes + 1) * 0.5 * reach * reach
    fit = np.polynomial.chebyshev.Chebyshev.fit(squares, function(np.sqrt(squares)), terms - 1)
    return [float(value) for value in fit.convert(kind=np.polynomial.Polynomial).coef]


ROOT2 = math.sqrt(2.0)
SINE = even_fit(lambda u: ROOT2 * math.pi * np.sinc(u), 4, 0.5)
COSINE = even_fit(lambda u: -ROOT2 * np.cos(np.pi * u), 5, 0.5)
ANGLE = even_fit(lambda r: np.arctan(r) / (2 * np.pi * r), 9, 1.0)
ROUNDER = 1.5 * 2.0**23


def horner(coefficients, x):
    total = coefficients[-1] * x + coefficients[-2]
    for value in coefficients[-3::-1]:
        total = total * x + value
    return total


def phase_of(re, im):
    wide = jnp.abs(re)
    high = jnp.abs(im)
    larger = jnp.maximum(wide, high)
    ratio = jnp.minimum(wide, high) / jnp.where(larger == 0.0, 1.0, larger)
    turn = ratio * horner(ANGLE, ratio * ratio)
    turn = jnp.where(high > wide, 0.25 - turn, turn)
    turn = jnp.where(re < 0.0, 0.5 - turn, turn)
    return jnp.where(im < 0.0, -turn, turn)


def pack_kernel(
    half_columns, gain, dest_hbm, tile_hbm, src_hbm, cur_hbm, blocks_hbm, copies_ref,
    dest_ref, tile_ref, src_ref, cur_ref, blocks_ref, message, near_all, sems
):
    moves = [
        pltpu.make_async_copy(source, target, sems.at[k])
        for k, (source, target) in enumerate((
            (src_hbm, src_ref), (cur_hbm, cur_ref), (blocks_hbm, blocks_ref), (dest_hbm, dest_ref), (tile_hbm, tile_ref)
        ))
    ]
    for move in moves:
        move.start()
    members = copies_ref.shape[0]
    tiles = src_ref.shape[1] // LANES
    items, _, row_dev, _ = blocks_ref.shape
    columns = 2 * half_columns
    lane = lax.broadcasted_iota(jnp.int32, (SUB, LANES), 1)
    sub = lax.broadcasted_iota(jnp.int32, (SUB, LANES), 0)
    moves[0].wait()
    moves[1].wait()

    for tile in range(tiles):
        part = pl.ds(tile * LANES, LANES)
        message[pl.ds(3 * tiles + tile, 2, stride=tiles), :] = cur_ref[:, part]
        message[pl.ds(tile, 3, stride=tiles), :] = src_ref[:, part]
    cr = message[3 * tiles : 4 * tiles, :]
    ci = message[4 * tiles : 5 * tiles, :]
    values = [message[c * tiles : (c + 1) * tiles, :] * TURNS for c in range(3)]
    values += [jnp.sqrt(cr * cr + ci * ci) * gain, phase_of(cr, ci)]
    pieces = [value[part * QUAD : (part + 1) * QUAD] for value in values for part in range(tiles // QUAD)]
    last = len(pieces) * LANES

    def copy(member, _):
        for slot, piece in enumerate(pieces):
            copies_ref[member, :, slot * LANES : (slot + 1) * LANES] = piece
        copies_ref[member, :, last:] = jnp.zeros((QUAD, LANES), jnp.float32)
        return 0

    lax.fori_loop(0, members, copy, 0, unroll=8)

    for move in moves[2:]:
        move.wait()
    near = [jnp.zeros((SUB, LANES), jnp.float32)] * (columns // SUB)
    for block in range(items):
        tile = pl.multiple_of(tile_ref[block] * LANES, LANES)
        cr = cur_ref[0:1, pl.ds(tile, LANES)]
        ci = cur_ref[1:2, pl.ds(tile, LANES)]
        br = blocks_ref[block, 0]
        bi = blocks_ref[block, 1]
        row = jnp.zeros((SUB, LANES), jnp.float32)
        for part, product in enumerate((br * cr - bi * ci, br * ci + bi * cr)):
            total = jnp.sum(product, axis=1, keepdims=True)
            for piece in range(row_dev // SUB):
                spot = lane == sub + (part * row_dev + piece * SUB)
                row = jnp.where(spot, total[piece * SUB : (piece + 1) * SUB], row)
        row = jnp.sum(row, axis=0, keepdims=True)
        for group in range(columns // SUB):
            near[group] = near[group] + jnp.where(sub + group * SUB == dest_ref[block], row, 0.0)
    for group in range(columns // SUB):
        near_all[pl.ds(group * SUB, SUB), :] = near[group]

    base = lax.axis_index("x") * half_columns
    for k in range(half_columns):
        for half in range(2):
            copies_ref[base + k, half : half + 1, last:] = near_all[half * half_columns + k : half * half_columns + k + 1, :]


def points_kernel(partner_ref, tests_ref, wide_ref):
    row_dev = tests_ref.shape[1]
    lane = lax.broadcasted_iota(jnp.int32, (row_dev, LANES), 1)
    sub = lax.broadcasted_iota(jnp.int32, (row_dev, LANES), 0)
    for which, ref in enumerate((partner_ref, tests_ref)):
        points = jnp.concatenate([ref[...], jnp.zeros((3, LANES - row_dev), jnp.float32)], axis=1) * TURNS
        for c in range(3):
            column = jnp.sum(jnp.where(lane == sub, points[c : c + 1, :], 0.0), axis=1, keepdims=True)
            wide_ref[which, c] = jnp.broadcast_to(column, (row_dev, LANES))


def groups_of(wide_ref, which):
    return [[wide_ref[which, c, pl.ds(g * SUB, SUB), :] for c in range(3)] for g in range(wide_ref.shape[2] // SUB)]


def far_loop(tests, sums, messages_ref):
    members = messages_ref.shape[0]
    slots = (messages_ref.shape[2] // LANES - 1) // 5
    soft = (SOFTENING * TURNS) ** 2

    def step(member, sums):
        for slot, row in [(slot, row) for slot in range(slots) for row in range(QUAD)]:
            sx, sy, sz, size, turn = [
                jnp.broadcast_to(
                    messages_ref[member, row : row + 1, (c * slots + slot) * LANES : (c * slots + slot + 1) * LANES], (SUB, LANES)
                )
                for c in range(5)
            ]
            new = []
            for (tx, ty, tz), (re, im) in zip(tests, sums):
                dx = tx - sx
                dy = ty - sy
                dz = tz - sz
                square = dx * dx + dy * dy + (dz * dz + soft)
                inverse = lax.rsqrt(square)
                t = square * inverse - turn
                u = t - ((t + ROUNDER) - ROUNDER)
                u2 = u * u
                s = u * horner(SINE, u2)
                c = horner(COSINE, u2)
                a = inverse * size
                p = a * s
                new.append(((re + a) - p * s, im + p * c))
            sums = tuple(new)
        return sums

    return lax.fori_loop(0, members, step, tuple(sums), unroll=8 // len(tests))


def rows_of(sums):
    row_dev = len(sums) * SUB
    diagonal = lax.broadcasted_iota(jnp.int32, (row_dev, LANES), 1) == lax.broadcasted_iota(jnp.int32, (row_dev, LANES), 0)
    rows = []
    for part in range(2):
        column = jnp.concatenate([jnp.sum(pair[part], axis=1, keepdims=True) for pair in sums], axis=0)
        rows.append(jnp.sum(jnp.where(diagonal, column, 0.0), axis=0, keepdims=True))
    return rows


def near_of(half_columns, other, messages_ref, sibling_ref):
    last = messages_ref.shape[2] - LANES
    base = lax.axis_index("x") * half_columns
    middle = half_columns // 2
    straight = crossed = jnp.zeros((QUAD, LANES), jnp.float32)
    for k in range(half_columns):
        own, sibling = messages_ref[base + k, :, last:], sibling_ref[base + k, :, last:]
        straight = straight + (own if k < middle else sibling)
        crossed = crossed + (sibling if k < middle else own)
    upper = lax.axis_index("column") >= middle
    total = jnp.where(upper, straight, crossed) if other else jnp.where(upper, crossed, straight)
    first = lax.axis_index("half") == (1 if other else 0)
    return jnp.where(first, total[0:1], total[1:2])


def first_kernel(wide_ref, messages_ref, sums_ref):
    groups = wide_ref.shape[2] // SUB
    tests = groups_of(wide_ref, 0) + groups_of(wide_ref, 1)
    zero = jnp.zeros((SUB, LANES), jnp.float32)
    for k, pair in enumerate(far_loop(tests, [(zero, zero)] * len(tests), messages_ref)):
        for part in range(2):
            sums_ref[k // groups, part, pl.ds(k % groups * SUB, SUB), :] = pair[part]


def second_kernel(half_columns, other, wide_ref, sums_ref, messages_ref, sibling_ref, out_ref):
    row_dev = wide_ref.shape[2]
    which = 0 if other else 1
    tests = groups_of(wide_ref, which)
    near = near_of(half_columns, other, messages_ref, sibling_ref)
    sums = [
        (sums_ref[which, 0, pl.ds(g * SUB, SUB), :], sums_ref[which, 1, pl.ds(g * SUB, SUB), :]) for g in range(len(tests))
    ]
    re, im = rows_of(far_loop(tests, sums, sibling_ref))
    out_ref[0:1, :] = re[:, :row_dev] + near[:, :row_dev]
    out_ref[1:2, :] = im[:, :row_dev] + near[:, row_dev : 2 * row_dev]


def across(x):
    return lax.ppermute(x, ("core", "half"), [(i, 3 - i) for i in range(4)])


def groups_for(xs, half_columns):
    def place(x, core, half, column):
        return ((x * 2 + core) * 2 + half) * half_columns + column

    return [
        [place(x, g ^ (column >= half_columns // 2), half, column) for x in range(xs) for column in range(half_columns)]
        for half in range(2)
        for g in range(2)
    ]


def local(rows, half_columns, test_points, src_points, currents, near_blocks, near_dest, near_tile):
    row_dev = test_points.shape[1]
    width = src_points.shape[1]
    items = near_blocks.shape[0]
    members = rows // 2 * half_columns
    gain = TURNS / math.sqrt(width * members * 4)
    message = (QUAD, 5 * width // QUAD + LANES)
    vmem = pl.BlockSpec(memory_space=pltpu.VMEM)
    hbm = pl.BlockSpec(memory_space=pltpu.HBM)
    params = pltpu.CompilerParams(vmem_limit_bytes=24 << 20)

    partner_points = across(test_points)
    copies = pl.pallas_call(
        functools.partial(pack_kernel, half_columns, gain),
        out_shape=jax.ShapeDtypeStruct((members,) + message, jnp.float32),
        in_specs=[hbm] * 5,
        out_specs=vmem,
        scratch_shapes=[
            pltpu.SMEM((items,), jnp.int32),
            pltpu.SMEM((items,), jnp.int32),
            pltpu.VMEM((3, width), jnp.float32),
            pltpu.VMEM((2, width), jnp.float32),
            pltpu.VMEM(near_blocks.shape, jnp.float32),
            pltpu.VMEM((5 * width // LANES, LANES), jnp.float32),
            pltpu.VMEM((2 * half_columns, LANES), jnp.float32),
            pltpu.SemaphoreType.DMA((5,)),
        ],
        cost_estimate=pl.CostEstimate(flops=1 << 20, bytes_accessed=1 << 20, transcendentals=0),
    )(near_dest.reshape(-1), near_tile.reshape(-1), src_points, currents, near_blocks)
    messages = lax.all_to_all(
        copies, ("x", "core", "half", "column"), split_axis=0, concat_axis=0, tiled=True,
        axis_index_groups=groups_for(rows // 2, half_columns),
    )


    evaluations = width * members * row_dev

    def cost(times):
        return dict(
            compiler_params=params,
            cost_estimate=pl.CostEstimate(
                flops=40 * evaluations * times, bytes_accessed=2 << 20, transcendentals=evaluations * times
            ),
        )

    wide = pl.pallas_call(
        points_kernel,
        out_shape=jax.ShapeDtypeStruct((2, 3, row_dev, LANES), jnp.float32),
        in_specs=[vmem] * 2,
        out_specs=vmem,
        **cost(1),
    )(partner_points, test_points)

    messages, wide = lax.optimization_barrier((messages, wide))
    sibling = lax.ppermute(messages, "core", [(0, 1), (1, 0)])
    sums = pl.pallas_call(
        first_kernel,
        out_shape=jax.ShapeDtypeStruct((2, 2, row_dev, LANES), jnp.float32),
        in_specs=[vmem] * 2,
        out_specs=vmem,
        **cost(2),
    )(wide, messages)

    def second(other):
        return pl.pallas_call(
            functools.partial(second_kernel, half_columns, other),
            out_shape=jax.ShapeDtypeStruct((2, row_dev), jnp.float32),
            in_specs=[vmem] * 4,
            out_specs=vmem,
            **cost(1),
        )(wide, sums, messages, sibling)

    from_partner = across(second(True))
    return second(False) + from_partner


def solution(mesh):
    rows, columns = mesh.shape["row"], mesh.shape["col"]
    finer = jax.sharding.Mesh(mesh.devices.reshape(rows // 2, 2, 2, columns // 2), ("x", "core", "half", "column"))
    every = ("x", "core", "half", "column")
    in_specs = (
        P(None, every),
        P(None, every),
        P(None, every),
        P(every, None, None, None),
        P(every, None),
        P(every, None),
    )
    body = functools.partial(local, rows, columns // 2)
    return jax.shard_map(body, mesh=finer, in_specs=in_specs, out_specs=P(None, every), check_vma=False)
```

```python
import functools
import math

import jax
import jax.numpy as jnp
import numpy as np
from jax import lax
from jax.experimental import pallas as pl
from jax.experimental.pallas import tpu as pltpu
from jax.sharding import PartitionSpec as P

WAVENUMBER = 40.0
SOFTENING = 0.01
TURNS = WAVENUMBER / (2.0 * math.pi)
LANES = 128
SUB = 8
QUAD = 4


def even_fit(function, terms, reach):
    nodes = np.cos((np.arange(400) + 0.5) * np.pi / 400)
    squares = (nodes + 1) * 0.5 * reach * reach
    fit = np.polynomial.chebyshev.Chebyshev.fit(squares, function(np.sqrt(squares)), terms - 1)
    return [float(value) for value in fit.convert(kind=np.polynomial.Polynomial).coef]


ROOT2 = math.sqrt(2.0)
SINE = even_fit(lambda u: ROOT2 * math.pi * np.sinc(u), 4, 0.5)
COSINE = even_fit(lambda u: -ROOT2 * np.cos(np.pi * u), 5, 0.5)
ANGLE = even_fit(lambda r: np.arctan(r) / (2 * np.pi * r), 9, 1.0)
ROUNDER = 1.5 * 2.0**23


def horner(coefficients, x):
    total = coefficients[-1] * x + coefficients[-2]
    for value in coefficients[-3::-1]:
        total = total * x + value
    return total


def phase_of(re, im):
    wide = jnp.abs(re)
    high = jnp.abs(im)
    larger = jnp.maximum(wide, high)
    ratio = jnp.minimum(wide, high) / jnp.where(larger == 0.0, 1.0, larger)
    turn = ratio * horner(ANGLE, ratio * ratio)
    turn = jnp.where(high > wide, 0.25 - turn, turn)
    turn = jnp.where(re < 0.0, 0.5 - turn, turn)
    return jnp.where(im < 0.0, -turn, turn)


def pack_kernel(
    half_columns, gain, dest_hbm, tile_hbm, src_hbm, cur_hbm, blocks_hbm, copies_ref,
    dest_ref, tile_ref, src_ref, cur_ref, blocks_ref, message, near_all, sems
):
    items = blocks_ref.shape[0]
    parts = [pl.ds(part * items // 2, items // 2) for part in range(2)]
    pairs = [(blocks_hbm.at[part], blocks_ref.at[part]) for part in parts]
    pairs += [(cur_hbm, cur_ref), (src_hbm, src_ref), (dest_hbm, dest_ref), (tile_hbm, tile_ref)]
    moves = [pltpu.make_async_copy(source, target, sems.at[k]) for k, (source, target) in enumerate(pairs)]
    for move in moves:
        move.start()
    members = copies_ref.shape[0]
    tiles = src_ref.shape[1] // LANES
    row_dev = blocks_ref.shape[2]
    columns = 2 * half_columns
    lane = lax.broadcasted_iota(jnp.int32, (SUB, LANES), 1)
    sub = lax.broadcasted_iota(jnp.int32, (SUB, LANES), 0)
    moves[2].wait()
    moves[3].wait()

    for tile in range(tiles):
        part = pl.ds(tile * LANES, LANES)
        message[pl.ds(3 * tiles + tile, 2, stride=tiles), :] = cur_ref[:, part]
        message[pl.ds(tile, 3, stride=tiles), :] = src_ref[:, part]
    cr = message[3 * tiles : 4 * tiles, :]
    ci = message[4 * tiles : 5 * tiles, :]
    values = [message[c * tiles : (c + 1) * tiles, :] * TURNS for c in range(3)]
    values += [jnp.sqrt(cr * cr + ci * ci) * gain, phase_of(cr, ci)]
    pieces = [value[part * QUAD : (part + 1) * QUAD] for value in values for part in range(tiles // QUAD)]
    last = len(pieces) * LANES

    def copy(member, _):
        for slot, piece in enumerate(pieces):
            copies_ref[member, :, slot * LANES : (slot + 1) * LANES] = piece
        copies_ref[member, :, last:] = jnp.zeros((QUAD, LANES), jnp.float32)
        return 0

    lax.fori_loop(0, members, copy, 0, unroll=8)

    moves[4].wait()
    moves[5].wait()
    near = [jnp.zeros((SUB, LANES), jnp.float32)] * (columns // SUB)
    for block in range(items):
        if block % (items // 2) == 0:
            moves[block // (items // 2)].wait()
        tile = pl.multiple_of(tile_ref[block] * LANES, LANES)
        cr = cur_ref[0:1, pl.ds(tile, LANES)]
        ci = cur_ref[1:2, pl.ds(tile, LANES)]
        br = blocks_ref[block, 0]
        bi = blocks_ref[block, 1]
        row = jnp.zeros((SUB, LANES), jnp.float32)
        for part, product in enumerate((br * cr - bi * ci, br * ci + bi * cr)):
            total = jnp.sum(product, axis=1, keepdims=True)
            for piece in range(row_dev // SUB):
                spot = lane == sub + (part * row_dev + piece * SUB)
                row = jnp.where(spot, total[piece * SUB : (piece + 1) * SUB], row)
        row = jnp.sum(row, axis=0, keepdims=True)
        for group in range(columns // SUB):
            near[group] = near[group] + jnp.where(sub + group * SUB == dest_ref[block], row, 0.0)
    for group in range(columns // SUB):
        near_all[pl.ds(group * SUB, SUB), :] = near[group]

    base = lax.axis_index("x") * half_columns
    for k in range(half_columns):
        for half in range(2):
            copies_ref[base + k, half : half + 1, last:] = near_all[half * half_columns + k : half * half_columns + k + 1, :]


def points_kernel(partner_ref, tests_ref, wide_ref):
    row_dev = tests_ref.shape[1]
    lane = lax.broadcasted_iota(jnp.int32, (row_dev, LANES), 1)
    sub = lax.broadcasted_iota(jnp.int32, (row_dev, LANES), 0)
    for which, ref in enumerate((partner_ref, tests_ref)):
        points = jnp.concatenate([ref[...], jnp.zeros((3, LANES - row_dev), jnp.float32)], axis=1) * TURNS
        for c in range(3):
            column = jnp.sum(jnp.where(lane == sub, points[c : c + 1, :], 0.0), axis=1, keepdims=True)
            wide_ref[which, c] = jnp.broadcast_to(column, (row_dev, LANES))


def groups_of(wide_ref, which):
    return [[wide_ref[which, c, pl.ds(g * SUB, SUB), :] for c in range(3)] for g in range(wide_ref.shape[2] // SUB)]


def far_loop(tests, sums, messages_ref):
    members = messages_ref.shape[0]
    slots = (messages_ref.shape[2] // LANES - 1) // 5
    soft = (SOFTENING * TURNS) ** 2

    def step(member, sums):
        for slot, row in [(slot, row) for slot in range(slots) for row in range(QUAD)]:
            sx, sy, sz, size, turn = [
                jnp.broadcast_to(
                    messages_ref[member, row : row + 1, (c * slots + slot) * LANES : (c * slots + slot + 1) * LANES], (SUB, LANES)
                )
                for c in range(5)
            ]
            new = []
            for (tx, ty, tz), (re, im) in zip(tests, sums):
                dx = tx - sx
                dy = ty - sy
                dz = tz - sz
                square = dx * dx + dy * dy + (dz * dz + soft)
                inverse = lax.rsqrt(square)
                t = square * inverse - turn
                u = t - ((t + ROUNDER) - ROUNDER)
                u2 = u * u
                s = u * horner(SINE, u2)
                c = horner(COSINE, u2)
                a = inverse * size
                p = a * s
                new.append(((re + a) - p * s, im + p * c))
            sums = tuple(new)
        return sums

    return lax.fori_loop(0, members, step, tuple(sums), unroll=8 // len(tests))


def rows_of(sums):
    row_dev = len(sums) * SUB
    diagonal = lax.broadcasted_iota(jnp.int32, (row_dev, LANES), 1) == lax.broadcasted_iota(jnp.int32, (row_dev, LANES), 0)
    rows = []
    for part in range(2):
        column = jnp.concatenate([jnp.sum(pair[part], axis=1, keepdims=True) for pair in sums], axis=0)
        rows.append(jnp.sum(jnp.where(diagonal, column, 0.0), axis=0, keepdims=True))
    return rows


def near_of(half_columns, other, messages_ref, sibling_ref):
    last = messages_ref.shape[2] - LANES
    base = lax.axis_index("x") * half_columns
    middle = half_columns // 2
    straight = crossed = jnp.zeros((QUAD, LANES), jnp.float32)
    for k in range(half_columns):
        own, sibling = messages_ref[base + k, :, last:], sibling_ref[base + k, :, last:]
        straight = straight + (own if k < middle else sibling)
        crossed = crossed + (sibling if k < middle else own)
    upper = lax.axis_index("column") >= middle
    total = jnp.where(upper, straight, crossed) if other else jnp.where(upper, crossed, straight)
    first = lax.axis_index("half") == (1 if other else 0)
    return jnp.where(first, total[0:1], total[1:2])


def first_kernel(wide_ref, messages_ref, sums_ref):
    groups = wide_ref.shape[2] // SUB
    tests = groups_of(wide_ref, 0) + groups_of(wide_ref, 1)
    zero = jnp.zeros((SUB, LANES), jnp.float32)
    for k, pair in enumerate(far_loop(tests, [(zero, zero)] * len(tests), messages_ref)):
        for part in range(2):
            sums_ref[k // groups, part, pl.ds(k % groups * SUB, SUB), :] = pair[part]


def second_kernel(half_columns, other, wide_ref, sums_ref, messages_ref, sibling_ref, out_ref):
    row_dev = wide_ref.shape[2]
    which = 0 if other else 1
    tests = groups_of(wide_ref, which)
    near = near_of(half_columns, other, messages_ref, sibling_ref)
    sums = [
        (sums_ref[which, 0, pl.ds(g * SUB, SUB), :], sums_ref[which, 1, pl.ds(g * SUB, SUB), :]) for g in range(len(tests))
    ]
    re, im = rows_of(far_loop(tests, sums, sibling_ref))
    out_ref[0:1, :] = re[:, :row_dev] + near[:, :row_dev]
    out_ref[1:2, :] = im[:, :row_dev] + near[:, row_dev : 2 * row_dev]


def across(x):
    return lax.ppermute(x, ("core", "half"), [(i, 3 - i) for i in range(4)])


def groups_for(xs, half_columns):
    def place(x, core, half, column):
        return ((x * 2 + core) * 2 + half) * half_columns + column

    return [
        [place(x, g ^ (column >= half_columns // 2), half, column) for x in range(xs) for column in range(half_columns)]
        for half in range(2)
        for g in range(2)
    ]


def local(rows, half_columns, test_points, src_points, currents, near_blocks, near_dest, near_tile):
    row_dev = test_points.shape[1]
    width = src_points.shape[1]
    items = near_blocks.shape[0]
    members = rows // 2 * half_columns
    gain = TURNS / math.sqrt(width * members * 4)
    message = (QUAD, 5 * width // QUAD + LANES)
    vmem = pl.BlockSpec(memory_space=pltpu.VMEM)
    hbm = pl.BlockSpec(memory_space=pltpu.HBM)
    params = pltpu.CompilerParams(vmem_limit_bytes=24 << 20)

    partner_points = across(test_points)
    copies = pl.pallas_call(
        functools.partial(pack_kernel, half_columns, gain),
        out_shape=jax.ShapeDtypeStruct((members,) + message, jnp.float32),
        in_specs=[hbm] * 5,
        out_specs=vmem,
        scratch_shapes=[
            pltpu.SMEM((items,), jnp.int32),
            pltpu.SMEM((items,), jnp.int32),
            pltpu.VMEM((3, width), jnp.float32),
            pltpu.VMEM((2, width), jnp.float32),
            pltpu.VMEM(near_blocks.shape, jnp.float32),
            pltpu.VMEM((5 * width // LANES, LANES), jnp.float32),
            pltpu.VMEM((2 * half_columns, LANES), jnp.float32),
            pltpu.SemaphoreType.DMA((6,)),
        ],
        cost_estimate=pl.CostEstimate(flops=1 << 20, bytes_accessed=1 << 20, transcendentals=0),
    )(near_dest.reshape(-1), near_tile.reshape(-1), src_points, currents, near_blocks)
    messages = lax.all_to_all(
        copies, ("x", "core", "half", "column"), split_axis=0, concat_axis=0, tiled=True,
        axis_index_groups=groups_for(rows // 2, half_columns),
    )


    evaluations = width * members * row_dev

    def cost(times):
        return dict(
            compiler_params=params,
            cost_estimate=pl.CostEstimate(
                flops=40 * evaluations * times, bytes_accessed=2 << 20, transcendentals=evaluations * times
            ),
        )

    wide = pl.pallas_call(
        points_kernel,
        out_shape=jax.ShapeDtypeStruct((2, 3, row_dev, LANES), jnp.float32),
        in_specs=[vmem] * 2,
        out_specs=vmem,
        **cost(1),
    )(partner_points, test_points)

    messages, wide = lax.optimization_barrier((messages, wide))
    sibling = lax.ppermute(messages, "core", [(0, 1), (1, 0)])
    sums = pl.pallas_call(
        first_kernel,
        out_shape=jax.ShapeDtypeStruct((2, 2, row_dev, LANES), jnp.float32),
        in_specs=[vmem] * 2,
        out_specs=vmem,
        **cost(2),
    )(wide, messages)

    def second(other):
        return pl.pallas_call(
            functools.partial(second_kernel, half_columns, other),
            out_shape=jax.ShapeDtypeStruct((2, row_dev), jnp.float32),
            in_specs=[vmem] * 4,
            out_specs=vmem,
            **cost(1),
        )(wide, sums, messages, sibling)

    from_partner = across(second(True))
    return second(False) + from_partner


def solution(mesh):
    rows, columns = mesh.shape["row"], mesh.shape["col"]
    finer = jax.sharding.Mesh(mesh.devices.reshape(rows // 2, 2, 2, columns // 2), ("x", "core", "half", "column"))
    every = ("x", "core", "half", "column")
    in_specs = (
        P(None, every),
        P(None, every),
        P(None, every),
        P(every, None, None, None),
        P(every, None),
        P(every, None),
    )
    body = functools.partial(local, rows, columns // 2)
    return jax.shard_map(body, mesh=finer, in_specs=in_specs, out_specs=P(None, every), check_vma=False)
```

```python
import functools
import math

import jax
import jax.numpy as jnp
import numpy as np
from jax import lax
from jax.experimental import pallas as pl
from jax.experimental.pallas import tpu as pltpu
from jax.sharding import PartitionSpec as P

WAVENUMBER = 40.0
SOFTENING = 0.01
TURNS = WAVENUMBER / (2.0 * math.pi)
LANES = 128
SUB = 8
QUAD = 4


def even_fit(function, terms, reach):
    nodes = np.cos((np.arange(400) + 0.5) * np.pi / 400)
    squares = (nodes + 1) * 0.5 * reach * reach
    fit = np.polynomial.chebyshev.Chebyshev.fit(squares, function(np.sqrt(squares)), terms - 1)
    return [float(value) for value in fit.convert(kind=np.polynomial.Polynomial).coef]


ROOT2 = math.sqrt(2.0)
SINE = even_fit(lambda u: ROOT2 * math.pi * np.sinc(u), 4, 0.5)
COSINE = even_fit(lambda u: -ROOT2 * np.cos(np.pi * u), 5, 0.5)
ANGLE = even_fit(lambda r: np.arctan(r) / (2 * np.pi * r), 9, 1.0)
ROUNDER = 1.5 * 2.0**23


def horner(coefficients, x):
    total = coefficients[-1] * x + coefficients[-2]
    for value in coefficients[-3::-1]:
        total = total * x + value
    return total


def phase_of(re, im):
    wide = jnp.abs(re)
    high = jnp.abs(im)
    larger = jnp.maximum(wide, high)
    ratio = jnp.minimum(wide, high) / jnp.where(larger == 0.0, 1.0, larger)
    turn = ratio * horner(ANGLE, ratio * ratio)
    turn = jnp.where(high > wide, 0.25 - turn, turn)
    turn = jnp.where(re < 0.0, 0.5 - turn, turn)
    return jnp.where(im < 0.0, -turn, turn)


def pack_kernel(
    half_columns, gain, dest_hbm, tile_hbm, src_hbm, cur_hbm, blocks_hbm, copies_ref,
    dest_ref, tile_ref, src_ref, cur_ref, blocks_ref, message, near_all, sems
):
    moves = [
        pltpu.make_async_copy(source, target, sems.at[k])
        for k, (source, target) in enumerate((
            (src_hbm, src_ref), (cur_hbm, cur_ref), (blocks_hbm, blocks_ref), (dest_hbm, dest_ref), (tile_hbm, tile_ref)
        ))
    ]
    for move in moves:
        move.start()
    members = copies_ref.shape[0]
    tiles = src_ref.shape[1] // LANES
    items, _, row_dev, _ = blocks_ref.shape
    columns = 2 * half_columns
    lane = lax.broadcasted_iota(jnp.int32, (SUB, LANES), 1)
    sub = lax.broadcasted_iota(jnp.int32, (SUB, LANES), 0)
    moves[0].wait()
    moves[1].wait()

    for tile in range(tiles):
        part = pl.ds(tile * LANES, LANES)
        message[pl.ds(3 * tiles + tile, 2, stride=tiles), :] = cur_ref[:, part]
        message[pl.ds(tile, 3, stride=tiles), :] = src_ref[:, part]
    cr = message[3 * tiles : 4 * tiles, :]
    ci = message[4 * tiles : 5 * tiles, :]
    values = [message[c * tiles : (c + 1) * tiles, :] * TURNS for c in range(3)]
    values += [jnp.sqrt(cr * cr + ci * ci) * gain, phase_of(cr, ci)]
    pieces = [value[part * QUAD : (part + 1) * QUAD] for value in values for part in range(tiles // QUAD)]
    last = len(pieces) * LANES

    def copy(member, _):
        for slot, piece in enumerate(pieces):
            copies_ref[member, :, slot * LANES : (slot + 1) * LANES] = piece
        copies_ref[member, :, last:] = jnp.zeros((QUAD, LANES), jnp.float32)
        return 0

    lax.fori_loop(0, members, copy, 0, unroll=8)

    for move in moves[2:]:
        move.wait()
    near = [jnp.zeros((SUB, LANES), jnp.float32)] * (columns // SUB)
    for block in range(items):
        tile = pl.multiple_of(tile_ref[block] * LANES, LANES)
        cr = cur_ref[0:1, pl.ds(tile, LANES)]
        ci = cur_ref[1:2, pl.ds(tile, LANES)]
        br = blocks_ref[block, 0]
        bi = blocks_ref[block, 1]
        row = jnp.zeros((SUB, LANES), jnp.float32)
        for part, product in enumerate((br * cr - bi * ci, br * ci + bi * cr)):
            total = jnp.sum(product, axis=1, keepdims=True)
            for piece in range(row_dev // SUB):
                spot = lane == sub + (part * row_dev + piece * SUB)
                row = jnp.where(spot, total[piece * SUB : (piece + 1) * SUB], row)
        row = jnp.sum(row, axis=0, keepdims=True)
        for group in range(columns // SUB):
            near[group] = near[group] + jnp.where(sub + group * SUB == dest_ref[block], row, 0.0)
    for group in range(columns // SUB):
        near_all[pl.ds(group * SUB, SUB), :] = near[group]

    base = lax.axis_index("x") * half_columns
    for k in range(half_columns):
        for half in range(2):
            copies_ref[base + k, half : half + 1, last:] = near_all[half * half_columns + k : half * half_columns + k + 1, :]


def points_kernel(partner_ref, tests_ref, wide_ref):
    row_dev = tests_ref.shape[1]
    lane = lax.broadcasted_iota(jnp.int32, (row_dev, LANES), 1)
    sub = lax.broadcasted_iota(jnp.int32, (row_dev, LANES), 0)
    for which, ref in enumerate((partner_ref, tests_ref)):
        points = jnp.concatenate([ref[...], jnp.zeros((3, LANES - row_dev), jnp.float32)], axis=1) * TURNS
        for c in range(3):
            column = jnp.sum(jnp.where(lane == sub, points[c : c + 1, :], 0.0), axis=1, keepdims=True)
            wide_ref[which, c] = jnp.broadcast_to(column, (row_dev, LANES))


def groups_of(wide_ref, which):
    return [[wide_ref[which, c, pl.ds(g * SUB, SUB), :] for c in range(3)] for g in range(wide_ref.shape[2] // SUB)]


def far_loop(tests, sums, messages_ref):
    members = messages_ref.shape[0]
    slots = (messages_ref.shape[2] // LANES - 1) // 5
    soft = (SOFTENING * TURNS) ** 2

    def step(member, sums):
        for slot, row in [(slot, row) for slot in range(slots) for row in range(QUAD)]:
            sx, sy, sz, size, turn = [
                jnp.broadcast_to(
                    messages_ref[member, row : row + 1, (c * slots + slot) * LANES : (c * slots + slot + 1) * LANES], (SUB, LANES)
                )
                for c in range(5)
            ]
            new = []
            for (tx, ty, tz), (re, im) in zip(tests, sums):
                dx = tx - sx
                dy = ty - sy
                dz = tz - sz
                square = dx * dx + dy * dy + (dz * dz + soft)
                inverse = lax.rsqrt(square)
                t = square * inverse - turn
                u = t - ((t + ROUNDER) - ROUNDER)
                u2 = u * u
                s = u * horner(SINE, u2)
                c = horner(COSINE, u2)
                a = inverse * size
                p = a * s
                new.append(((re + a) - p * s, im + p * c))
            sums = tuple(new)
        return sums

    return lax.fori_loop(0, members, step, tuple(sums), unroll=8 // len(tests))


def rows_of(sums):
    row_dev = len(sums) * SUB
    diagonal = lax.broadcasted_iota(jnp.int32, (row_dev, LANES), 1) == lax.broadcasted_iota(jnp.int32, (row_dev, LANES), 0)
    rows = []
    for part in range(2):
        column = jnp.concatenate([jnp.sum(pair[part], axis=1, keepdims=True) for pair in sums], axis=0)
        rows.append(jnp.sum(jnp.where(diagonal, column, 0.0), axis=0, keepdims=True))
    return rows


def side_of(column, half_columns):
    return (column // (half_columns // 2) + column % 2) % 2


def near_of(half_columns, other, messages_ref, sibling_ref):
    last = messages_ref.shape[2] - LANES
    base = lax.axis_index("x") * half_columns
    middle = half_columns // 2
    straight = crossed = jnp.zeros((QUAD, LANES), jnp.float32)
    for k in range(half_columns):
        own, sibling = messages_ref[base + k, :, last:], sibling_ref[base + k, :, last:]
        side = side_of(k, half_columns)
        straight = straight + (sibling if side else own)
        crossed = crossed + (own if side else sibling)
    column = lax.axis_index("column")
    upper = (column // middle + column % 2) % 2 == 1
    total = jnp.where(upper, straight, crossed) if other else jnp.where(upper, crossed, straight)
    first = lax.axis_index("half") == (1 if other else 0)
    return jnp.where(first, total[0:1], total[1:2])


def first_kernel(wide_ref, messages_ref, sums_ref):
    groups = wide_ref.shape[2] // SUB
    tests = groups_of(wide_ref, 0) + groups_of(wide_ref, 1)
    zero = jnp.zeros((SUB, LANES), jnp.float32)
    for k, pair in enumerate(far_loop(tests, [(zero, zero)] * len(tests), messages_ref)):
        for part in range(2):
            sums_ref[k // groups, part, pl.ds(k % groups * SUB, SUB), :] = pair[part]


def second_kernel(half_columns, other, wide_ref, sums_ref, messages_ref, sibling_ref, out_ref):
    row_dev = wide_ref.shape[2]
    which = 0 if other else 1
    tests = groups_of(wide_ref, which)
    near = near_of(half_columns, other, messages_ref, sibling_ref)
    sums = [
        (sums_ref[which, 0, pl.ds(g * SUB, SUB), :], sums_ref[which, 1, pl.ds(g * SUB, SUB), :]) for g in range(len(tests))
    ]
    re, im = rows_of(far_loop(tests, sums, sibling_ref))
    out_ref[0:1, :] = re[:, :row_dev] + near[:, :row_dev]
    out_ref[1:2, :] = im[:, :row_dev] + near[:, row_dev : 2 * row_dev]


def across(x):
    return lax.ppermute(x, ("core", "half"), [(i, 3 - i) for i in range(4)])


def groups_for(xs, half_columns):
    def place(x, core, half, column):
        return ((x * 2 + core) * 2 + half) * half_columns + column

    return [
        [place(x, g ^ side_of(column, half_columns), half, column) for x in range(xs) for column in range(half_columns)]
        for half in range(2)
        for g in range(2)
    ]


def local(rows, half_columns, test_points, src_points, currents, near_blocks, near_dest, near_tile):
    row_dev = test_points.shape[1]
    width = src_points.shape[1]
    items = near_blocks.shape[0]
    members = rows // 2 * half_columns
    gain = TURNS / math.sqrt(width * members * 4)
    message = (QUAD, 5 * width // QUAD + LANES)
    vmem = pl.BlockSpec(memory_space=pltpu.VMEM)
    hbm = pl.BlockSpec(memory_space=pltpu.HBM)
    params = pltpu.CompilerParams(vmem_limit_bytes=24 << 20)

    partner_points = across(test_points)
    copies = pl.pallas_call(
        functools.partial(pack_kernel, half_columns, gain),
        out_shape=jax.ShapeDtypeStruct((members,) + message, jnp.float32),
        in_specs=[hbm] * 5,
        out_specs=vmem,
        scratch_shapes=[
            pltpu.SMEM((items,), jnp.int32),
            pltpu.SMEM((items,), jnp.int32),
            pltpu.VMEM((3, width), jnp.float32),
            pltpu.VMEM((2, width), jnp.float32),
            pltpu.VMEM(near_blocks.shape, jnp.float32),
            pltpu.VMEM((5 * width // LANES, LANES), jnp.float32),
            pltpu.VMEM((2 * half_columns, LANES), jnp.float32),
            pltpu.SemaphoreType.DMA((5,)),
        ],
        cost_estimate=pl.CostEstimate(flops=1 << 20, bytes_accessed=1 << 20, transcendentals=0),
    )(near_dest.reshape(-1), near_tile.reshape(-1), src_points, currents, near_blocks)
    messages = lax.all_to_all(
        copies, ("x", "core", "half", "column"), split_axis=0, concat_axis=0, tiled=True,
        axis_index_groups=groups_for(rows // 2, half_columns),
    )


    evaluations = width * members * row_dev

    def cost(times):
        return dict(
            compiler_params=params,
            cost_estimate=pl.CostEstimate(
                flops=40 * evaluations * times, bytes_accessed=2 << 20, transcendentals=evaluations * times
            ),
        )

    wide = pl.pallas_call(
        points_kernel,
        out_shape=jax.ShapeDtypeStruct((2, 3, row_dev, LANES), jnp.float32),
        in_specs=[vmem] * 2,
        out_specs=vmem,
        **cost(1),
    )(partner_points, test_points)

    messages, wide = lax.optimization_barrier((messages, wide))
    sibling = lax.ppermute(messages, "core", [(0, 1), (1, 0)])
    sums = pl.pallas_call(
        first_kernel,
        out_shape=jax.ShapeDtypeStruct((2, 2, row_dev, LANES), jnp.float32),
        in_specs=[vmem] * 2,
        out_specs=vmem,
        **cost(2),
    )(wide, messages)

    def second(other):
        return pl.pallas_call(
            functools.partial(second_kernel, half_columns, other),
            out_shape=jax.ShapeDtypeStruct((2, row_dev), jnp.float32),
            in_specs=[vmem] * 4,
            out_specs=vmem,
            **cost(1),
        )(wide, sums, messages, sibling)

    from_partner = across(second(True))
    return second(False) + from_partner


def solution(mesh):
    rows, columns = mesh.shape["row"], mesh.shape["col"]
    finer = jax.sharding.Mesh(mesh.devices.reshape(rows // 2, 2, 2, columns // 2), ("x", "core", "half", "column"))
    every = ("x", "core", "half", "column")
    in_specs = (
        P(None, every),
        P(None, every),
        P(None, every),
        P(every, None, None, None),
        P(every, None),
        P(every, None),
    )
    body = functools.partial(local, rows, columns // 2)
    return jax.shard_map(body, mesh=finer, in_specs=in_specs, out_specs=P(None, every), check_vma=False)
```

```python
import functools
import math

import jax
import jax.numpy as jnp
import numpy as np
from jax import lax
from jax.experimental import pallas as pl
from jax.experimental.pallas import tpu as pltpu
from jax.sharding import PartitionSpec as P

WAVENUMBER = 40.0
SOFTENING = 0.01
TURNS = WAVENUMBER / (2.0 * math.pi)
LANES = 128
SUB = 8
QUAD = 4


def even_fit(function, terms, reach):
    nodes = np.cos((np.arange(400) + 0.5) * np.pi / 400)
    squares = (nodes + 1) * 0.5 * reach * reach
    fit = np.polynomial.chebyshev.Chebyshev.fit(squares, function(np.sqrt(squares)), terms - 1)
    return [float(value) for value in fit.convert(kind=np.polynomial.Polynomial).coef]


ROOT2 = math.sqrt(2.0)
SINE = even_fit(lambda u: ROOT2 * math.pi * np.sinc(u), 4, 0.5)
COSINE = even_fit(lambda u: -ROOT2 * np.cos(np.pi * u), 5, 0.5)
ANGLE = even_fit(lambda r: np.arctan(r) / (2 * np.pi * r), 9, 1.0)
ROUNDER = 1.5 * 2.0**23


def horner(coefficients, x):
    total = coefficients[-1] * x + coefficients[-2]
    for value in coefficients[-3::-1]:
        total = total * x + value
    return total


def phase_of(re, im):
    wide = jnp.abs(re)
    high = jnp.abs(im)
    larger = jnp.maximum(wide, high)
    ratio = jnp.minimum(wide, high) / jnp.where(larger == 0.0, 1.0, larger)
    turn = ratio * horner(ANGLE, ratio * ratio)
    turn = jnp.where(high > wide, 0.25 - turn, turn)
    turn = jnp.where(re < 0.0, 0.5 - turn, turn)
    return jnp.where(im < 0.0, -turn, turn)


def pack_kernel(
    half_columns, gain, dest_hbm, tile_hbm, src_hbm, cur_hbm, blocks_hbm, copies_ref,
    dest_ref, tile_ref, src_ref, cur_ref, blocks_ref, message, near_all, sems
):
    moves = [
        pltpu.make_async_copy(source, target, sems.at[k])
        for k, (source, target) in enumerate((
            (src_hbm, src_ref), (cur_hbm, cur_ref), (blocks_hbm, blocks_ref), (dest_hbm, dest_ref), (tile_hbm, tile_ref)
        ))
    ]
    for move in moves:
        move.start()
    members = copies_ref.shape[0]
    tiles = src_ref.shape[1] // LANES
    items, _, row_dev, _ = blocks_ref.shape
    columns = 2 * half_columns
    lane = lax.broadcasted_iota(jnp.int32, (SUB, LANES), 1)
    sub = lax.broadcasted_iota(jnp.int32, (SUB, LANES), 0)
    moves[0].wait()
    moves[1].wait()

    for tile in range(tiles):
        part = pl.ds(tile * LANES, LANES)
        message[pl.ds(3 * tiles + tile, 2, stride=tiles), :] = cur_ref[:, part]
        message[pl.ds(tile, 3, stride=tiles), :] = src_ref[:, part]
    cr = message[3 * tiles : 4 * tiles, :]
    ci = message[4 * tiles : 5 * tiles, :]
    values = [message[c * tiles : (c + 1) * tiles, :] * TURNS for c in range(3)]
    values += [jnp.sqrt(cr * cr + ci * ci) * gain, phase_of(cr, ci)]
    pieces = [value[part * QUAD : (part + 1) * QUAD] for value in values for part in range(tiles // QUAD)]
    last = len(pieces) * LANES

    def copy(member, _):
        for slot, piece in enumerate(pieces):
            copies_ref[member, :, slot * LANES : (slot + 1) * LANES] = piece
        copies_ref[member, :, last:] = jnp.zeros((QUAD, LANES), jnp.float32)
        return 0

    lax.fori_loop(0, members, copy, 0, unroll=8)

    for move in moves[2:]:
        move.wait()
    near = [jnp.zeros((SUB, LANES), jnp.float32)] * (columns // SUB)
    for block in range(items):
        tile = pl.multiple_of(tile_ref[block] * LANES, LANES)
        cr = cur_ref[0:1, pl.ds(tile, LANES)]
        ci = cur_ref[1:2, pl.ds(tile, LANES)]
        br = blocks_ref[block, 0]
        bi = blocks_ref[block, 1]
        row = jnp.zeros((SUB, LANES), jnp.float32)
        for part, product in enumerate((br * cr - bi * ci, br * ci + bi * cr)):
            total = jnp.sum(product, axis=1, keepdims=True)
            for piece in range(row_dev // SUB):
                spot = lane == sub + (part * row_dev + piece * SUB)
                row = jnp.where(spot, total[piece * SUB : (piece + 1) * SUB], row)
        row = jnp.sum(row, axis=0, keepdims=True)
        for group in range(columns // SUB):
            near[group] = near[group] + jnp.where(sub + group * SUB == dest_ref[block], row, 0.0)
    for group in range(columns // SUB):
        near_all[pl.ds(group * SUB, SUB), :] = near[group]

    base = lax.axis_index("x") * half_columns
    for k in range(half_columns):
        for half in range(2):
            copies_ref[base + k, half : half + 1, last:] = near_all[half * half_columns + k : half * half_columns + k + 1, :]


def points_kernel(partner_ref, tests_ref, wide_ref):
    row_dev = tests_ref.shape[1]
    lane = lax.broadcasted_iota(jnp.int32, (row_dev, LANES), 1)
    sub = lax.broadcasted_iota(jnp.int32, (row_dev, LANES), 0)
    for which, ref in enumerate((partner_ref, tests_ref)):
        points = jnp.concatenate([ref[...], jnp.zeros((3, LANES - row_dev), jnp.float32)], axis=1) * TURNS
        for c in range(3):
            column = jnp.sum(jnp.where(lane == sub, points[c : c + 1, :], 0.0), axis=1, keepdims=True)
            wide_ref[which, c] = jnp.broadcast_to(column, (row_dev, LANES))


def groups_of(wide_ref, which):
    return [[wide_ref[which, c, pl.ds(g * SUB, SUB), :] for c in range(3)] for g in range(wide_ref.shape[2] // SUB)]


def far_loop(tests, sums, messages_ref):
    members = messages_ref.shape[0]
    slots = (messages_ref.shape[2] // LANES - 1) // 5
    soft = (SOFTENING * TURNS) ** 2

    def step(member, sums):
        for slot, row in [(slot, row) for slot in range(slots) for row in range(QUAD)]:
            sx, sy, sz, size, turn = [
                jnp.broadcast_to(
                    messages_ref[member, row : row + 1, (c * slots + slot) * LANES : (c * slots + slot + 1) * LANES], (SUB, LANES)
                )
                for c in range(5)
            ]
            new = []
            for (tx, ty, tz), (re, im) in zip(tests, sums):
                dx = tx - sx
                dy = ty - sy
                dz = tz - sz
                square = dx * dx + dy * dy + (dz * dz + soft)
                inverse = lax.rsqrt(square)
                t = square * inverse - turn
                u = t - ((t + ROUNDER) - ROUNDER)
                u2 = u * u
                s = u * horner(SINE, u2)
                c = horner(COSINE, u2)
                a = inverse * size
                p = a * s
                new.append(((re + a) - p * s, im + p * c))
            sums = tuple(new)
        return sums

    return lax.fori_loop(0, members, step, tuple(sums), unroll=8 // len(tests))


def rows_of(sums):
    row_dev = len(sums) * SUB
    diagonal = lax.broadcasted_iota(jnp.int32, (row_dev, LANES), 1) == lax.broadcasted_iota(jnp.int32, (row_dev, LANES), 0)
    rows = []
    for part in range(2):
        column = jnp.concatenate([jnp.sum(pair[part], axis=1, keepdims=True) for pair in sums], axis=0)
        rows.append(jnp.sum(jnp.where(diagonal, column, 0.0), axis=0, keepdims=True))
    return rows


def side_of(column):
    return column % 2


def near_of(half_columns, other, messages_ref, sibling_ref):
    last = messages_ref.shape[2] - LANES
    base = lax.axis_index("x") * half_columns
    straight = crossed = jnp.zeros((QUAD, LANES), jnp.float32)
    for k in range(half_columns):
        own, sibling = messages_ref[base + k, :, last:], sibling_ref[base + k, :, last:]
        side = side_of(k)
        straight = straight + (sibling if side else own)
        crossed = crossed + (own if side else sibling)
    upper = side_of(lax.axis_index("column")) == 1
    total = jnp.where(upper, straight, crossed) if other else jnp.where(upper, crossed, straight)
    first = lax.axis_index("half") == (1 if other else 0)
    return jnp.where(first, total[0:1], total[1:2])


def first_kernel(wide_ref, messages_ref, sums_ref):
    groups = wide_ref.shape[2] // SUB
    tests = groups_of(wide_ref, 0) + groups_of(wide_ref, 1)
    zero = jnp.zeros((SUB, LANES), jnp.float32)
    for k, pair in enumerate(far_loop(tests, [(zero, zero)] * len(tests), messages_ref)):
        for part in range(2):
            sums_ref[k // groups, part, pl.ds(k % groups * SUB, SUB), :] = pair[part]


def second_kernel(half_columns, other, wide_ref, sums_ref, messages_ref, sibling_ref, out_ref):
    row_dev = wide_ref.shape[2]
    which = 0 if other else 1
    tests = groups_of(wide_ref, which)
    near = near_of(half_columns, other, messages_ref, sibling_ref)
    sums = [
        (sums_ref[which, 0, pl.ds(g * SUB, SUB), :], sums_ref[which, 1, pl.ds(g * SUB, SUB), :]) for g in range(len(tests))
    ]
    re, im = rows_of(far_loop(tests, sums, sibling_ref))
    out_ref[0:1, :] = re[:, :row_dev] + near[:, :row_dev]
    out_ref[1:2, :] = im[:, :row_dev] + near[:, row_dev : 2 * row_dev]


def across(x):
    return lax.ppermute(x, ("core", "half"), [(i, 3 - i) for i in range(4)])


def groups_for(xs, half_columns):
    def place(x, core, half, column):
        return ((x * 2 + core) * 2 + half) * half_columns + column

    return [
        [place(x, g ^ side_of(column), half, column) for x in range(xs) for column in range(half_columns)]
        for half in range(2)
        for g in range(2)
    ]


def local(rows, half_columns, test_points, src_points, currents, near_blocks, near_dest, near_tile):
    row_dev = test_points.shape[1]
    width = src_points.shape[1]
    items = near_blocks.shape[0]
    members = rows // 2 * half_columns
    gain = TURNS / math.sqrt(width * members * 4)
    message = (QUAD, 5 * width // QUAD + LANES)
    vmem = pl.BlockSpec(memory_space=pltpu.VMEM)
    hbm = pl.BlockSpec(memory_space=pltpu.HBM)
    params = pltpu.CompilerParams(vmem_limit_bytes=24 << 20)

    partner_points = across(test_points)
    copies = pl.pallas_call(
        functools.partial(pack_kernel, half_columns, gain),
        out_shape=jax.ShapeDtypeStruct((members,) + message, jnp.float32),
        in_specs=[hbm] * 5,
        out_specs=vmem,
        scratch_shapes=[
            pltpu.SMEM((items,), jnp.int32),
            pltpu.SMEM((items,), jnp.int32),
            pltpu.VMEM((3, width), jnp.float32),
            pltpu.VMEM((2, width), jnp.float32),
            pltpu.VMEM(near_blocks.shape, jnp.float32),
            pltpu.VMEM((5 * width // LANES, LANES), jnp.float32),
            pltpu.VMEM((2 * half_columns, LANES), jnp.float32),
            pltpu.SemaphoreType.DMA((5,)),
        ],
        cost_estimate=pl.CostEstimate(flops=1 << 20, bytes_accessed=1 << 20, transcendentals=0),
    )(near_dest.reshape(-1), near_tile.reshape(-1), src_points, currents, near_blocks)
    messages = lax.all_to_all(
        copies, ("x", "core", "half", "column"), split_axis=0, concat_axis=0, tiled=True,
        axis_index_groups=groups_for(rows // 2, half_columns),
    )


    evaluations = width * members * row_dev

    def cost(times):
        return dict(
            compiler_params=params,
            cost_estimate=pl.CostEstimate(
                flops=40 * evaluations * times, bytes_accessed=2 << 20, transcendentals=evaluations * times
            ),
        )

    wide = pl.pallas_call(
        points_kernel,
        out_shape=jax.ShapeDtypeStruct((2, 3, row_dev, LANES), jnp.float32),
        in_specs=[vmem] * 2,
        out_specs=vmem,
        **cost(1),
    )(partner_points, test_points)

    messages, wide = lax.optimization_barrier((messages, wide))
    sibling = lax.ppermute(messages, "core", [(0, 1), (1, 0)])
    sums = pl.pallas_call(
        first_kernel,
        out_shape=jax.ShapeDtypeStruct((2, 2, row_dev, LANES), jnp.float32),
        in_specs=[vmem] * 2,
        out_specs=vmem,
        **cost(2),
    )(wide, messages)

    def second(other):
        return pl.pallas_call(
            functools.partial(second_kernel, half_columns, other),
            out_shape=jax.ShapeDtypeStruct((2, row_dev), jnp.float32),
            in_specs=[vmem] * 4,
            out_specs=vmem,
            **cost(1),
        )(wide, sums, messages, sibling)

    from_partner = across(second(True))
    return second(False) + from_partner


def solution(mesh):
    rows, columns = mesh.shape["row"], mesh.shape["col"]
    finer = jax.sharding.Mesh(mesh.devices.reshape(rows // 2, 2, 2, columns // 2), ("x", "core", "half", "column"))
    every = ("x", "core", "half", "column")
    in_specs = (
        P(None, every),
        P(None, every),
        P(None, every),
        P(every, None, None, None),
        P(every, None),
        P(every, None),
    )
    body = functools.partial(local, rows, columns // 2)
    return jax.shard_map(body, mesh=finer, in_specs=in_specs, out_specs=P(None, every), check_vma=False)
```

```python
import functools
import math

import jax
import jax.numpy as jnp
import numpy as np
from jax import lax
from jax.experimental import pallas as pl
from jax.experimental.pallas import tpu as pltpu
from jax.sharding import PartitionSpec as P

WAVENUMBER = 40.0
SOFTENING = 0.01
TURNS = WAVENUMBER / (2.0 * math.pi)
LANES = 128
SUB = 8
QUAD = 4


def even_fit(function, terms, reach):
    nodes = np.cos((np.arange(400) + 0.5) * np.pi / 400)
    squares = (nodes + 1) * 0.5 * reach * reach
    fit = np.polynomial.chebyshev.Chebyshev.fit(squares, function(np.sqrt(squares)), terms - 1)
    return [float(value) for value in fit.convert(kind=np.polynomial.Polynomial).coef]


ROOT2 = math.sqrt(2.0)
SINE = even_fit(lambda u: ROOT2 * math.pi * np.sinc(u), 4, 0.5)
COSINE = even_fit(lambda u: -ROOT2 * np.cos(np.pi * u), 5, 0.5)
ANGLE = even_fit(lambda r: np.arctan(r) / (2 * np.pi * r), 9, 1.0)
ROUNDER = 1.5 * 2.0**23


def horner(coefficients, x):
    total = coefficients[-1] * x + coefficients[-2]
    for value in coefficients[-3::-1]:
        total = total * x + value
    return total


def phase_of(re, im):
    wide = jnp.abs(re)
    high = jnp.abs(im)
    larger = jnp.maximum(wide, high)
    ratio = jnp.minimum(wide, high) / jnp.where(larger == 0.0, 1.0, larger)
    turn = ratio * horner(ANGLE, ratio * ratio)
    turn = jnp.where(high > wide, 0.25 - turn, turn)
    turn = jnp.where(re < 0.0, 0.5 - turn, turn)
    return jnp.where(im < 0.0, -turn, turn)


def pack_kernel(
    half_columns, gain, dest_hbm, tile_hbm, src_hbm, cur_hbm, blocks_hbm, copies_ref,
    dest_ref, tile_ref, src_ref, cur_ref, blocks_ref, message, near_all, sems
):
    moves = [
        pltpu.make_async_copy(source, target, sems.at[k])
        for k, (source, target) in enumerate((
            (src_hbm, src_ref), (cur_hbm, cur_ref), (blocks_hbm, blocks_ref), (dest_hbm, dest_ref), (tile_hbm, tile_ref)
        ))
    ]
    for move in moves:
        move.start()
    members = copies_ref.shape[0]
    tiles = src_ref.shape[1] // LANES
    items, _, row_dev, _ = blocks_ref.shape
    columns = 2 * half_columns
    lane = lax.broadcasted_iota(jnp.int32, (SUB, LANES), 1)
    sub = lax.broadcasted_iota(jnp.int32, (SUB, LANES), 0)
    moves[0].wait()
    moves[1].wait()

    for tile in range(tiles):
        part = pl.ds(tile * LANES, LANES)
        message[pl.ds(3 * tiles + tile, 2, stride=tiles), :] = cur_ref[:, part]
        message[pl.ds(tile, 3, stride=tiles), :] = src_ref[:, part]
    cr = message[3 * tiles : 4 * tiles, :]
    ci = message[4 * tiles : 5 * tiles, :]
    values = [message[c * tiles : (c + 1) * tiles, :] * TURNS for c in range(3)]
    values += [jnp.sqrt(cr * cr + ci * ci) * gain, phase_of(cr, ci)]
    pieces = [value[part * QUAD : (part + 1) * QUAD] for value in values for part in range(tiles // QUAD)]
    last = len(pieces) * LANES

    def copy(member, _):
        for slot, piece in enumerate(pieces):
            copies_ref[member, :, slot * LANES : (slot + 1) * LANES] = piece
        copies_ref[member, :, last:] = jnp.zeros((QUAD, LANES), jnp.float32)
        return 0

    lax.fori_loop(0, members, copy, 0, unroll=8)

    for move in moves[2:]:
        move.wait()
    near = [jnp.zeros((SUB, LANES), jnp.float32)] * (columns // SUB)
    for block in range(items):
        tile = pl.multiple_of(tile_ref[block] * LANES, LANES)
        cr = cur_ref[0:1, pl.ds(tile, LANES)]
        ci = cur_ref[1:2, pl.ds(tile, LANES)]
        br = blocks_ref[block, 0]
        bi = blocks_ref[block, 1]
        row = jnp.zeros((SUB, LANES), jnp.float32)
        for part, product in enumerate((br * cr - bi * ci, br * ci + bi * cr)):
            total = jnp.sum(product, axis=1, keepdims=True)
            for piece in range(row_dev // SUB):
                spot = lane == sub + (part * row_dev + piece * SUB)
                row = jnp.where(spot, total[piece * SUB : (piece + 1) * SUB], row)
        row = jnp.sum(row, axis=0, keepdims=True)
        for group in range(columns // SUB):
            near[group] = near[group] + jnp.where(sub + group * SUB == dest_ref[block], row, 0.0)
    for group in range(columns // SUB):
        near_all[pl.ds(group * SUB, SUB), :] = near[group]

    xs = members // half_columns
    for k in range(half_columns):
        for half in range(2):
            copies_ref[k * xs + lax.axis_index("x"), half : half + 1, last:] = near_all[half * half_columns + k : half * half_columns + k + 1, :]


def points_kernel(partner_ref, tests_ref, wide_ref):
    row_dev = tests_ref.shape[1]
    lane = lax.broadcasted_iota(jnp.int32, (row_dev, LANES), 1)
    sub = lax.broadcasted_iota(jnp.int32, (row_dev, LANES), 0)
    for which, ref in enumerate((partner_ref, tests_ref)):
        points = jnp.concatenate([ref[...], jnp.zeros((3, LANES - row_dev), jnp.float32)], axis=1) * TURNS
        for c in range(3):
            column = jnp.sum(jnp.where(lane == sub, points[c : c + 1, :], 0.0), axis=1, keepdims=True)
            wide_ref[which, c] = jnp.broadcast_to(column, (row_dev, LANES))


def groups_of(wide_ref, which):
    return [[wide_ref[which, c, pl.ds(g * SUB, SUB), :] for c in range(3)] for g in range(wide_ref.shape[2] // SUB)]


def far_loop(tests, sums, messages_ref):
    members = messages_ref.shape[0]
    slots = (messages_ref.shape[2] // LANES - 1) // 5
    soft = (SOFTENING * TURNS) ** 2

    def step(member, sums):
        for slot, row in [(slot, row) for slot in range(slots) for row in range(QUAD)]:
            sx, sy, sz, size, turn = [
                jnp.broadcast_to(
                    messages_ref[member, row : row + 1, (c * slots + slot) * LANES : (c * slots + slot + 1) * LANES], (SUB, LANES)
                )
                for c in range(5)
            ]
            new = []
            for (tx, ty, tz), (re, im) in zip(tests, sums):
                dx = tx - sx
                dy = ty - sy
                dz = tz - sz
                square = dx * dx + dy * dy + (dz * dz + soft)
                inverse = lax.rsqrt(square)
                t = square * inverse - turn
                u = t - ((t + ROUNDER) - ROUNDER)
                u2 = u * u
                s = u * horner(SINE, u2)
                c = horner(COSINE, u2)
                a = inverse * size
                p = a * s
                new.append(((re + a) - p * s, im + p * c))
            sums = tuple(new)
        return sums

    return lax.fori_loop(0, members, step, tuple(sums), unroll=8 // len(tests))


def rows_of(sums):
    row_dev = len(sums) * SUB
    diagonal = lax.broadcasted_iota(jnp.int32, (row_dev, LANES), 1) == lax.broadcasted_iota(jnp.int32, (row_dev, LANES), 0)
    rows = []
    for part in range(2):
        column = jnp.concatenate([jnp.sum(pair[part], axis=1, keepdims=True) for pair in sums], axis=0)
        rows.append(jnp.sum(jnp.where(diagonal, column, 0.0), axis=0, keepdims=True))
    return rows


def near_of(half_columns, other, messages_ref, sibling_ref):
    last = messages_ref.shape[2] - LANES
    xs = messages_ref.shape[0] // half_columns
    middle = half_columns // 2
    straight = crossed = jnp.zeros((QUAD, LANES), jnp.float32)
    for k in range(half_columns):
        member = k * xs + lax.axis_index("x")
        own, sibling = messages_ref[member, :, last:], sibling_ref[member, :, last:]
        straight = straight + (own if k < middle else sibling)
        crossed = crossed + (sibling if k < middle else own)
    upper = lax.axis_index("column") >= middle
    total = jnp.where(upper, straight, crossed) if other else jnp.where(upper, crossed, straight)
    first = lax.axis_index("half") == (1 if other else 0)
    return jnp.where(first, total[0:1], total[1:2])


def first_kernel(wide_ref, messages_ref, sums_ref):
    groups = wide_ref.shape[2] // SUB
    tests = groups_of(wide_ref, 0) + groups_of(wide_ref, 1)
    zero = jnp.zeros((SUB, LANES), jnp.float32)
    for k, pair in enumerate(far_loop(tests, [(zero, zero)] * len(tests), messages_ref)):
        for part in range(2):
            sums_ref[k // groups, part, pl.ds(k % groups * SUB, SUB), :] = pair[part]


def second_kernel(half_columns, other, wide_ref, sums_ref, messages_ref, sibling_ref, out_ref):
    row_dev = wide_ref.shape[2]
    which = 0 if other else 1
    tests = groups_of(wide_ref, which)
    near = near_of(half_columns, other, messages_ref, sibling_ref)
    sums = [
        (sums_ref[which, 0, pl.ds(g * SUB, SUB), :], sums_ref[which, 1, pl.ds(g * SUB, SUB), :]) for g in range(len(tests))
    ]
    re, im = rows_of(far_loop(tests, sums, sibling_ref))
    out_ref[0:1, :] = re[:, :row_dev] + near[:, :row_dev]
    out_ref[1:2, :] = im[:, :row_dev] + near[:, row_dev : 2 * row_dev]


def across(x):
    return lax.ppermute(x, ("core", "half"), [(i, 3 - i) for i in range(4)])


def groups_for(xs, half_columns):
    def place(x, core, half, column):
        return ((x * 2 + core) * 2 + half) * half_columns + column

    return [
        [place(x, g ^ (column >= half_columns // 2), half, column) for column in range(half_columns) for x in range(xs)]
        for half in range(2)
        for g in range(2)
    ]


def local(rows, half_columns, test_points, src_points, currents, near_blocks, near_dest, near_tile):
    row_dev = test_points.shape[1]
    width = src_points.shape[1]
    items = near_blocks.shape[0]
    members = rows // 2 * half_columns
    gain = TURNS / math.sqrt(width * members * 4)
    message = (QUAD, 5 * width // QUAD + LANES)
    vmem = pl.BlockSpec(memory_space=pltpu.VMEM)
    hbm = pl.BlockSpec(memory_space=pltpu.HBM)
    params = pltpu.CompilerParams(vmem_limit_bytes=24 << 20)

    partner_points = across(test_points)
    copies = pl.pallas_call(
        functools.partial(pack_kernel, half_columns, gain),
        out_shape=jax.ShapeDtypeStruct((members,) + message, jnp.float32),
        in_specs=[hbm] * 5,
        out_specs=vmem,
        scratch_shapes=[
            pltpu.SMEM((items,), jnp.int32),
            pltpu.SMEM((items,), jnp.int32),
            pltpu.VMEM((3, width), jnp.float32),
            pltpu.VMEM((2, width), jnp.float32),
            pltpu.VMEM(near_blocks.shape, jnp.float32),
            pltpu.VMEM((5 * width // LANES, LANES), jnp.float32),
            pltpu.VMEM((2 * half_columns, LANES), jnp.float32),
            pltpu.SemaphoreType.DMA((5,)),
        ],
        cost_estimate=pl.CostEstimate(flops=1 << 20, bytes_accessed=1 << 20, transcendentals=0),
    )(near_dest.reshape(-1), near_tile.reshape(-1), src_points, currents, near_blocks)
    messages = lax.all_to_all(
        copies, ("x", "core", "half", "column"), split_axis=0, concat_axis=0, tiled=True,
        axis_index_groups=groups_for(rows // 2, half_columns),
    )


    evaluations = width * members * row_dev

    def cost(times):
        return dict(
            compiler_params=params,
            cost_estimate=pl.CostEstimate(
                flops=40 * evaluations * times, bytes_accessed=2 << 20, transcendentals=evaluations * times
            ),
        )

    wide = pl.pallas_call(
        points_kernel,
        out_shape=jax.ShapeDtypeStruct((2, 3, row_dev, LANES), jnp.float32),
        in_specs=[vmem] * 2,
        out_specs=vmem,
        **cost(1),
    )(partner_points, test_points)

    messages, wide = lax.optimization_barrier((messages, wide))
    sibling = lax.ppermute(messages, "core", [(0, 1), (1, 0)])
    sums = pl.pallas_call(
        first_kernel,
        out_shape=jax.ShapeDtypeStruct((2, 2, row_dev, LANES), jnp.float32),
        in_specs=[vmem] * 2,
        out_specs=vmem,
        **cost(2),
    )(wide, messages)

    def second(other):
        return pl.pallas_call(
            functools.partial(second_kernel, half_columns, other),
            out_shape=jax.ShapeDtypeStruct((2, row_dev), jnp.float32),
            in_specs=[vmem] * 4,
            out_specs=vmem,
            **cost(1),
        )(wide, sums, messages, sibling)

    from_partner = across(second(True))
    return second(False) + from_partner


def solution(mesh):
    rows, columns = mesh.shape["row"], mesh.shape["col"]
    finer = jax.sharding.Mesh(mesh.devices.reshape(rows // 2, 2, 2, columns // 2), ("x", "core", "half", "column"))
    every = ("x", "core", "half", "column")
    in_specs = (
        P(None, every),
        P(None, every),
        P(None, every),
        P(every, None, None, None),
        P(every, None),
        P(every, None),
    )
    body = functools.partial(local, rows, columns // 2)
    return jax.shard_map(body, mesh=finer, in_specs=in_specs, out_specs=P(None, every), check_vma=False)
```

```python
import functools
import math

import jax
import jax.numpy as jnp
import numpy as np
from jax import lax
from jax.experimental import pallas as pl
from jax.experimental.pallas import tpu as pltpu
from jax.sharding import PartitionSpec as P

WAVENUMBER = 40.0
SOFTENING = 0.01
TURNS = WAVENUMBER / (2.0 * math.pi)
LANES = 128
SUB = 8
QUAD = 4


def even_fit(function, terms, reach):
    nodes = np.cos((np.arange(400) + 0.5) * np.pi / 400)
    squares = (nodes + 1) * 0.5 * reach * reach
    fit = np.polynomial.chebyshev.Chebyshev.fit(squares, function(np.sqrt(squares)), terms - 1)
    return [float(value) for value in fit.convert(kind=np.polynomial.Polynomial).coef]


ROOT2 = math.sqrt(2.0)
SINE = even_fit(lambda u: ROOT2 * math.pi * np.sinc(u), 4, 0.5)
COSINE = even_fit(lambda u: -ROOT2 * np.cos(np.pi * u), 5, 0.5)
ANGLE = even_fit(lambda r: np.arctan(r) / (2 * np.pi * r), 9, 1.0)
ROUNDER = 1.5 * 2.0**23


def horner(coefficients, x):
    total = coefficients[-1] * x + coefficients[-2]
    for value in coefficients[-3::-1]:
        total = total * x + value
    return total


def phase_of(re, im):
    wide = jnp.abs(re)
    high = jnp.abs(im)
    larger = jnp.maximum(wide, high)
    ratio = jnp.minimum(wide, high) / jnp.where(larger == 0.0, 1.0, larger)
    turn = ratio * horner(ANGLE, ratio * ratio)
    turn = jnp.where(high > wide, 0.25 - turn, turn)
    turn = jnp.where(re < 0.0, 0.5 - turn, turn)
    return jnp.where(im < 0.0, -turn, turn)


def pack_kernel(
    half_columns, gain, dest_hbm, tile_hbm, src_hbm, cur_hbm, blocks_hbm, copies_ref,
    dest_ref, tile_ref, src_ref, cur_ref, blocks_ref, message, near_all, sems
):
    moves = [
        pltpu.make_async_copy(source, target, sems.at[k])
        for k, (source, target) in enumerate((
            (src_hbm, src_ref), (cur_hbm, cur_ref), (blocks_hbm, blocks_ref), (dest_hbm, dest_ref), (tile_hbm, tile_ref)
        ))
    ]
    for move in moves:
        move.start()
    members = copies_ref.shape[0]
    tiles = src_ref.shape[1] // LANES
    items, _, row_dev, _ = blocks_ref.shape
    columns = 2 * half_columns
    lane = lax.broadcasted_iota(jnp.int32, (SUB, LANES), 1)
    sub = lax.broadcasted_iota(jnp.int32, (SUB, LANES), 0)
    moves[0].wait()
    moves[1].wait()

    for tile in range(tiles):
        part = pl.ds(tile * LANES, LANES)
        message[pl.ds(3 * tiles + tile, 2, stride=tiles), :] = cur_ref[:, part]
        message[pl.ds(tile, 3, stride=tiles), :] = src_ref[:, part]
    cr = message[3 * tiles : 4 * tiles, :]
    ci = message[4 * tiles : 5 * tiles, :]
    values = [message[c * tiles : (c + 1) * tiles, :] * TURNS for c in range(3)]
    values += [jnp.sqrt(cr * cr + ci * ci) * gain, phase_of(cr, ci)]
    pieces = [value[part * QUAD : (part + 1) * QUAD] for value in values for part in range(tiles // QUAD)]
    last = len(pieces) * LANES

    def copy(member, _):
        for slot, piece in enumerate(pieces):
            copies_ref[member, :, slot * LANES : (slot + 1) * LANES] = piece
        copies_ref[member, :, last:] = jnp.zeros((QUAD, LANES), jnp.float32)
        return 0

    lax.fori_loop(0, members, copy, 0, unroll=8)

    for move in moves[2:]:
        move.wait()
    near = [jnp.zeros((SUB, LANES), jnp.float32)] * (columns // SUB)
    for block in range(items):
        tile = pl.multiple_of(tile_ref[block] * LANES, LANES)
        cr = cur_ref[0:1, pl.ds(tile, LANES)]
        ci = cur_ref[1:2, pl.ds(tile, LANES)]
        br = blocks_ref[block, 0]
        bi = blocks_ref[block, 1]
        row = jnp.zeros((SUB, LANES), jnp.float32)
        for part, product in enumerate((br * cr - bi * ci, br * ci + bi * cr)):
            total = jnp.sum(product, axis=1, keepdims=True)
            for piece in range(row_dev // SUB):
                spot = lane == sub + (part * row_dev + piece * SUB)
                row = jnp.where(spot, total[piece * SUB : (piece + 1) * SUB], row)
        row = jnp.sum(row, axis=0, keepdims=True)
        for group in range(columns // SUB):
            near[group] = near[group] + jnp.where(sub + group * SUB == dest_ref[block], row, 0.0)
    for group in range(columns // SUB):
        near_all[pl.ds(group * SUB, SUB), :] = near[group]

    xs = members // half_columns
    for k in range(half_columns):
        for half in range(2):
            copies_ref[members - 1 - k * xs - lax.axis_index("x"), half : half + 1, last:] = near_all[half * half_columns + k : half * half_columns + k + 1, :]


def points_kernel(partner_ref, tests_ref, wide_ref):
    row_dev = tests_ref.shape[1]
    lane = lax.broadcasted_iota(jnp.int32, (row_dev, LANES), 1)
    sub = lax.broadcasted_iota(jnp.int32, (row_dev, LANES), 0)
    for which, ref in enumerate((partner_ref, tests_ref)):
        points = jnp.concatenate([ref[...], jnp.zeros((3, LANES - row_dev), jnp.float32)], axis=1) * TURNS
        for c in range(3):
            column = jnp.sum(jnp.where(lane == sub, points[c : c + 1, :], 0.0), axis=1, keepdims=True)
            wide_ref[which, c] = jnp.broadcast_to(column, (row_dev, LANES))


def groups_of(wide_ref, which):
    return [[wide_ref[which, c, pl.ds(g * SUB, SUB), :] for c in range(3)] for g in range(wide_ref.shape[2] // SUB)]


def far_loop(tests, sums, messages_ref):
    members = messages_ref.shape[0]
    slots = (messages_ref.shape[2] // LANES - 1) // 5
    soft = (SOFTENING * TURNS) ** 2

    def step(member, sums):
        for slot, row in [(slot, row) for slot in range(slots) for row in range(QUAD)]:
            sx, sy, sz, size, turn = [
                jnp.broadcast_to(
                    messages_ref[member, row : row + 1, (c * slots + slot) * LANES : (c * slots + slot + 1) * LANES], (SUB, LANES)
                )
                for c in range(5)
            ]
            new = []
            for (tx, ty, tz), (re, im) in zip(tests, sums):
                dx = tx - sx
                dy = ty - sy
                dz = tz - sz
                square = dx * dx + dy * dy + (dz * dz + soft)
                inverse = lax.rsqrt(square)
                t = square * inverse - turn
                u = t - ((t + ROUNDER) - ROUNDER)
                u2 = u * u
                s = u * horner(SINE, u2)
                c = horner(COSINE, u2)
                a = inverse * size
                p = a * s
                new.append(((re + a) - p * s, im + p * c))
            sums = tuple(new)
        return sums

    return lax.fori_loop(0, members, step, tuple(sums), unroll=8 // len(tests))


def rows_of(sums):
    row_dev = len(sums) * SUB
    diagonal = lax.broadcasted_iota(jnp.int32, (row_dev, LANES), 1) == lax.broadcasted_iota(jnp.int32, (row_dev, LANES), 0)
    rows = []
    for part in range(2):
        column = jnp.concatenate([jnp.sum(pair[part], axis=1, keepdims=True) for pair in sums], axis=0)
        rows.append(jnp.sum(jnp.where(diagonal, column, 0.0), axis=0, keepdims=True))
    return rows


def near_of(half_columns, other, messages_ref, sibling_ref):
    last = messages_ref.shape[2] - LANES
    xs = messages_ref.shape[0] // half_columns
    middle = half_columns // 2
    straight = crossed = jnp.zeros((QUAD, LANES), jnp.float32)
    for k in range(half_columns):
        member = messages_ref.shape[0] - 1 - k * xs - lax.axis_index("x")
        own, sibling = messages_ref[member, :, last:], sibling_ref[member, :, last:]
        straight = straight + (own if k < middle else sibling)
        crossed = crossed + (sibling if k < middle else own)
    upper = lax.axis_index("column") >= middle
    total = jnp.where(upper, straight, crossed) if other else jnp.where(upper, crossed, straight)
    first = lax.axis_index("half") == (1 if other else 0)
    return jnp.where(first, total[0:1], total[1:2])


def first_kernel(wide_ref, messages_ref, sums_ref):
    groups = wide_ref.shape[2] // SUB
    tests = groups_of(wide_ref, 0) + groups_of(wide_ref, 1)
    zero = jnp.zeros((SUB, LANES), jnp.float32)
    for k, pair in enumerate(far_loop(tests, [(zero, zero)] * len(tests), messages_ref)):
        for part in range(2):
            sums_ref[k // groups, part, pl.ds(k % groups * SUB, SUB), :] = pair[part]


def second_kernel(half_columns, other, wide_ref, sums_ref, messages_ref, sibling_ref, out_ref):
    row_dev = wide_ref.shape[2]
    which = 0 if other else 1
    tests = groups_of(wide_ref, which)
    near = near_of(half_columns, other, messages_ref, sibling_ref)
    sums = [
        (sums_ref[which, 0, pl.ds(g * SUB, SUB), :], sums_ref[which, 1, pl.ds(g * SUB, SUB), :]) for g in range(len(tests))
    ]
    re, im = rows_of(far_loop(tests, sums, sibling_ref))
    out_ref[0:1, :] = re[:, :row_dev] + near[:, :row_dev]
    out_ref[1:2, :] = im[:, :row_dev] + near[:, row_dev : 2 * row_dev]


def across(x):
    return lax.ppermute(x, ("core", "half"), [(i, 3 - i) for i in range(4)])


def groups_for(xs, half_columns):
    def place(x, core, half, column):
        return ((x * 2 + core) * 2 + half) * half_columns + column

    return [
        [place(x, g ^ (column >= half_columns // 2), half, column) for column in reversed(range(half_columns)) for x in reversed(range(xs))]
        for half in range(2)
        for g in range(2)
    ]


def local(rows, half_columns, test_points, src_points, currents, near_blocks, near_dest, near_tile):
    row_dev = test_points.shape[1]
    width = src_points.shape[1]
    items = near_blocks.shape[0]
    members = rows // 2 * half_columns
    gain = TURNS / math.sqrt(width * members * 4)
    message = (QUAD, 5 * width // QUAD + LANES)
    vmem = pl.BlockSpec(memory_space=pltpu.VMEM)
    hbm = pl.BlockSpec(memory_space=pltpu.HBM)
    params = pltpu.CompilerParams(vmem_limit_bytes=24 << 20)

    partner_points = across(test_points)
    copies = pl.pallas_call(
        functools.partial(pack_kernel, half_columns, gain),
        out_shape=jax.ShapeDtypeStruct((members,) + message, jnp.float32),
        in_specs=[hbm] * 5,
        out_specs=vmem,
        scratch_shapes=[
            pltpu.SMEM((items,), jnp.int32),
            pltpu.SMEM((items,), jnp.int32),
            pltpu.VMEM((3, width), jnp.float32),
            pltpu.VMEM((2, width), jnp.float32),
            pltpu.VMEM(near_blocks.shape, jnp.float32),
            pltpu.VMEM((5 * width // LANES, LANES), jnp.float32),
            pltpu.VMEM((2 * half_columns, LANES), jnp.float32),
            pltpu.SemaphoreType.DMA((5,)),
        ],
        cost_estimate=pl.CostEstimate(flops=1 << 20, bytes_accessed=1 << 20, transcendentals=0),
    )(near_dest.reshape(-1), near_tile.reshape(-1), src_points, currents, near_blocks)
    messages = lax.all_to_all(
        copies, ("x", "core", "half", "column"), split_axis=0, concat_axis=0, tiled=True,
        axis_index_groups=groups_for(rows // 2, half_columns),
    )


    evaluations = width * members * row_dev

    def cost(times):
        return dict(
            compiler_params=params,
            cost_estimate=pl.CostEstimate(
                flops=40 * evaluations * times, bytes_accessed=2 << 20, transcendentals=evaluations * times
            ),
        )

    wide = pl.pallas_call(
        points_kernel,
        out_shape=jax.ShapeDtypeStruct((2, 3, row_dev, LANES), jnp.float32),
        in_specs=[vmem] * 2,
        out_specs=vmem,
        **cost(1),
    )(partner_points, test_points)

    messages, wide = lax.optimization_barrier((messages, wide))
    sibling = lax.ppermute(messages, "core", [(0, 1), (1, 0)])
    sums = pl.pallas_call(
        first_kernel,
        out_shape=jax.ShapeDtypeStruct((2, 2, row_dev, LANES), jnp.float32),
        in_specs=[vmem] * 2,
        out_specs=vmem,
        **cost(2),
    )(wide, messages)

    def second(other):
        return pl.pallas_call(
            functools.partial(second_kernel, half_columns, other),
            out_shape=jax.ShapeDtypeStruct((2, row_dev), jnp.float32),
            in_specs=[vmem] * 4,
            out_specs=vmem,
            **cost(1),
        )(wide, sums, messages, sibling)

    from_partner = across(second(True))
    return second(False) + from_partner


def solution(mesh):
    rows, columns = mesh.shape["row"], mesh.shape["col"]
    finer = jax.sharding.Mesh(mesh.devices.reshape(rows // 2, 2, 2, columns // 2), ("x", "core", "half", "column"))
    every = ("x", "core", "half", "column")
    in_specs = (
        P(None, every),
        P(None, every),
        P(None, every),
        P(every, None, None, None),
        P(every, None),
        P(every, None),
    )
    body = functools.partial(local, rows, columns // 2)
    return jax.shard_map(body, mesh=finer, in_specs=in_specs, out_specs=P(None, every), check_vma=False)
```

```python
import functools
import math

import jax
import jax.numpy as jnp
import numpy as np
from jax import lax
from jax.experimental import pallas as pl
from jax.experimental.pallas import tpu as pltpu
from jax.sharding import PartitionSpec as P

WAVENUMBER = 40.0
SOFTENING = 0.01
TURNS = WAVENUMBER / (2.0 * math.pi)
LANES = 128
SUB = 8
QUAD = 4


def even_fit(function, terms, reach):
    nodes = np.cos((np.arange(400) + 0.5) * np.pi / 400)
    squares = (nodes + 1) * 0.5 * reach * reach
    fit = np.polynomial.chebyshev.Chebyshev.fit(squares, function(np.sqrt(squares)), terms - 1)
    return [float(value) for value in fit.convert(kind=np.polynomial.Polynomial).coef]


ROOT2 = math.sqrt(2.0)
SINE = even_fit(lambda u: ROOT2 * math.pi * np.sinc(u), 4, 0.5)
COSINE = even_fit(lambda u: -ROOT2 * np.cos(np.pi * u), 5, 0.5)
ANGLE = even_fit(lambda r: np.arctan(r) / (2 * np.pi * r), 9, 1.0)
ROUNDER = 1.5 * 2.0**23


def horner(coefficients, x):
    total = coefficients[-1] * x + coefficients[-2]
    for value in coefficients[-3::-1]:
        total = total * x + value
    return total


def phase_of(re, im):
    wide = jnp.abs(re)
    high = jnp.abs(im)
    larger = jnp.maximum(wide, high)
    ratio = jnp.minimum(wide, high) / jnp.where(larger == 0.0, 1.0, larger)
    turn = ratio * horner(ANGLE, ratio * ratio)
    turn = jnp.where(high > wide, 0.25 - turn, turn)
    turn = jnp.where(re < 0.0, 0.5 - turn, turn)
    return jnp.where(im < 0.0, -turn, turn)


def pack_kernel(
    half_columns, gain, dest_hbm, tile_hbm, src_hbm, cur_hbm, blocks_hbm, copies_ref,
    dest_ref, tile_ref, src_ref, cur_ref, blocks_ref, message, near_all, sems
):
    moves = [
        pltpu.make_async_copy(source, target, sems.at[k])
        for k, (source, target) in enumerate((
            (src_hbm, src_ref), (cur_hbm, cur_ref), (blocks_hbm, blocks_ref), (dest_hbm, dest_ref), (tile_hbm, tile_ref)
        ))
    ]
    for move in moves:
        move.start()
    members = copies_ref.shape[0]
    tiles = src_ref.shape[1] // LANES
    items, _, row_dev, _ = blocks_ref.shape
    columns = 2 * half_columns
    lane = lax.broadcasted_iota(jnp.int32, (SUB, LANES), 1)
    sub = lax.broadcasted_iota(jnp.int32, (SUB, LANES), 0)
    moves[0].wait()
    moves[1].wait()

    for tile in range(tiles):
        part = pl.ds(tile * LANES, LANES)
        message[pl.ds(3 * tiles + tile, 2, stride=tiles), :] = cur_ref[:, part]
        message[pl.ds(tile, 3, stride=tiles), :] = src_ref[:, part]
    cr = message[3 * tiles : 4 * tiles, :]
    ci = message[4 * tiles : 5 * tiles, :]
    values = [message[c * tiles : (c + 1) * tiles, :] * TURNS for c in range(3)]
    values += [jnp.sqrt(cr * cr + ci * ci) * gain, phase_of(cr, ci)]
    pieces = [value[part * QUAD : (part + 1) * QUAD] for value in values for part in range(tiles // QUAD)]
    last = len(pieces) * LANES

    def copy(member, _):
        for slot, piece in enumerate(pieces):
            copies_ref[member, :, slot * LANES : (slot + 1) * LANES] = piece
        copies_ref[member, :, last:] = jnp.zeros((QUAD, LANES), jnp.float32)
        return 0

    lax.fori_loop(0, members, copy, 0, unroll=8)

    for move in moves[2:]:
        move.wait()
    near = [jnp.zeros((SUB, LANES), jnp.float32)] * (columns // SUB)
    for block in range(items):
        tile = pl.multiple_of(tile_ref[block] * LANES, LANES)
        cr = cur_ref[0:1, pl.ds(tile, LANES)]
        ci = cur_ref[1:2, pl.ds(tile, LANES)]
        br = blocks_ref[block, 0]
        bi = blocks_ref[block, 1]
        row = jnp.zeros((SUB, LANES), jnp.float32)
        for part, product in enumerate((br * cr - bi * ci, br * ci + bi * cr)):
            total = jnp.sum(product, axis=1, keepdims=True)
            for piece in range(row_dev // SUB):
                spot = lane == sub + (part * row_dev + piece * SUB)
                row = jnp.where(spot, total[piece * SUB : (piece + 1) * SUB], row)
        row = jnp.sum(row, axis=0, keepdims=True)
        for group in range(columns // SUB):
            near[group] = near[group] + jnp.where(sub + group * SUB == dest_ref[block], row, 0.0)
    for group in range(columns // SUB):
        near_all[pl.ds(group * SUB, SUB), :] = near[group]

    xs = members // half_columns
    for k in range(half_columns):
        for half in range(2):
            copies_ref[k * xs + lax.axis_index("x"), half : half + 1, last:] = near_all[half * half_columns + k : half * half_columns + k + 1, :]


def points_kernel(partner_ref, tests_ref, wide_ref):
    row_dev = tests_ref.shape[1]
    lane = lax.broadcasted_iota(jnp.int32, (row_dev, LANES), 1)
    sub = lax.broadcasted_iota(jnp.int32, (row_dev, LANES), 0)
    for which, ref in enumerate((partner_ref, tests_ref)):
        points = jnp.concatenate([ref[...], jnp.zeros((3, LANES - row_dev), jnp.float32)], axis=1) * TURNS
        for c in range(3):
            column = jnp.sum(jnp.where(lane == sub, points[c : c + 1, :], 0.0), axis=1, keepdims=True)
            wide_ref[which, c] = jnp.broadcast_to(column, (row_dev, LANES))


def groups_of(wide_ref, which):
    return [[wide_ref[which, c, pl.ds(g * SUB, SUB), :] for c in range(3)] for g in range(wide_ref.shape[2] // SUB)]


def far_loop(tests, sums, messages_ref):
    members = messages_ref.shape[0]
    slots = (messages_ref.shape[2] // LANES - 1) // 5
    soft = (SOFTENING * TURNS) ** 2

    def step(member, sums):
        for slot, row in [(slot, row) for slot in range(slots) for row in range(QUAD)]:
            sx, sy, sz, size, turn = [
                jnp.broadcast_to(
                    messages_ref[member, row : row + 1, (c * slots + slot) * LANES : (c * slots + slot + 1) * LANES], (SUB, LANES)
                )
                for c in range(5)
            ]
            new = []
            for (tx, ty, tz), (re, im) in zip(tests, sums):
                dx = tx - sx
                dy = ty - sy
                dz = tz - sz
                square = dx * dx + dy * dy + (dz * dz + soft)
                inverse = lax.rsqrt(square)
                t = square * inverse - turn
                u = t - ((t + ROUNDER) - ROUNDER)
                u2 = u * u
                s = u * horner(SINE, u2)
                c = horner(COSINE, u2)
                a = inverse * size
                p = a * s
                new.append(((re + a) - p * s, im + p * c))
            sums = tuple(new)
        return sums

    return lax.fori_loop(0, members, step, tuple(sums), unroll=16 // len(tests))


def rows_of(sums):
    row_dev = len(sums) * SUB
    diagonal = lax.broadcasted_iota(jnp.int32, (row_dev, LANES), 1) == lax.broadcasted_iota(jnp.int32, (row_dev, LANES), 0)
    rows = []
    for part in range(2):
        column = jnp.concatenate([jnp.sum(pair[part], axis=1, keepdims=True) for pair in sums], axis=0)
        rows.append(jnp.sum(jnp.where(diagonal, column, 0.0), axis=0, keepdims=True))
    return rows


def near_of(half_columns, other, messages_ref, sibling_ref):
    last = messages_ref.shape[2] - LANES
    xs = messages_ref.shape[0] // half_columns
    middle = half_columns // 2
    straight = crossed = jnp.zeros((QUAD, LANES), jnp.float32)
    for k in range(half_columns):
        member = k * xs + lax.axis_index("x")
        own, sibling = messages_ref[member, :, last:], sibling_ref[member, :, last:]
        straight = straight + (own if k < middle else sibling)
        crossed = crossed + (sibling if k < middle else own)
    upper = lax.axis_index("column") >= middle
    total = jnp.where(upper, straight, crossed) if other else jnp.where(upper, crossed, straight)
    first = lax.axis_index("half") == (1 if other else 0)
    return jnp.where(first, total[0:1], total[1:2])


def first_kernel(wide_ref, messages_ref, sums_ref):
    groups = wide_ref.shape[2] // SUB
    tests = groups_of(wide_ref, 0) + groups_of(wide_ref, 1)
    zero = jnp.zeros((SUB, LANES), jnp.float32)
    for k, pair in enumerate(far_loop(tests, [(zero, zero)] * len(tests), messages_ref)):
        for part in range(2):
            sums_ref[k // groups, part, pl.ds(k % groups * SUB, SUB), :] = pair[part]


def second_kernel(half_columns, other, wide_ref, sums_ref, messages_ref, sibling_ref, out_ref):
    row_dev = wide_ref.shape[2]
    which = 0 if other else 1
    tests = groups_of(wide_ref, which)
    near = near_of(half_columns, other, messages_ref, sibling_ref)
    sums = [
        (sums_ref[which, 0, pl.ds(g * SUB, SUB), :], sums_ref[which, 1, pl.ds(g * SUB, SUB), :]) for g in range(len(tests))
    ]
    re, im = rows_of(far_loop(tests, sums, sibling_ref))
    out_ref[0:1, :] = re[:, :row_dev] + near[:, :row_dev]
    out_ref[1:2, :] = im[:, :row_dev] + near[:, row_dev : 2 * row_dev]


def across(x):
    return lax.ppermute(x, ("core", "half"), [(i, 3 - i) for i in range(4)])


def groups_for(xs, half_columns):
    def place(x, core, half, column):
        return ((x * 2 + core) * 2 + half) * half_columns + column

    return [
        [place(x, g ^ (column >= half_columns // 2), half, column) for column in range(half_columns) for x in range(xs)]
        for half in range(2)
        for g in range(2)
    ]


def local(rows, half_columns, test_points, src_points, currents, near_blocks, near_dest, near_tile):
    row_dev = test_points.shape[1]
    width = src_points.shape[1]
    items = near_blocks.shape[0]
    members = rows // 2 * half_columns
    gain = TURNS / math.sqrt(width * members * 4)
    message = (QUAD, 5 * width // QUAD + LANES)
    vmem = pl.BlockSpec(memory_space=pltpu.VMEM)
    hbm = pl.BlockSpec(memory_space=pltpu.HBM)
    params = pltpu.CompilerParams(vmem_limit_bytes=24 << 20)

    partner_points = across(test_points)
    copies = pl.pallas_call(
        functools.partial(pack_kernel, half_columns, gain),
        out_shape=jax.ShapeDtypeStruct((members,) + message, jnp.float32),
        in_specs=[hbm] * 5,
        out_specs=vmem,
        scratch_shapes=[
            pltpu.SMEM((items,), jnp.int32),
            pltpu.SMEM((items,), jnp.int32),
            pltpu.VMEM((3, width), jnp.float32),
            pltpu.VMEM((2, width), jnp.float32),
            pltpu.VMEM(near_blocks.shape, jnp.float32),
            pltpu.VMEM((5 * width // LANES, LANES), jnp.float32),
            pltpu.VMEM((2 * half_columns, LANES), jnp.float32),
            pltpu.SemaphoreType.DMA((5,)),
        ],
        cost_estimate=pl.CostEstimate(flops=1 << 20, bytes_accessed=1 << 20, transcendentals=0),
    )(near_dest.reshape(-1), near_tile.reshape(-1), src_points, currents, near_blocks)
    messages = lax.all_to_all(
        copies, ("x", "core", "half", "column"), split_axis=0, concat_axis=0, tiled=True,
        axis_index_groups=groups_for(rows // 2, half_columns),
    )


    evaluations = width * members * row_dev

    def cost(times):
        return dict(
            compiler_params=params,
            cost_estimate=pl.CostEstimate(
                flops=40 * evaluations * times, bytes_accessed=2 << 20, transcendentals=evaluations * times
            ),
        )

    wide = pl.pallas_call(
        points_kernel,
        out_shape=jax.ShapeDtypeStruct((2, 3, row_dev, LANES), jnp.float32),
        in_specs=[vmem] * 2,
        out_specs=vmem,
        **cost(1),
    )(partner_points, test_points)

    messages, wide = lax.optimization_barrier((messages, wide))
    sibling = lax.ppermute(messages, "core", [(0, 1), (1, 0)])
    sums = pl.pallas_call(
        first_kernel,
        out_shape=jax.ShapeDtypeStruct((2, 2, row_dev, LANES), jnp.float32),
        in_specs=[vmem] * 2,
        out_specs=vmem,
        **cost(2),
    )(wide, messages)

    def second(other):
        return pl.pallas_call(
            functools.partial(second_kernel, half_columns, other),
            out_shape=jax.ShapeDtypeStruct((2, row_dev), jnp.float32),
            in_specs=[vmem] * 4,
            out_specs=vmem,
            **cost(1),
        )(wide, sums, messages, sibling)

    from_partner = across(second(True))
    return second(False) + from_partner


def solution(mesh):
    rows, columns = mesh.shape["row"], mesh.shape["col"]
    finer = jax.sharding.Mesh(mesh.devices.reshape(rows // 2, 2, 2, columns // 2), ("x", "core", "half", "column"))
    every = ("x", "core", "half", "column")
    in_specs = (
        P(None, every),
        P(None, every),
        P(None, every),
        P(every, None, None, None),
        P(every, None),
        P(every, None),
    )
    body = functools.partial(local, rows, columns // 2)
    return jax.shard_map(body, mesh=finer, in_specs=in_specs, out_specs=P(None, every), check_vma=False)
```

```python
import functools
import math

import jax
import jax.numpy as jnp
import numpy as np
from jax import lax
from jax.experimental import pallas as pl
from jax.experimental.pallas import tpu as pltpu
from jax.sharding import PartitionSpec as P

WAVENUMBER = 40.0
SOFTENING = 0.01
TURNS = WAVENUMBER / (2.0 * math.pi)
LANES = 128
SUB = 8
QUAD = 4


def even_fit(function, terms, reach):
    nodes = np.cos((np.arange(400) + 0.5) * np.pi / 400)
    squares = (nodes + 1) * 0.5 * reach * reach
    fit = np.polynomial.chebyshev.Chebyshev.fit(squares, function(np.sqrt(squares)), terms - 1)
    return [float(value) for value in fit.convert(kind=np.polynomial.Polynomial).coef]


ROOT2 = math.sqrt(2.0)
SINE = even_fit(lambda u: ROOT2 * math.pi * np.sinc(u), 4, 0.5)
COSINE = even_fit(lambda u: -ROOT2 * np.cos(np.pi * u), 5, 0.5)
ANGLE = even_fit(lambda r: np.arctan(r) / (2 * np.pi * r), 9, 1.0)
ROUNDER = 1.5 * 2.0**23


def horner(coefficients, x):
    total = coefficients[-1] * x + coefficients[-2]
    for value in coefficients[-3::-1]:
        total = total * x + value
    return total


def phase_of(re, im):
    wide = jnp.abs(re)
    high = jnp.abs(im)
    larger = jnp.maximum(wide, high)
    ratio = jnp.minimum(wide, high) / jnp.where(larger == 0.0, 1.0, larger)
    turn = ratio * horner(ANGLE, ratio * ratio)
    turn = jnp.where(high > wide, 0.25 - turn, turn)
    turn = jnp.where(re < 0.0, 0.5 - turn, turn)
    return jnp.where(im < 0.0, -turn, turn)


def pack_kernel(
    half_columns, gain, dest_hbm, tile_hbm, src_hbm, cur_hbm, blocks_hbm, copies_ref,
    dest_ref, tile_ref, src_ref, cur_ref, blocks_ref, message, near_all, sems
):
    moves = [
        pltpu.make_async_copy(source, target, sems.at[k])
        for k, (source, target) in enumerate((
            (src_hbm, src_ref), (cur_hbm, cur_ref), (blocks_hbm, blocks_ref), (dest_hbm, dest_ref), (tile_hbm, tile_ref)
        ))
    ]
    for move in (*moves[3:], *moves[:3]):
        move.start()
    members = copies_ref.shape[0]
    tiles = src_ref.shape[1] // LANES
    items, _, row_dev, _ = blocks_ref.shape
    columns = 2 * half_columns
    lane = lax.broadcasted_iota(jnp.int32, (SUB, LANES), 1)
    sub = lax.broadcasted_iota(jnp.int32, (SUB, LANES), 0)
    moves[0].wait()
    moves[1].wait()

    for tile in range(tiles):
        part = pl.ds(tile * LANES, LANES)
        message[pl.ds(3 * tiles + tile, 2, stride=tiles), :] = cur_ref[:, part]
        message[pl.ds(tile, 3, stride=tiles), :] = src_ref[:, part]
    cr = message[3 * tiles : 4 * tiles, :]
    ci = message[4 * tiles : 5 * tiles, :]
    values = [message[c * tiles : (c + 1) * tiles, :] * TURNS for c in range(3)]
    values += [jnp.sqrt(cr * cr + ci * ci) * gain, phase_of(cr, ci)]
    pieces = [value[part * QUAD : (part + 1) * QUAD] for value in values for part in range(tiles // QUAD)]
    last = len(pieces) * LANES

    def copy(member, _):
        for slot, piece in enumerate(pieces):
            copies_ref[member, :, slot * LANES : (slot + 1) * LANES] = piece
        copies_ref[member, :, last:] = jnp.zeros((QUAD, LANES), jnp.float32)
        return 0

    lax.fori_loop(0, members, copy, 0, unroll=8)

    for move in moves[2:]:
        move.wait()
    near = [jnp.zeros((SUB, LANES), jnp.float32)] * (columns // SUB)
    for block in range(items):
        tile = pl.multiple_of(tile_ref[block] * LANES, LANES)
        cr = cur_ref[0:1, pl.ds(tile, LANES)]
        ci = cur_ref[1:2, pl.ds(tile, LANES)]
        br = blocks_ref[block, 0]
        bi = blocks_ref[block, 1]
        row = jnp.zeros((SUB, LANES), jnp.float32)
        for part, product in enumerate((br * cr - bi * ci, br * ci + bi * cr)):
            total = jnp.sum(product, axis=1, keepdims=True)
            for piece in range(row_dev // SUB):
                spot = lane == sub + (part * row_dev + piece * SUB)
                row = jnp.where(spot, total[piece * SUB : (piece + 1) * SUB], row)
        row = jnp.sum(row, axis=0, keepdims=True)
        for group in range(columns // SUB):
            near[group] = near[group] + jnp.where(sub + group * SUB == dest_ref[block], row, 0.0)
    for group in range(columns // SUB):
        near_all[pl.ds(group * SUB, SUB), :] = near[group]

    xs = members // half_columns
    for k in range(half_columns):
        for half in range(2):
            copies_ref[k * xs + lax.axis_index("x"), half : half + 1, last:] = near_all[half * half_columns + k : half * half_columns + k + 1, :]


def points_kernel(partner_ref, tests_ref, wide_ref):
    row_dev = tests_ref.shape[1]
    lane = lax.broadcasted_iota(jnp.int32, (row_dev, LANES), 1)
    sub = lax.broadcasted_iota(jnp.int32, (row_dev, LANES), 0)
    for which, ref in enumerate((partner_ref, tests_ref)):
        points = jnp.concatenate([ref[...], jnp.zeros((3, LANES - row_dev), jnp.float32)], axis=1) * TURNS
        for c in range(3):
            column = jnp.sum(jnp.where(lane == sub, points[c : c + 1, :], 0.0), axis=1, keepdims=True)
            wide_ref[which, c] = jnp.broadcast_to(column, (row_dev, LANES))


def groups_of(wide_ref, which):
    return [[wide_ref[which, c, pl.ds(g * SUB, SUB), :] for c in range(3)] for g in range(wide_ref.shape[2] // SUB)]


def far_loop(tests, sums, messages_ref):
    members = messages_ref.shape[0]
    slots = (messages_ref.shape[2] // LANES - 1) // 5
    soft = (SOFTENING * TURNS) ** 2

    def step(member, sums):
        for slot, row in [(slot, row) for slot in range(slots) for row in range(QUAD)]:
            sx, sy, sz, size, turn = [
                jnp.broadcast_to(
                    messages_ref[member, row : row + 1, (c * slots + slot) * LANES : (c * slots + slot + 1) * LANES], (SUB, LANES)
                )
                for c in range(5)
            ]
            new = []
            for (tx, ty, tz), (re, im) in zip(tests, sums):
                dx = tx - sx
                dy = ty - sy
                dz = tz - sz
                square = dx * dx + dy * dy + (dz * dz + soft)
                inverse = lax.rsqrt(square)
                t = square * inverse - turn
                u = t - ((t + ROUNDER) - ROUNDER)
                u2 = u * u
                s = u * horner(SINE, u2)
                c = horner(COSINE, u2)
                a = inverse * size
                p = a * s
                new.append(((re + a) - p * s, im + p * c))
            sums = tuple(new)
        return sums

    return lax.fori_loop(0, members, step, tuple(sums), unroll=8 // len(tests))


def rows_of(sums):
    row_dev = len(sums) * SUB
    diagonal = lax.broadcasted_iota(jnp.int32, (row_dev, LANES), 1) == lax.broadcasted_iota(jnp.int32, (row_dev, LANES), 0)
    rows = []
    for part in range(2):
        column = jnp.concatenate([jnp.sum(pair[part], axis=1, keepdims=True) for pair in sums], axis=0)
        rows.append(jnp.sum(jnp.where(diagonal, column, 0.0), axis=0, keepdims=True))
    return rows


def near_of(half_columns, other, messages_ref, sibling_ref):
    last = messages_ref.shape[2] - LANES
    xs = messages_ref.shape[0] // half_columns
    middle = half_columns // 2
    straight = crossed = jnp.zeros((QUAD, LANES), jnp.float32)
    for k in range(half_columns):
        member = k * xs + lax.axis_index("x")
        own, sibling = messages_ref[member, :, last:], sibling_ref[member, :, last:]
        straight = straight + (own if k < middle else sibling)
        crossed = crossed + (sibling if k < middle else own)
    upper = lax.axis_index("column") >= middle
    total = jnp.where(upper, straight, crossed) if other else jnp.where(upper, crossed, straight)
    first = lax.axis_index("half") == (1 if other else 0)
    return jnp.where(first, total[0:1], total[1:2])


def first_kernel(wide_ref, messages_ref, sums_ref):
    groups = wide_ref.shape[2] // SUB
    tests = groups_of(wide_ref, 0) + groups_of(wide_ref, 1)
    zero = jnp.zeros((SUB, LANES), jnp.float32)
    for k, pair in enumerate(far_loop(tests, [(zero, zero)] * len(tests), messages_ref)):
        for part in range(2):
            sums_ref[k // groups, part, pl.ds(k % groups * SUB, SUB), :] = pair[part]


def second_kernel(half_columns, other, wide_ref, sums_ref, messages_ref, sibling_ref, out_ref):
    row_dev = wide_ref.shape[2]
    which = 0 if other else 1
    tests = groups_of(wide_ref, which)
    near = near_of(half_columns, other, messages_ref, sibling_ref)
    sums = [
        (sums_ref[which, 0, pl.ds(g * SUB, SUB), :], sums_ref[which, 1, pl.ds(g * SUB, SUB), :]) for g in range(len(tests))
    ]
    re, im = rows_of(far_loop(tests, sums, sibling_ref))
    out_ref[0:1, :] = re[:, :row_dev] + near[:, :row_dev]
    out_ref[1:2, :] = im[:, :row_dev] + near[:, row_dev : 2 * row_dev]


def across(x):
    return lax.ppermute(x, ("core", "half"), [(i, 3 - i) for i in range(4)])


def groups_for(xs, half_columns):
    def place(x, core, half, column):
        return ((x * 2 + core) * 2 + half) * half_columns + column

    return [
        [place(x, g ^ (column >= half_columns // 2), half, column) for column in range(half_columns) for x in range(xs)]
        for half in range(2)
        for g in range(2)
    ]


def local(rows, half_columns, test_points, src_points, currents, near_blocks, near_dest, near_tile):
    row_dev = test_points.shape[1]
    width = src_points.shape[1]
    items = near_blocks.shape[0]
    members = rows // 2 * half_columns
    gain = TURNS / math.sqrt(width * members * 4)
    message = (QUAD, 5 * width // QUAD + LANES)
    vmem = pl.BlockSpec(memory_space=pltpu.VMEM)
    hbm = pl.BlockSpec(memory_space=pltpu.HBM)
    params = pltpu.CompilerParams(vmem_limit_bytes=24 << 20)

    partner_points = across(test_points)
    copies = pl.pallas_call(
        functools.partial(pack_kernel, half_columns, gain),
        out_shape=jax.ShapeDtypeStruct((members,) + message, jnp.float32),
        in_specs=[hbm] * 5,
        out_specs=vmem,
        scratch_shapes=[
            pltpu.SMEM((items,), jnp.int32),
            pltpu.SMEM((items,), jnp.int32),
            pltpu.VMEM((3, width), jnp.float32),
            pltpu.VMEM((2, width), jnp.float32),
            pltpu.VMEM(near_blocks.shape, jnp.float32),
            pltpu.VMEM((5 * width // LANES, LANES), jnp.float32),
            pltpu.VMEM((2 * half_columns, LANES), jnp.float32),
            pltpu.SemaphoreType.DMA((5,)),
        ],
        cost_estimate=pl.CostEstimate(flops=1 << 20, bytes_accessed=1 << 20, transcendentals=0),
    )(near_dest.reshape(-1), near_tile.reshape(-1), src_points, currents, near_blocks)
    messages = lax.all_to_all(
        copies, ("x", "core", "half", "column"), split_axis=0, concat_axis=0, tiled=True,
        axis_index_groups=groups_for(rows // 2, half_columns),
    )


    evaluations = width * members * row_dev

    def cost(times):
        return dict(
            compiler_params=params,
            cost_estimate=pl.CostEstimate(
                flops=40 * evaluations * times, bytes_accessed=2 << 20, transcendentals=evaluations * times
            ),
        )

    wide = pl.pallas_call(
        points_kernel,
        out_shape=jax.ShapeDtypeStruct((2, 3, row_dev, LANES), jnp.float32),
        in_specs=[vmem] * 2,
        out_specs=vmem,
        **cost(1),
    )(partner_points, test_points)

    messages, wide = lax.optimization_barrier((messages, wide))
    sibling = lax.ppermute(messages, "core", [(0, 1), (1, 0)])
    sums = pl.pallas_call(
        first_kernel,
        out_shape=jax.ShapeDtypeStruct((2, 2, row_dev, LANES), jnp.float32),
        in_specs=[vmem] * 2,
        out_specs=vmem,
        **cost(2),
    )(wide, messages)

    def second(other):
        return pl.pallas_call(
            functools.partial(second_kernel, half_columns, other),
            out_shape=jax.ShapeDtypeStruct((2, row_dev), jnp.float32),
            in_specs=[vmem] * 4,
            out_specs=vmem,
            **cost(1),
        )(wide, sums, messages, sibling)

    from_partner = across(second(True))
    return second(False) + from_partner


def solution(mesh):
    rows, columns = mesh.shape["row"], mesh.shape["col"]
    finer = jax.sharding.Mesh(mesh.devices.reshape(rows // 2, 2, 2, columns // 2), ("x", "core", "half", "column"))
    every = ("x", "core", "half", "column")
    in_specs = (
        P(None, every),
        P(None, every),
        P(None, every),
        P(every, None, None, None),
        P(every, None),
        P(every, None),
    )
    body = functools.partial(local, rows, columns // 2)
    return jax.shard_map(body, mesh=finer, in_specs=in_specs, out_specs=P(None, every), check_vma=False)
```
